32 devices in a mesh: seq: 16 (over z, y, x), tp: 2 (over core).
Axes of the slice: x: 2, y: 2, z: 4, core: 2. Of those that a mesh axis runs over, the one named last changes fastest.
Arguments:
- tokens: bfloat16 [32768, 768], P(('seq', 'tp')), may hold values from -6 to 6
- glob_tokens: bfloat16 [512, 768], P(('seq', 'tp')), may hold values from -6 to 6
- w_query: bfloat16 [768, 768], P(None, 'tp'), may hold values from -0.21875 to 0.21875
- b_query: float32 [768], P('tp'), may hold values from -2.5 to 2.5
- w_key: bfloat16 [768, 768], P(None, 'tp'), may hold values from -0.21875 to 0.21875
- w_value: bfloat16 [768, 768], P(None, 'tp'), may hold values from -0.21875 to 0.21875
- b_value: float32 [768], P('tp'), may hold values from -2.5 to 2.5
- w_out: bfloat16 [768, 768], P('tp'), may hold values from -0.875 to 0.875
- b_out: float32 [768], replicated, may hold values from -1.5 to 1.5
- w_up: bfloat16 [768, 3072], P(None, 'tp'), may hold values from -0.21875 to 0.21875
- b_up: float32 [3072], P('tp'), may hold values from -2.5 to 2.5
- w_down: bfloat16 [3072, 768], P('tp'), may hold values from -0.109375 to 0.109375
- b_down: float32 [768], replicated, may hold values from -1.5 to 1.5
- gain_attn: float32 [768], replicated, may hold values from 0.5 to 1.5
- shift_attn: float32 [768], replicated, may hold values from -1 to 1
- gain_ffn: float32 [768], replicated, may hold values from 0.5 to 1.5
- shift_ffn: float32 [768], replicated, may hold values from -1 to 1
- doc_blocks: int32 [4], replicated, may hold values from 1 to 31, as said below
- doc_tail: int32 [4], replicated, may hold values from 1 to 512
- grad_tokens: bfloat16 [32768, 768], P(('seq', 'tp')), may hold values from -6 to 6
- grad_glob: bfloat16 [512, 768], P(('seq', 'tp')), may hold values from -6 to 6
Outputs:
- out_tokens: bfloat16 [32768, 768], P(('seq', 'tp'))
- out_glob: bfloat16 [512, 768], P(('seq', 'tp'))
- tokens_grad: float32 [32768, 768], P(('seq', 'tp'))
- glob_grad: float32 [512, 768], P(('seq', 'tp'))
- w_query_grad: float32 [768, 768], P(None, 'tp')
- b_query_grad: float32 [768], P('tp')
- w_key_grad: float32 [768, 768], P(None, 'tp')
- w_value_grad: float32 [768, 768], P(None, 'tp')
- b_value_grad: float32 [768], P('tp')
- w_out_grad: float32 [768, 768], P('tp')
- b_out_grad: float32 [768], replicated
- w_up_grad: float32 [768, 3072], P(None, 'tp')
- b_up_grad: float32 [3072], P('tp')
- w_down_grad: float32 [3072, 768], P('tp')
- b_down_grad: float32 [768], replicated
- gain_attn_grad: float32 [768], replicated
- shift_attn_grad: float32 [768], replicated
- gain_ffn_grad: float32 [768], replicated
- shift_ffn_grad: float32 [768], replicated
The draws below stay inside these ranges and needn't reach their ends.
Inputs may be any that keep to these rules, and one draw needn't show every extreme that they name: `doc_blocks`: documents lie one after another in tokens; documents 2p and 2p + 1 together span exactly 32 blocks, and one of the two is shorter than 4 blocks, so the entries sum to 64. `doc_tail`: the positions of a document's last block at or past this count are padding.
All inputs are finite; a program needn't handle non-finite values.
Results may differ from the reference program's by a relative error of at most 0.015.
Values may be sent and summed in bfloat16 or wider, within the bound.
No kernel may reach another device: no remote copies, remote signals or barrier semaphores. Data moves between devices by JAX's collectives and lax.ppermute only.
A program may use at most 192 MiB of HBM per device.

```python
import jax
import jax.numpy as jnp
from jax import lax

D = 768
HEADS = 12
HD = 64
FF = 3072
BLOCK = 512
GLOB = 128
BLK_DEV = 4
TOKENS = 32768
DOCS = 4
GROWS = 512


def draw_doc_blocks(key, part):
    key = jax.random.fold_in(key, 11)
    key_len, key_pick, key_flip = jax.random.split(key, 3)
    pair_count = DOCS // 2
    short_len = jax.random.randint(key_len, (pair_count,), 1, BLK_DEV, dtype=jnp.int32)
    forced = jax.random.randint(key_pick, (), 0, pair_count, dtype=jnp.int32)
    short_len = jnp.where(jnp.arange(pair_count, dtype=jnp.int32) == forced, 1, short_len)
    flipped = jax.random.randint(key_flip, (pair_count,), 0, 2, dtype=jnp.int32)
    left_len = jnp.where(flipped == 1, short_len, 32 - short_len)
    right_len = 32 - left_len
    return jnp.stack([left_len, right_len], axis=1).reshape(DOCS).astype(jnp.int32)


def touch_ends(array, key, least, top_value):
    extent = array.shape
    index_at = [jax.random.randint(jax.random.fold_in(key, axis), (), 0, extent[axis]) for axis in range(len(extent))]
    array = array.at[tuple(index_at)].set(least)
    longest = extent.index(max(extent))
    index_at[longest] = (index_at[longest] + 1) % extent[longest]
    return array.at[tuple(index_at)].set(top_value)


def steps_of(own_key, dims, cuts, low, top_value):
    loudness = 1.0
    for dim, shards_of in cuts:
        draws = jax.random.uniform(jax.random.fold_in(jax.random.fold_in(own_key, 6), dim), (shards_of,), jnp.float32, low / len(cuts), top_value / len(cuts))
        loudness = loudness * jnp.repeat(jnp.exp(draws), dims[dim] // shards_of).reshape((-1,) + (1,) * (len(dims) - 1 - dim))
    return loudness


def gaussian(rng, shape, deviation, reach, cuts=(), held_as=jnp.bfloat16):
    entries = deviation * jax.random.normal(rng, shape, jnp.float32)
    if cuts:
        entries = entries * steps_of(rng, shape, cuts, -0.22, 0.18)
    return jnp.clip(entries, -reach, reach).astype(held_as)


def setup_inputs(seed: int = 0) -> dict:
    streams_of = jax.random.split(jax.random.key(seed), 22)
    return {
        "tokens": gaussian(streams_of[0], (TOKENS, D), 1.0, 6.0, ((0, 32),)),
        "glob_tokens": gaussian(streams_of[1], (GROWS, D), 1.0, 6.0, ((0, 32),)),
        "w_query": gaussian(streams_of[2], (D, D), D ** -0.5, 0.21875, ((1, 2),)),
        "b_query": gaussian(streams_of[3], (D,), 0.5, 2.5, ((0, 2),), jnp.float32),
        "w_key": gaussian(streams_of[4], (D, D), D ** -0.5, 0.21875, ((1, 2),)),
        "w_value": gaussian(streams_of[5], (D, D), D ** -0.5, 0.21875, ((1, 2),)),
        "b_value": gaussian(streams_of[6], (D,), 0.5, 2.5, ((0, 2),), jnp.float32),
        "w_out": gaussian(streams_of[7], (D, D), (D // 16) ** -0.5, 0.875, ((0, 2),)),
        "b_out": gaussian(streams_of[8], (D,), 0.3, 1.5, (), jnp.float32),
        "w_up": gaussian(streams_of[9], (D, FF), D ** -0.5, 0.21875, ((1, 2),)),
        "b_up": gaussian(streams_of[10], (FF,), 0.5, 2.5, ((0, 2),), jnp.float32),
        "w_down": gaussian(streams_of[11], (FF, D), FF ** -0.5, 0.109375, ((0, 2),)),
        "b_down": gaussian(streams_of[12], (D,), 0.3, 1.5, (), jnp.float32),
        "gain_attn": jnp.clip(1.0 + 0.1 * jax.random.normal(streams_of[13], (D,), jnp.float32), 0.5, 1.5),
        "shift_attn": gaussian(streams_of[14], (D,), 0.2, 1.0, (), jnp.float32),
        "gain_ffn": jnp.clip(1.0 + 0.1 * jax.random.normal(streams_of[15], (D,), jnp.float32), 0.5, 1.5),
        "shift_ffn": gaussian(streams_of[16], (D,), 0.2, 1.0, (), jnp.float32),
        "doc_blocks": draw_doc_blocks(jax.random.fold_in(streams_of[21], 71), 0),
        "doc_tail": touch_ends(jax.random.randint(streams_of[18], (DOCS,), 1, BLOCK + 1), jax.random.fold_in(streams_of[18], 1), 1, BLOCK).astype(jnp.int32),
        "grad_tokens": gaussian(streams_of[19], (TOKENS, D), 1.0, 6.0, ((0, 32),)),
        "grad_glob": gaussian(streams_of[20], (GROWS, D), 1.0, 6.0, ((0, 32),)),
    }


EPS = 1e-05
SCALE = 0.125

@jax.custom_vjp
def low(v):
    return lax.optimization_barrier(v.astype(jnp.bfloat16)).astype(jnp.float32)

@jax.custom_vjp
def low_back(v):
    return v

def low_keep(v):
    return (low(v), None)

def low_pass(kept, grad):
    return (grad,)

def back_keep(v):
    return (v, None)

def back_low(kept, grad):
    return (low(grad),)
low.defvjp(low_keep, low_pass)
low_back.defvjp(back_keep, back_low)

def norm_rows(values, gain_vec, shift_vec):
    row_mean = lax.optimization_barrier(jnp.mean(values, axis=-1, keepdims=True))
    centred = values - row_mean
    row_var = lax.optimization_barrier(jnp.mean(centred * centred, axis=-1, keepdims=True))
    return centred * lax.rsqrt(row_var + EPS) * gain_vec + shift_vec

def exact_gelu(values):
    return jax.nn.gelu(values, approximate=False)

def mat_prod(left, right):
    return jnp.dot(left, right, precision=lax.Precision.HIGHEST)

def block_layout(doc_blocks, doc_tail, first_block, block_count, block_len):
    doc_ends = jnp.cumsum(doc_blocks).astype(jnp.int32)
    block_ids = first_block + jnp.arange(block_count, dtype=jnp.int32)
    doc_of = lax.optimization_barrier(jnp.sum((block_ids[:, None] >= doc_ends[None, :]).astype(jnp.int32), axis=1)).astype(jnp.int32)
    picked = doc_of[:, None] == jnp.arange(doc_ends.shape[0], dtype=jnp.int32)[None, :]
    last_end = lax.optimization_barrier(jnp.sum(jnp.where(picked, doc_ends[None, :], 0), axis=1)).astype(jnp.int32)
    tail_len = lax.optimization_barrier(jnp.sum(jnp.where(picked, doc_tail[None, :], 0), axis=1)).astype(jnp.int32)
    tail_all = jnp.where(block_ids == last_end - 1, tail_len, block_len)
    key_valid = jnp.arange(block_len, dtype=jnp.int32)[None, :] < tail_all[:, None]
    return (doc_of, key_valid)

def attend(queries, key_cat, value_cat, key_mask):
    scores = low_back(jnp.einsum('rhe,khe->hrk', queries, key_cat, precision=lax.Precision.HIGHEST))
    exp_scores = jnp.where(key_mask[None, None, :], jnp.exp(scores), 0.0)
    totals = lax.optimization_barrier(jnp.sum(exp_scores, axis=-1, keepdims=True))
    prob_low = low(exp_scores / totals)
    return jnp.einsum('hrk,khe->rhe', prob_low, value_cat, precision=lax.Precision.HIGHEST)

def layer(token_in, glob_in, w_query, b_query, w_key, w_value, b_value, w_out, b_out, w_up, b_up, w_down, b_down, gain_attn, shift_attn, gain_ffn, shift_ffn, doc_of, key_valid):
    block_count = doc_of.shape[0]
    doc_count = glob_in.shape[0] // GLOB

    def project(hidden):
        queries = low_back(low((mat_prod(hidden, w_query) + b_query) * SCALE))
        key_rows = low_back(low(mat_prod(hidden, w_key)))
        value_rows = low_back(low(mat_prod(hidden, w_value) + b_value))
        return (queries.reshape(-1, HEADS, HD), key_rows.reshape(-1, HEADS, HD), value_rows.reshape(-1, HEADS, HD))
    hidden_tok = low(norm_rows(token_in, gain_attn, shift_attn))
    hidden_glob = low(norm_rows(glob_in, gain_attn, shift_attn))
    query_tok, key_tok, value_tok = project(hidden_tok)
    query_glob, key_glob, value_glob = project(hidden_glob)

    def local_block(block_item):
        query_blk, key_blk, value_blk, valid_blk, doc_num = block_item
        key_doc = lax.dynamic_slice_in_dim(key_glob, doc_num * GLOB, GLOB, 0)
        value_doc = lax.dynamic_slice_in_dim(value_glob, doc_num * GLOB, GLOB, 0)
        mask_cat = jnp.concatenate([valid_blk, jnp.ones((GLOB,), dtype=bool)])
        return attend(query_blk, jnp.concatenate([key_blk, key_doc], 0), jnp.concatenate([value_blk, value_doc], 0), mask_cat)
    out_tok = lax.map(jax.checkpoint(local_block), (query_tok.reshape(block_count, BLOCK, HEADS, HD), key_tok.reshape(block_count, BLOCK, HEADS, HD), value_tok.reshape(block_count, BLOCK, HEADS, HD), key_valid, doc_of))
    token_doc = jnp.repeat(doc_of, BLOCK)
    token_ok = key_valid.reshape(-1)

    def doc_globals(doc_item):
        query_doc, key_doc, value_doc, doc_num = doc_item
        mask_cat = jnp.concatenate([(token_doc == doc_num) & token_ok, jnp.ones((GLOB,), dtype=bool)])
        return attend(query_doc, jnp.concatenate([key_tok, key_doc], 0), jnp.concatenate([value_tok, value_doc], 0), mask_cat)
    out_glob = lax.map(jax.checkpoint(doc_globals), (query_glob.reshape(doc_count, GLOB, HEADS, HD), key_glob.reshape(doc_count, GLOB, HEADS, HD), value_glob.reshape(doc_count, GLOB, HEADS, HD), jnp.arange(doc_count, dtype=jnp.int32)))
    attn_tok = low_back(low(out_tok.reshape(-1, HEADS * HD)))
    attn_glob = low_back(low(out_glob.reshape(-1, HEADS * HD)))

    def finish(residual, attn_low):
        branch = low_back(mat_prod(attn_low, w_out) + b_out)
        middle = residual + branch
        hidden = low(norm_rows(middle, gain_ffn, shift_ffn))
        up_proj = low_back(mat_prod(hidden, w_up) + b_up)
        active = low(exact_gelu(up_proj))
        return middle + mat_prod(active, w_down) + b_down
    return (finish(token_in, attn_tok), finish(glob_in, attn_glob))

def reference(tokens, glob_tokens, w_query, b_query, w_key, w_value, b_value, w_out, b_out, w_up, b_up, w_down, b_down, gain_attn, shift_attn, gain_ffn, shift_ffn, doc_blocks, doc_tail, grad_tokens, grad_glob):
    block_count = tokens.shape[0] // BLOCK
    doc_of, key_valid = block_layout(doc_blocks, doc_tail, jnp.int32(0), block_count, BLOCK)
    floats = tuple((array_in.astype(jnp.float32) for array_in in (tokens, glob_tokens, w_query, b_query, w_key, w_value, b_value, w_out, b_out, w_up, b_up, w_down, b_down, gain_attn, shift_attn, gain_ffn, shift_ffn)))

    def wrapped(*params):
        return layer(*params, doc_of, key_valid)
    outputs, pullback = jax.vjp(wrapped, *floats)
    all_grads = pullback((grad_tokens.astype(jnp.float32), grad_glob.astype(jnp.float32)))
    return (outputs[0].astype(jnp.bfloat16), outputs[1].astype(jnp.bfloat16), all_grads[0], all_grads[1], all_grads[2], all_grads[3], all_grads[4], all_grads[5], all_grads[6], all_grads[7], all_grads[8], all_grads[9], all_grads[10], all_grads[11], all_grads[12], all_grads[13], all_grads[14], all_grads[15], all_grads[16])
```

```python
import functools

import jax
import jax.numpy as jnp
from jax import lax
from jax.experimental import pallas as pl
from jax.experimental.pallas import tpu as pltpu
from jax.sharding import PartitionSpec as P

HD = 64
BLOCK = 512
GLOB = 128
GROUP_BLOCKS = 32
EPS = 1e-05
SCALE = 0.125
NEG = -1e30
TILE = 256
PAIR = 2 * HD
LANES = 128
STATS = 16
F32 = jnp.float32
BF16 = jnp.bfloat16
VMEM_BYTES = 56 * 2**20


def nn(left, right):
    return jnp.dot(left, right, preferred_element_type=F32)


def nt(left, right):
    return lax.dot_general(left, right, (((1,), (1,)), ((), ())), preferred_element_type=F32)


def tn(left, right):
    return lax.dot_general(left, right, (((0,), (0,)), ((), ())), preferred_element_type=F32)


def normed(values):
    row_mean = jnp.mean(values, axis=-1, keepdims=True)
    centred = values - row_mean
    row_var = jnp.mean(centred * centred, axis=-1, keepdims=True)
    inv = lax.rsqrt(row_var + EPS)
    return centred * inv, inv


def norm_back(xhat, inv, gain_vec, cotangent):
    scaled = cotangent * gain_vec
    mean_one = jnp.mean(scaled, axis=-1, keepdims=True)
    mean_two = jnp.mean(scaled * xhat, axis=-1, keepdims=True)
    return inv * (scaled - mean_one - xhat * mean_two)


def full(shape):
    zeros = (0,) * len(shape)
    return pl.BlockSpec(shape, lambda *_: zeros, pipeline_mode=pl.Buffered(1))


def params(dims=1):
    return pltpu.CompilerParams(
        vmem_limit_bytes=VMEM_BYTES, dimension_semantics=("arbitrary",) * dims
    )


def cost(flops, nbytes, trans=0):
    return pl.CostEstimate(flops=int(flops), bytes_accessed=int(nbytes), transcendentals=int(trans))


def head_lanes(head):
    lane = lax.broadcasted_iota(jnp.int32, (1, LANES), 1)
    here = jnp.where(lane < HD, 1.0, 0.0)
    mine = here if head == 0 else 1.0 - here
    return mine.astype(BF16), (1.0 - mine).astype(BF16)


def lane_one(slot):
    lane = lax.broadcasted_iota(jnp.int32, (1, LANES), 1)
    return jnp.where((lane == slot) | (lane == slot + HD), 1.0, 0.0).astype(BF16)


def project_body(x_ref, gain_ref, shift_ref, own_ref, par_ref, bias_ref, scale_ref, *rest):
    qkv_ref, turned_ref = rest[-2:]
    xhat, _ = normed(x_ref[...].astype(F32))
    hidden = (xhat * gain_ref[...] + shift_ref[...]).astype(BF16)
    turned_ref[...] = hidden.T
    width = own_ref.shape[1]
    for half, weight in enumerate((own_ref, par_ref)):
        cols = slice(half * width, (half + 1) * width)
        made = nn(hidden, weight[...])
        qkv_ref[:, cols] = ((made + bias_ref[:, cols]) * scale_ref[:, cols]).astype(BF16)


def project(x, gain, shift, w_own, w_par, bias, scale, rows_all, first, held=None):
    rows, dim = x.shape
    width = 2 * w_own.shape[1]
    tiles = rows // TILE
    vec = full((1, dim))
    specs = [
        pl.BlockSpec((TILE, dim), lambda i: (i, 0)),
        vec,
        vec,
        full(w_own.shape),
        full(w_par.shape),
        full((1, width)),
        full((1, width)),
    ]
    operands = [x, gain, shift, w_own, w_par, bias, scale]
    aliases = {}
    if held is not None:
        aliases = {len(operands): 0, len(operands) + 1: 1}
        operands += list(held)
        specs += [pl.BlockSpec(memory_space=pl.ANY)] * 2
    return pl.pallas_call(
        project_body,
        grid=(tiles,),
        in_specs=specs,
        out_specs=[
            pl.BlockSpec((TILE, width), lambda i: (i + first, 0)),
            pl.BlockSpec((dim, TILE), lambda i: (0, i + first)),
        ],
        out_shape=[
            jax.ShapeDtypeStruct((rows_all, width), BF16),
            jax.ShapeDtypeStruct((dim, rows_all), BF16),
        ],
        input_output_aliases=aliases,
        compiler_params=params(),
        cost_estimate=cost(2 * rows * dim * width, 2 * (rows * (2 * dim + width) + dim * width)),
        name="project",
    )(*operands)


def pair_column(kind, pairs):
    half = pairs // 2
    return lambda p: (p // half) * 3 * half + kind * half + p % half


def glob_forward_body(q_ref, k_ref, v_ref, augk_ref, augq_ref, out_ref):
    rows_all = k_ref.shape[0]
    count = augq_ref.shape[0]
    queries = q_ref[rows_all - count :, :]
    keys = k_ref[...]
    values_turned = v_ref[...].T
    for head in range(2):
        mine, other = head_lanes(head)
        key_head = keys * mine + augk_ref[...] * other
        query_head = queries * mine + augq_ref[...] * other
        scores = nt(key_head, query_head)
        top = jnp.max(scores, axis=0, keepdims=True)
        weights = jnp.exp(scores - top)
        total = jnp.sum(weights, axis=0, keepdims=True)
        summed = nn(values_turned[head * HD : (head + 1) * HD, :], weights.astype(BF16))
        out_ref[head, :HD, :] = (summed / total).astype(BF16)
        write_stats(out_ref, head, top + jnp.log(total))


def write_stats(out_ref, head, lse):
    first = lse.astype(BF16).astype(F32)
    second = (lse - first).astype(BF16).astype(F32)
    third = lse - first - second
    row = lax.broadcasted_iota(jnp.int32, (STATS, lse.shape[1]), 0)
    held = jnp.where(row == 0, first, jnp.where(row == 1, second, jnp.where(row == 2, third, 0.0)))
    out_ref[head, HD : HD + STATS, :] = held.astype(BF16)


def glob_forward(qkv, augk, augq, pairs):
    rows_all = qkv.shape[0]
    count = augq.shape[0]

    def block(kind):
        column = pair_column(kind, pairs)
        return pl.BlockSpec((rows_all, LANES), lambda p: (0, column(p)))

    work = 2 * pairs * rows_all * count
    return pl.pallas_call(
        glob_forward_body,
        grid=(pairs,),
        in_specs=[block(0), block(1), block(2), full(augk.shape), full(augq.shape)],
        out_specs=pl.BlockSpec((2, HD + STATS, count), lambda p: (p, 0, 0)),
        out_shape=jax.ShapeDtypeStruct((2 * pairs, HD + STATS, count), BF16),
        compiler_params=params(),
        cost_estimate=cost(work * 2 * 512, qkv.size * 2, work),
        name="glob_forward",
    )(qkv, qkv, qkv, augk, augq)


def read_stats(ref, head):
    held = ref[head, HD : HD + STATS, :].astype(F32)
    return held[0:1] + held[1:2] + held[2:3]


def merge_head(left_ref, right_ref, head):
    lse_left, lse_right = read_stats(left_ref, head), read_stats(right_ref, head)
    top = jnp.maximum(lse_left, lse_right)
    weight_left, weight_right = jnp.exp(lse_left - top), jnp.exp(lse_right - top)
    total = weight_left + weight_right
    out_left = left_ref[head, :HD, :].astype(F32)
    out_right = right_ref[head, :HD, :].astype(F32)
    merged = (out_left * weight_left + out_right * weight_right) / total
    return merged, top + jnp.log(total)


def merge_body(left_ref, right_ref, out_ref):
    for head in range(left_ref.shape[0]):
        merged, lse = merge_head(left_ref, right_ref, head)
        out_ref[head, :HD, :] = merged.astype(BF16)
        write_stats(out_ref, head, lse)


def merge(left, right):
    return pl.pallas_call(
        merge_body,
        out_shape=jax.ShapeDtypeStruct(left.shape, BF16),
        compiler_params=pltpu.CompilerParams(vmem_limit_bytes=VMEM_BYTES),
        cost_estimate=cost(left.size * 8, left.size * 6),
        name="merge",
    )(left, right)


def local_forward_body(
    docs_ref, q_ref, k_ref, v_ref, kg_ref, vg_ref, augk_ref, high_ref, low_ref, turned_ref, lse_ref
):
    keys = jnp.concatenate([k_ref[...], kg_ref[...]], 0)
    values_turned = jnp.concatenate([v_ref[...], vg_ref[...]], 0).T
    bias = jnp.concatenate([augk_ref[...], jnp.zeros((GLOB, LANES), BF16)], 0)
    outs = []
    for head in range(2):
        mine, other = head_lanes(head)
        key_head = keys * mine + bias * other
        query_head = q_ref[...] * mine + lane_one(0) * other
        scores = nt(key_head, query_head)
        top = jnp.max(scores, axis=0, keepdims=True)
        weights = jnp.exp(scores - top)
        total = jnp.sum(weights, axis=0, keepdims=True)
        summed = nn(values_turned[head * HD : (head + 1) * HD, :], weights.astype(BF16))
        outs.append(summed / total)
        lse_ref[0, 0, head : head + 1, :] = top + jnp.log(total)
    turned = jnp.concatenate(outs, 0)
    turned_ref[...] = turned.astype(BF16)
    straight = turned.T
    high = straight.astype(BF16)
    high_ref[...] = high
    low_ref[...] = (straight - high.astype(F32)).astype(BF16)


def local_forward(docs, qkv, augk, pairs, blocks):
    rows_all = qkv.shape[0]
    local_rows = blocks * BLOCK
    glob_first = local_rows // GLOB

    def block(kind):
        column = pair_column(kind, pairs)
        return pl.BlockSpec((BLOCK, LANES), lambda b, p, docs: (b, column(p)))

    def glob_block(kind):
        column = pair_column(kind, pairs)
        return pl.BlockSpec((GLOB, LANES), lambda b, p, docs: (glob_first + docs[b], column(p)))

    work = 2 * pairs * local_rows * (BLOCK + GLOB)
    width = pairs * LANES
    straight = pl.BlockSpec((BLOCK, LANES), lambda b, p, docs: (b, p))
    return pl.pallas_call(
        local_forward_body,
        grid_spec=pltpu.PrefetchScalarGridSpec(
            num_scalar_prefetch=1,
            grid=(blocks, pairs),
            in_specs=[
                block(0),
                block(1),
                block(2),
                glob_block(1),
                glob_block(2),
                pl.BlockSpec((BLOCK, LANES), lambda b, p, docs: (b, 0)),
            ],
            out_specs=[
                straight,
                straight,
                pl.BlockSpec((LANES, BLOCK), lambda b, p, docs: (p, b)),
                pl.BlockSpec((1, 1, 2, BLOCK), lambda b, p, docs: (b, p, 0, 0)),
            ],
        ),
        out_shape=[
            jax.ShapeDtypeStruct((rows_all, width), BF16),
            jax.ShapeDtypeStruct((rows_all, width), BF16),
            jax.ShapeDtypeStruct((width, rows_all), BF16),
            jax.ShapeDtypeStruct((blocks, pairs, 2, BLOCK), F32),
        ],
        compiler_params=params(2),
        cost_estimate=cost(work * 2 * 512, qkv.size * 2, work),
        name="local_forward",
    )(docs, qkv, qkv, qkv, qkv, qkv, augk)


def middle_of(out_high, x, own_ref, par_ref, bias_ref, gain_ref, shift_ref):
    half = own_ref.shape[0]
    branch = nn(out_high[:, :half], own_ref[...]) + nn(out_high[:, half:], par_ref[...])
    middle = x.astype(F32) + branch + bias_ref[...]
    xhat, _ = normed(middle)
    hidden = (xhat * gain_ref[...] + shift_ref[...]).astype(BF16)
    return middle, hidden


def middle_body(
    out_ref, x_ref, own_ref, par_ref, bias_ref, gain_ref, shift_ref, mid_ref, hid_ref, turned_ref
):
    middle, hidden = middle_of(
        out_ref[...], x_ref[...], own_ref, par_ref, bias_ref, gain_ref, shift_ref
    )
    mid_ref[...] = middle
    hid_ref[...] = hidden
    turned_ref[...] = hidden.T


def middle_local(out_high, x, w_own, w_par, bias, gain, shift):
    rows_all, dim = out_high.shape
    rows = x.shape[0]
    row = pl.BlockSpec((TILE, dim), lambda i: (i, 0))
    vec = full((1, dim))
    return pl.pallas_call(
        middle_body,
        grid=(rows // TILE,),
        in_specs=[row, row, full(w_own.shape), full(w_par.shape), vec, vec, vec],
        out_specs=[row, row, pl.BlockSpec((dim, TILE), lambda i: (0, i))],
        out_shape=[
            jax.ShapeDtypeStruct((rows_all, dim), F32),
            jax.ShapeDtypeStruct((rows_all, dim), BF16),
            jax.ShapeDtypeStruct((dim, rows_all), BF16),
        ],
        compiler_params=params(),
        cost_estimate=cost(2 * rows * dim * dim, 12 * rows * dim + 2 * dim * dim),
        name="middle_local",
    )(out_high, x, w_own, w_par, bias, gain, shift)


def middle_glob_body(own_out_ref, par_out_ref, x_ref, own_ref, par_ref, bias_ref, gain_ref, shift_ref, *rest):
    mid_ref, hid_ref, turned_ref, high_ref, low_ref, out_turned_ref, lse_ref = rest[-7:]
    heads = own_out_ref.shape[0]
    parts = [own_out_ref[head, :HD, :] for head in range(heads)]
    parts += [par_out_ref[head, :HD, :] for head in range(heads)]
    turned = jnp.concatenate(parts, 0)
    out_turned_ref[...] = turned
    high = turned.T
    high_ref[...] = high
    low_ref[...] = jnp.zeros_like(high)
    stats = [read_stats(own_out_ref, head) for head in range(heads)]
    stats += [read_stats(par_out_ref, head) for head in range(heads)]
    spare = lse_ref.shape[0] - 2 * heads
    lse_ref[...] = jnp.concatenate(stats + [jnp.zeros((spare, x_ref.shape[0]), F32)], 0)
    middle, hidden = middle_of(high, x_ref[...], own_ref, par_ref, bias_ref, gain_ref, shift_ref)
    mid_ref[...] = middle
    hid_ref[...] = hidden
    turned_ref[...] = hidden.T


def middle_glob(own_out, par_out, x, w_own, w_par, bias, gain, shift, held):
    rows, dim = x.shape
    rows_all = held[0].shape[0]
    first = rows_all // rows - 1
    vec = full((1, dim))
    row = pl.BlockSpec((rows, dim), lambda i: (first, 0))
    col = pl.BlockSpec((dim, rows), lambda i: (0, first))
    lse_rows = 16
    return pl.pallas_call(
        middle_glob_body,
        grid=(1,),
        in_specs=[
            full(own_out.shape),
            full(par_out.shape),
            full((rows, dim)),
            full(w_own.shape),
            full(w_par.shape),
            vec,
            vec,
            vec,
        ]
        + [pl.BlockSpec(memory_space=pl.ANY)] * 6,
        out_specs=[row, row, col, row, row, col, full((lse_rows, rows))],
        out_shape=[jax.ShapeDtypeStruct(h.shape, h.dtype) for h in held]
        + [jax.ShapeDtypeStruct((lse_rows, rows), F32)],
        input_output_aliases={8 + i: i for i in range(6)},
        compiler_params=params(),
        cost_estimate=cost(2 * rows * dim * dim, 12 * rows * dim + 2 * dim * dim),
        name="middle_glob",
    )(own_out, par_out, x, w_own, w_par, bias, gain, shift, *held)


def ffn_body(
    hid_ref, turned_ref, dz_ref, up_ref, bias_ref, down_ref, mask_ref,
    dnorm_ref, out_ref, grads_ref, bias_grad_ref, act_s, dup_s,
):
    step = pl.program_id(0)
    rows_all, dim = hid_ref.shape
    chunk = up_ref.shape[1]
    tiles = rows_all // TILE
    bias_grad = jnp.zeros((1, chunk), F32)
    for tile in range(tiles):
        rows = slice(tile * TILE, (tile + 1) * TILE)
        up = nn(hid_ref[rows, :], up_ref[...]) + bias_ref[...]
        share = 0.5 * (1.0 + lax.erf(up * (2.0**-0.5)))
        density = jnp.exp(up * up * -0.5) * 0.3989422804014327
        active = (up * share).astype(BF16)
        slope = share + up * density
        d_up = (nt(dz_ref[rows, :], down_ref[...]) * slope).astype(BF16)
        d_norm = nt(d_up, up_ref[...])
        out = nn(active, down_ref[...])

        @pl.when(step == 0)
        def _():
            dnorm_ref[rows, :] = d_norm
            out_ref[rows, :] = out

        @pl.when(step > 0)
        def _():
            dnorm_ref[rows, :] += d_norm
            out_ref[rows, :] += out

        if tile == tiles - 1:
            mask = mask_ref[...]
            d_up = (d_up.astype(F32) * mask).astype(BF16)
            active = (active.astype(F32) * mask).astype(BF16)
        bias_grad += jnp.sum(d_up.astype(F32), axis=0, keepdims=True)
        act_s[rows, :] = active
        dup_s[rows, :] = d_up
    bias_grad_ref[...] = bias_grad
    up_grad = nn(turned_ref[...], dup_s[...]).astype(BF16)
    down_grad = tn(act_s[...], dz_ref[...]).astype(BF16)
    place = 0
    for grad in (up_grad, down_grad):
        rows = grad.shape[0]
        for col in range(grad.shape[1] // LANES):
            grads_ref[0, place : place + rows, :] = grad[:, col * LANES : (col + 1) * LANES]
            place += rows


def ffn_half(hidden, turned, dz, w_up, b_up, w_down, mask):
    rows_all, dim = hidden.shape
    units = w_up.shape[1]
    chunk = TILE
    steps = units // chunk
    packed = 2 * chunk * dim // LANES
    return pl.pallas_call(
        ffn_body,
        grid=(steps,),
        in_specs=[
            full(hidden.shape),
            full(turned.shape),
            full(dz.shape),
            pl.BlockSpec((dim, chunk), lambda j: (0, j)),
            pl.BlockSpec((1, chunk), lambda j: (0, j)),
            pl.BlockSpec((chunk, dim), lambda j: (j, 0)),
            full(mask.shape),
        ],
        out_specs=[
            full((rows_all, dim)),
            full((rows_all, dim)),
            pl.BlockSpec((1, packed, LANES), lambda j: (j, 0, 0)),
            pl.BlockSpec((1, chunk), lambda j: (0, j)),
        ],
        out_shape=[
            jax.ShapeDtypeStruct((rows_all, dim), F32),
            jax.ShapeDtypeStruct((rows_all, dim), F32),
            jax.ShapeDtypeStruct((steps, packed, LANES), BF16),
            jax.ShapeDtypeStruct((1, units), F32),
        ],
        scratch_shapes=[pltpu.VMEM((rows_all, chunk), BF16), pltpu.VMEM((rows_all, chunk), BF16)],
        compiler_params=params(),
        cost_estimate=cost(
            12 * rows_all * dim * units, rows_all * dim * 14 + units * dim * 8, 2 * rows_all * units
        ),
        name="ffn_half",
    )(hidden, turned, dz, w_up, b_up, w_down, mask)


def middle_back_body(
    dn_one_ref, dn_two_ref, mid_ref, dz_ref, high_ref, low_ref, out_turned_ref, own_ref, par_ref,
    gain_ref, mask_ref, dmid_ref, dattn_ref, delta_ref, grads_ref, sums_ref, acc_s,
):
    step = pl.program_id(0)
    dim = mid_ref.shape[1]
    half = own_ref.shape[0]
    xhat, inv = normed(mid_ref[...])
    dn = dn_one_ref[...] + dn_two_ref[...]
    dz = dz_ref[...].astype(F32)
    d_mid = dz + norm_back(xhat, inv, gain_ref[...], dn)
    dmid_ref[...] = d_mid
    d_branch = d_mid.astype(BF16)
    for part, weight in enumerate((own_ref, par_ref)):
        dattn_ref[:, part * half : (part + 1) * half] = nt(d_branch, weight[...]).astype(BF16)
    straight = high_ref[...].astype(F32) + low_ref[...].astype(F32)
    product = dattn_ref[...].astype(F32) * straight
    first = product.astype(BF16)
    second = (product - first.astype(F32)).astype(BF16)
    head = lax.broadcasted_iota(jnp.int32, (delta_ref.shape[0], dim), 0)
    column = lax.broadcasted_iota(jnp.int32, (delta_ref.shape[0], dim), 1)
    picked = jnp.where((column >= head * HD) & (column < (head + 1) * HD), 1.0, 0.0).astype(BF16)
    delta_ref[...] = nt(picked, first) + nt(picked, second)
    mask = mask_ref[...]
    masked = (d_branch.astype(F32) * mask).astype(BF16)
    made = nn(out_turned_ref[...], masked)
    sums = [
        jnp.sum(dn * xhat * mask, axis=0, keepdims=True),
        jnp.sum(dn * mask, axis=0, keepdims=True),
        jnp.sum(masked.astype(F32), axis=0, keepdims=True),
        jnp.sum(dz * mask, axis=0, keepdims=True),
    ]
    sums = jnp.concatenate(sums + [jnp.zeros((4, dim), F32)], 0)

    @pl.when(step == 0)
    def _():
        acc_s[...] = made
        sums_ref[...] = sums

    @pl.when(step > 0)
    def _():
        acc_s[...] += made
        sums_ref[...] += sums

    @pl.when(step == pl.num_programs(0) - 1)
    def _():
        for part in range(2):
            for col in range(dim // LANES):
                grads_ref[part, col * half : (col + 1) * half, :] = acc_s[
                    part * half : (part + 1) * half, col * LANES : (col + 1) * LANES
                ].astype(BF16)


def middle_back(dn_one, dn_two, middle, dz, high, low, out_turned, w_own, w_par, gain, mask):
    rows_all, dim = middle.shape
    row = pl.BlockSpec((TILE, dim), lambda i: (i, 0))
    col = pl.BlockSpec((dim, TILE), lambda i: (0, i))
    lse_rows = 16
    packed = w_own.size // LANES
    return pl.pallas_call(
        middle_back_body,
        grid=(rows_all // TILE,),
        in_specs=[
            row, row, row, row, row, row, col, full(w_own.shape), full(w_par.shape),
            full((1, dim)), pl.BlockSpec((TILE, 1), lambda i: (i, 0)),
        ],
        out_specs=[
            row,
            row,
            pl.BlockSpec((lse_rows, TILE), lambda i: (0, i)),
            full((2, packed, LANES)),
            full((8, dim)),
        ],
        out_shape=[
            jax.ShapeDtypeStruct((rows_all, dim), F32),
            jax.ShapeDtypeStruct((rows_all, dim), BF16),
            jax.ShapeDtypeStruct((lse_rows, rows_all), F32),
            jax.ShapeDtypeStruct((2, packed, LANES), BF16),
            jax.ShapeDtypeStruct((8, dim), F32),
        ],
        scratch_shapes=[pltpu.VMEM((dim, dim), F32)],
        compiler_params=params(),
        cost_estimate=cost(4 * rows_all * dim * dim, rows_all * dim * 28),
        name="middle_back",
    )(dn_one, dn_two, middle, dz, high, low, out_turned, w_own, w_par, gain, mask)


def attention_back_body(
    docs_ref, q_ref, k_ref, v_ref, do_ref, lse_ref, lseg_ref, delta_ref, augk_ref, augq_ref,
    dq_ref, dk_ref, dv_ref, key_s, value_s, turned_s, dk_s, dv_s,
):
    pair = pl.program_id(0)
    rows_all = q_ref.shape[0]
    count = augq_ref.shape[0]
    local_rows = rows_all - count
    blocks = local_rows // BLOCK
    turned_s[...] = k_ref[...].T
    dk_s[...] = jnp.zeros_like(dk_s)
    dv_s[...] = jnp.zeros_like(dv_s)
    dq_parts = [[] for _ in range(blocks + 1)]
    for head in range(2):
        mine, other = head_lanes(head)
        key_s[...] = k_ref[...] * mine + augk_ref[...] * other
        value_s[...] = v_ref[...] * mine
        head_rows = slice(head * HD, (head + 1) * HD)
        index = 2 * pair + head

        def grads(key_cat, value_cat, turned_cat, query_rows, aug, lse):
            queries = q_ref[query_rows, :] * mine
            douts = do_ref[query_rows, :] * mine
            delta = delta_ref[pl.ds(index, 1), query_rows]
            probs = jnp.exp(nt(key_cat, queries + aug * other) - lse)
            d_scores = (probs * (nt(value_cat, douts) - delta)).astype(BF16)
            d_key = nn(d_scores, queries)
            d_value = nn(probs.astype(BF16), douts)
            return nn(turned_cat, d_scores), d_key, d_value

        for block in range(blocks):
            rows = slice(block * BLOCK, (block + 1) * BLOCK)
            start = pl.multiple_of(local_rows + docs_ref[block] * GLOB, GLOB)
            doc_rows = pl.ds(start, GLOB)
            key_cat = jnp.concatenate([key_s[rows, :], key_s[doc_rows, :]], 0)
            value_cat = jnp.concatenate([value_s[rows, :], value_s[doc_rows, :]], 0)
            turned_cat = jnp.concatenate(
                [turned_s[head_rows, rows], turned_s[head_rows, doc_rows]], 1
            )
            d_query, d_key, d_value = grads(
                key_cat, value_cat, turned_cat, rows, lane_one(0), lse_ref[block, 0, head : head + 1, :]
            )
            dq_parts[block].append(d_query)
            dk_s[rows, :] += d_key[:BLOCK]
            dk_s[doc_rows, :] += d_key[BLOCK:]
            dv_s[rows, :] += d_value[:BLOCK]
            dv_s[doc_rows, :] += d_value[BLOCK:]
        rows = slice(local_rows, rows_all)
        d_query, d_key, d_value = grads(
            key_s[...], value_s[...], turned_s[head_rows, :], rows, augq_ref[...],
            lseg_ref[pl.ds(index, 1), :],
        )
        dq_parts[blocks].append(d_query)
        dk_s[...] += d_key
        dv_s[...] += d_value
    for block in range(blocks + 1):
        first = block * BLOCK
        made = jnp.concatenate(dq_parts[block], 0).T
        dq_ref[first : first + made.shape[0], :] = (made.astype(BF16).astype(F32) * SCALE).astype(BF16)
    dk_ref[...] = dk_s[...].astype(BF16)
    dv_ref[...] = dv_s[...].astype(BF16)


def attention_back(docs, qkv, d_attn, lse, lse_glob, delta, augk, augq, pairs):
    rows_all = qkv.shape[0]
    count = augq.shape[0]
    blocks = (rows_all - count) // BLOCK

    def block(kind):
        column = pair_column(kind, pairs)
        return pl.BlockSpec((rows_all, LANES), lambda p, docs: (0, column(p)))

    straight = pl.BlockSpec((rows_all, LANES), lambda p, docs: (0, p))
    shape = jax.ShapeDtypeStruct((rows_all, pairs * LANES), BF16)
    work = 2 * pairs * (blocks * BLOCK * (BLOCK + GLOB) + rows_all * count)
    return pl.pallas_call(
        attention_back_body,
        grid_spec=pltpu.PrefetchScalarGridSpec(
            num_scalar_prefetch=1,
            grid=(pairs,),
            in_specs=[
                block(0),
                block(1),
                block(2),
                straight,
                pl.BlockSpec((blocks, 1, 2, BLOCK), lambda p, docs: (0, p, 0, 0)),
                full(lse_glob.shape),
                full(delta.shape),
                full(augk.shape),
                full(augq.shape),
            ],
            out_specs=[straight] * 3,
            scratch_shapes=[
                pltpu.VMEM((rows_all, LANES), BF16),
                pltpu.VMEM((rows_all, LANES), BF16),
                pltpu.VMEM((LANES, rows_all), BF16),
                pltpu.VMEM((rows_all, LANES), F32),
                pltpu.VMEM((rows_all, LANES), F32),
            ],
        ),
        out_shape=[shape] * 3,
        compiler_params=params(),
        cost_estimate=cost(work * 5 * 512, qkv.size * 4, work),
        name="attention_back",
    )(docs, qkv, qkv, qkv, d_attn, lse, lse_glob, delta, augk, augq)


def project_grad_body(turned_ref, dq_ref, dk_ref, dv_ref, grads_ref, sums_ref):
    step = pl.program_id(0)
    width = dq_ref.shape[1]
    for kind, ref in enumerate((dq_ref, dk_ref, dv_ref)):
        made = nn(turned_ref[...], ref[...]).astype(BF16)
        for col in range(width // LANES):
            grads_ref[kind * (width // LANES) + col, :, :] = made[:, col * LANES : (col + 1) * LANES]

    @pl.when(step == 0)
    def _():
        sums_ref[...] = jnp.zeros_like(sums_ref)
        for slot, ref in enumerate((dq_ref, dv_ref)):
            sums_ref[slot : slot + 1, :] = jnp.sum(ref[...].astype(F32), axis=0, keepdims=True)


def project_grad(turned, dq, dk, dv, half):
    dim, rows_all = turned.shape
    width = dq.shape[1] // 2
    grads = pl.BlockSpec((rows_all, width), lambda i: (0, half), pipeline_mode=pl.Buffered(1))
    blocks = 3 * width // LANES
    return pl.pallas_call(
        project_grad_body,
        grid=(dim // TILE,),
        in_specs=[pl.BlockSpec((TILE, rows_all), lambda i: (i, 0)), grads, grads, grads],
        out_specs=[pl.BlockSpec((blocks, TILE, LANES), lambda i: (0, i, 0)), full((8, width))],
        out_shape=[
            jax.ShapeDtypeStruct((blocks, dim, LANES), BF16),
            jax.ShapeDtypeStruct((8, width), F32),
        ],
        compiler_params=params(),
        cost_estimate=cost(6 * rows_all * dim * width, rows_all * (dim + 3 * width) * 2),
        name="project_grad",
    )(turned, dq, dk, dv)


def input_back_body(
    dq_ref, dk_ref, dv_ref, own_ref, par_ref, x_ref, xg_ref, dmid_ref, gain_ref,
    tokens_ref, glob_ref, sums_ref,
):
    step = pl.program_id(0)
    last = pl.num_programs(0) - 1
    half = own_ref.shape[1] // 3
    d_hidden = None
    for part, weight in enumerate((own_ref, par_ref)):
        cols = slice(part * half, (part + 1) * half)
        joined = jnp.concatenate([dq_ref[:, cols], dk_ref[:, cols], dv_ref[:, cols]], 1)
        made = nt(joined, weight[...])
        d_hidden = made if d_hidden is None else d_hidden + made

    @pl.when(step == 0)
    def _():
        sums_ref[...] = jnp.zeros_like(sums_ref)

    def add_sums(xhat):
        sums_ref[0:1, :] += jnp.sum(d_hidden * xhat, axis=0, keepdims=True)
        sums_ref[1:2, :] += jnp.sum(d_hidden, axis=0, keepdims=True)

    @pl.when(step < last)
    def _():
        xhat, inv = normed(x_ref[...].astype(F32))
        tokens_ref[...] = dmid_ref[...] + norm_back(xhat, inv, gain_ref[...], d_hidden)
        add_sums(xhat)

    @pl.when(step == last)
    def _():
        xhat, _ = normed(xg_ref[...].astype(F32))
        glob_ref[...] = d_hidden.astype(BF16)
        add_sums(xhat)


def input_back(dq, dk, dv, w_own, w_par, x, x_glob, d_mid, gain):
    rows_all, dim = dq.shape
    tiles = rows_all // TILE
    row = pl.BlockSpec((TILE, dim), lambda i: (i, 0))
    local = pl.BlockSpec((TILE, dim), lambda i: (jnp.minimum(i, tiles - 2), 0))
    return pl.pallas_call(
        input_back_body,
        grid=(tiles,),
        in_specs=[
            row, row, row, full(w_own.shape), full(w_par.shape), local, full(x_glob.shape), row,
            full((1, dim)),
        ],
        out_specs=[local, full(x_glob.shape), full((8, dim))],
        out_shape=[
            jax.ShapeDtypeStruct(x.shape, F32),
            jax.ShapeDtypeStruct(x_glob.shape, BF16),
            jax.ShapeDtypeStruct((8, dim), F32),
        ],
        compiler_params=params(),
        cost_estimate=cost(6 * rows_all * dim * dim, rows_all * dim * 16 + 6 * dim * dim),
        name="input_back",
    )(dq, dk, dv, w_own, w_par, x, x_glob, d_mid, gain)


def glob_input_body(own_ref, par_ref, x_ref, dmid_ref, gain_ref, out_ref):
    d_hidden = own_ref[...].astype(F32) + par_ref[...].astype(F32)
    xhat, inv = normed(x_ref[...].astype(F32))
    out_ref[...] = dmid_ref[...] + norm_back(xhat, inv, gain_ref[...], d_hidden)


def glob_input(kept, received, x, d_mid, gain):
    return pl.pallas_call(
        glob_input_body,
        out_shape=jax.ShapeDtypeStruct(x.shape, F32),
        name="glob_input",
    )(kept, received, x, d_mid, gain)


def block_layout(doc_blocks, doc_tail, first_block, block_count, block_len):
    doc_ends = jnp.cumsum(doc_blocks)
    block_ids = first_block + jnp.arange(block_count, dtype=jnp.int32)
    doc_of = jnp.sum((block_ids[:, None] >= doc_ends[None, :]).astype(jnp.int32), axis=1)
    picked = doc_of[:, None] == jnp.arange(doc_ends.shape[0], dtype=jnp.int32)[None, :]
    last_end = jnp.sum(jnp.where(picked, doc_ends[None, :], 0), axis=1)
    tail_len = jnp.sum(jnp.where(picked, doc_tail[None, :], 0), axis=1)
    tail_all = jnp.where(block_ids == last_end - 1, tail_len, block_len)
    key_valid = jnp.arange(block_len, dtype=jnp.int32)[None, :] < tail_all[:, None]
    return (doc_of, key_valid)


def per_device(
    tokens, glob_tokens, w_query, b_query, w_key, w_value, b_value, w_out, b_out, w_up, b_up,
    w_down, b_down, gain_attn, shift_attn, gain_ffn, shift_ffn, doc_blocks, doc_tail,
    grad_tokens, grad_glob,
):
    seq_size = lax.axis_size("seq")
    seq_pos = lax.axis_index("seq")
    tp_pos = lax.axis_index("tp")
    rows, dim = tokens.shape
    own_glob = glob_tokens.shape[0]
    half = w_query.shape[1]
    pairs = 2 * half // PAIR
    blocks = rows // BLOCK
    glob_rows = 2 * GLOB
    rows_all = rows + glob_rows
    group_size = GROUP_BLOCKS // (2 * blocks)
    group_bits = group_size.bit_length() - 1
    seq_bits = seq_size.bit_length() - 1
    group_pos = seq_pos % group_size
    own_first = (group_pos * 2 + tp_pos) * own_glob

    def flip(value, bit):
        return lax.ppermute(value, "seq", [(s, s ^ (1 << bit)) for s in range(seq_size)])

    def swap(value):
        return lax.ppermute(value, "tp", [(0, 1), (1, 0)])

    def row_vec(vector):
        return vector.reshape(1, -1)

    qkv_own = jnp.concatenate([w_query, w_key, w_value], 1)
    qkv_par = swap(qkv_own)
    out_par = swap(w_out)
    up_par = swap(w_up)
    down_par = swap(w_down)
    vec_own = jnp.concatenate([b_query, b_value, b_up])
    vec_par = swap(vec_own)

    gathered = jnp.stack([glob_tokens, grad_glob])[None]
    for bit in range(group_bits):
        upper = (group_pos >> bit) & 1 == 1
        other = flip(gathered, bit)
        gathered = jnp.where(
            upper,
            jnp.concatenate([other, gathered], 0),
            jnp.concatenate([gathered, other], 0),
        )
    other = swap(gathered)
    gathered = jnp.where(
        tp_pos == 1, jnp.stack([other, gathered], 1), jnp.stack([gathered, other], 1)
    )
    x_glob = gathered[:, :, 0].reshape(glob_rows, dim)
    dz_glob = gathered[:, :, 1].reshape(glob_rows, dim)
    dz_all = jnp.concatenate([grad_tokens, dz_glob], 0)

    first_block = (seq_pos * 2 + tp_pos) * blocks
    doc_of, key_valid = block_layout(doc_blocks, doc_tail, first_block, blocks, BLOCK)
    docs = doc_of - (seq_pos // group_size) * 2
    slot = jnp.arange(LANES, dtype=jnp.int32)[None, :] % HD
    valid = key_valid.reshape(-1)
    key_doc = jnp.concatenate(
        [jnp.repeat(docs, BLOCK), jnp.arange(glob_rows, dtype=jnp.int32) // GLOB]
    )
    is_glob = jnp.arange(rows_all) >= rows
    usable = jnp.concatenate([valid, jnp.ones((glob_rows,), bool)])
    closed = jnp.where(
        slot == 0,
        ~usable[:, None],
        jnp.where(
            slot == 3,
            is_glob[:, None],
            ((slot == 1) | (slot == 2)) & ~(usable & True)[:, None]
            | ((slot == 1) & (key_doc != 0)[:, None])
            | ((slot == 2) & (key_doc != 1)[:, None]),
        ),
    )
    augk = jnp.where(closed, NEG, 0.0).astype(BF16)
    glob_ids = jnp.arange(glob_rows, dtype=jnp.int32)
    owned = (glob_ids >= own_first) & (glob_ids < own_first + own_glob)
    augq = (
        ((slot == 1) & (glob_ids < GLOB)[:, None])
        | ((slot == 2) & (glob_ids >= GLOB)[:, None])
        | ((slot == 3) & ~owned[:, None])
    ).astype(BF16)
    mask_glob = owned.astype(F32)[:, None]
    mask_all = jnp.concatenate([jnp.ones((rows, 1), F32), mask_glob], 0)

    none = jnp.zeros((half,), F32)
    bias = row_vec(
        jnp.concatenate([b_query, none, b_value, vec_par[:half], none, vec_par[half : 2 * half]])
    )
    scale = row_vec(jnp.tile(jnp.repeat(jnp.array([SCALE, 1.0, 1.0], F32), half), 2))
    gain_a, shift_a, gain_f, shift_f = map(row_vec, (gain_attn, shift_attn, gain_ffn, shift_ffn))
    held = project(tokens, gain_a, shift_a, qkv_own, qkv_par, bias, scale, rows_all, 0)
    qkv, hidden_turned = project(
        x_glob, gain_a, shift_a, qkv_own, qkv_par, bias, scale, rows_all, rows // TILE, held
    )

    part = glob_forward(qkv, augk, augq, pairs)
    mine, theirs = part[:pairs], part[pairs:]
    state = merge(mine, swap(theirs))
    for bit in range(group_bits):
        state = merge(state, flip(state, bit))
    state_par = swap(state)
    high, low, out_turned, lse = local_forward(docs, qkv, augk, pairs, blocks)
    bias_out = row_vec(b_out)
    held = middle_local(high, tokens, w_out, out_par, bias_out, gain_f, shift_f)
    middle, hidden, ffn_turned, high, low, out_turned, lse_glob = middle_glob(
        state, state_par, x_glob, w_out, out_par, bias_out, gain_f, shift_f,
        [*held, high, low, out_turned],
    )

    b_up_par = row_vec(vec_par[2 * half :])
    dn_par, add_par, ffn_grad_par, up_sum_par = ffn_half(
        hidden, ffn_turned, dz_all, up_par, b_up_par, down_par, mask_glob
    )
    dn_own, add_own, ffn_grad_own, up_sum_own = ffn_half(
        hidden, ffn_turned, dz_all, w_up, row_vec(b_up), w_down, mask_glob
    )

    def add_pair(own, received):
        return (own.astype(F32) + received.astype(F32)).astype(BF16)

    def order_of(step):
        if seq_bits < 2:
            return step, step
        return step, (1, 0, *range(2, seq_bits))[step]

    def trade(value, step):
        zero, one = order_of(step)
        links = [(2 * s, 2 * (s ^ (1 << zero))) for s in range(seq_size)]
        links += [(2 * s + 1, 2 * (s ^ (1 << one)) + 1) for s in range(seq_size)]
        return lax.ppermute(value, ("seq", "tp"), links)

    def side_of(step):
        zero, one = order_of(step)
        return (seq_pos >> jnp.where(tp_pos == 0, zero, one)) & 1

    def reduce_all(value):
        for step in range(seq_bits):
            count = value.shape[0] // 2
            side = side_of(step)
            leaving = lax.dynamic_slice_in_dim(value, (1 - side) * count, count, 0)
            staying = lax.dynamic_slice_in_dim(value, side * count, count, 0)
            value = add_pair(staying, trade(leaving, step))
        for step in reversed(range(seq_bits)):
            side = side_of(step) == 1
            other = trade(value, step)
            value = jnp.where(
                side, jnp.concatenate([other, value], 0), jnp.concatenate([value, other], 0)
            )
        return value

    ffn_sum = reduce_all(
        add_pair(ffn_grad_own, swap(ffn_grad_par)).reshape(-1, LANES)
    )

    d_mid, d_attn, delta, out_grad, mid_sums = middle_back(
        dn_par, dn_own, middle, dz_all, high, low, out_turned, w_out, out_par, gain_f, mask_all
    )
    dq, dk, dv = attention_back(docs, qkv, d_attn, lse, lse_glob, delta, augk, augq, pairs)
    qkv_grad_par, qkv_sum_par = project_grad(hidden_turned, dq, dk, dv, 1)
    qkv_grad_own, qkv_sum_own = project_grad(hidden_turned, dq, dk, dv, 0)
    tokens_grad, d_hidden_glob, in_sums = input_back(
        dq, dk, dv, qkv_own, qkv_par, tokens, x_glob, d_mid, gain_a
    )

    rest = jnp.concatenate([mid_sums[:4], in_sums[:2]], 0).reshape(-1)

    def pack(qkv_grad, out_part, qkv_sum, up_sum):
        small = jnp.concatenate([rest, qkv_sum[0], qkv_sum[1], up_sum.reshape(-1)])
        small = small.reshape(-1, LANES).astype(BF16)
        whole = jnp.concatenate([qkv_grad.reshape(-1, LANES), out_part, small], 0)
        unit = 16 * seq_size
        return jnp.pad(whole, ((0, -whole.shape[0] % unit), (0, 0)))

    tail_own = pack(qkv_grad_own, out_grad[0], qkv_sum_own, up_sum_own)
    tail_par = pack(qkv_grad_par, out_grad[1], qkv_sum_par, up_sum_par)
    tail_sum = reduce_all(add_pair(tail_own, swap(tail_par)))

    shares = d_hidden_glob.reshape(group_size, 2, own_glob, dim)
    kept = lax.dynamic_index_in_dim(shares, tp_pos, 1, keepdims=False)
    sent = lax.dynamic_index_in_dim(shares, 1 - tp_pos, 1, keepdims=False)
    current = add_pair(kept, swap(sent))
    for bit in reversed(range(group_bits)):
        count = current.shape[0] // 2
        side = (group_pos >> bit) & 1
        sent = lax.dynamic_slice_in_dim(current, (1 - side) * count, count, 0)
        kept = lax.dynamic_slice_in_dim(current, side * count, count, 0)
        received = flip(sent, bit)
        if bit:
            current = add_pair(kept, received)
    d_mid_own = lax.dynamic_slice_in_dim(d_mid, rows + own_first, own_glob, 0)
    glob_grad = glob_input(kept[0], received[0], glob_tokens, d_mid_own, gain_a)

    out_tokens = (middle[:rows] + add_par[:rows] + add_own[:rows] + b_down).astype(BF16)

    def own_rows(array_in):
        return lax.dynamic_slice_in_dim(array_in, rows + own_first, own_glob, 0)

    out_glob = (own_rows(middle) + own_rows(add_par) + own_rows(add_own) + b_down).astype(BF16)
    units = w_up.shape[1]
    chunks = units // TILE
    ffn_sum = ffn_sum.reshape(chunks, -1, LANES)
    cut = TILE * dim // LANES
    up_grad = (
        ffn_sum[:, :cut]
        .reshape(chunks, TILE // LANES, dim, LANES)
        .transpose(2, 0, 1, 3)
        .reshape(dim, units)
        .astype(F32)
    )
    down_grad = (
        ffn_sum[:, cut:]
        .reshape(chunks, dim // LANES, TILE, LANES)
        .transpose(0, 2, 1, 3)
        .reshape(units, dim)
        .astype(F32)
    )
    count = 3 * half * dim // LANES
    qkv_all = (
        tail_sum[:count].reshape(3, half // LANES, dim, LANES).transpose(0, 2, 1, 3).astype(F32)
    ).reshape(3, dim, half)
    out_all = (
        tail_sum[count : count + half * dim // LANES]
        .reshape(dim // LANES, half, LANES)
        .transpose(1, 0, 2)
        .reshape(half, dim)
        .astype(F32)
    )
    small = tail_sum[count + half * dim // LANES :].reshape(-1).astype(F32)
    shared = small[: 6 * dim]
    shared = jnp.where(tp_pos == 0, shared, swap(shared))
    gain_f_grad, shift_f_grad, out_bias, down_bias, gain_a_grad, shift_a_grad = (
        shared.reshape(6, dim)
    )
    b_query_grad = small[6 * dim : 6 * dim + half]
    b_value_grad = small[6 * dim + half : 6 * dim + 2 * half]
    b_up_grad = small[6 * dim + 2 * half : 6 * dim + 2 * half + units]
    return (
        out_tokens, out_glob, tokens_grad, glob_grad, qkv_all[0], b_query_grad, qkv_all[1],
        qkv_all[2], b_value_grad, out_all, out_bias, up_grad, b_up_grad, down_grad, down_bias,
        gain_a_grad, shift_a_grad, gain_f_grad, shift_f_grad,
    )


def solution(mesh):
    rows = P(("seq", "tp"), None)
    cols, part, whole = P(None, "tp"), P("tp"), P()
    lines = P("tp", None)
    return jax.shard_map(
        per_device,
        mesh=mesh,
        in_specs=(
            rows, rows, cols, part, cols, cols, part, lines, whole, cols, part, lines, whole,
            whole, whole, whole, whole, whole, whole, rows, rows,
        ),
        out_specs=(
            rows, rows, rows, rows, cols, part, cols, cols, part, lines, whole, cols, part, lines,
            whole, whole, whole, whole, whole,
        ),
        check_vma=False,
    )
```

```python
import functools

import jax
import jax.numpy as jnp
from jax import lax
from jax.experimental import pallas as pl
from jax.experimental.pallas import tpu as pltpu
from jax.sharding import PartitionSpec as P

HD = 64
BLOCK = 512
GLOB = 128
GROUP_BLOCKS = 32
EPS = 1e-05
SCALE = 0.125
NEG = -1e30
TILE = 256
PAIR = 2 * HD
LANES = 128
STATS = 16
HEAD_ROWS = 16
FFN_CHUNK = 384
F32 = jnp.float32
BF16 = jnp.bfloat16
VMEM_BYTES = 16 * 2**20


def nn(left, right):
    return jnp.dot(left, right, preferred_element_type=F32)


def nt(left, right):
    return lax.dot_general(left, right, (((1,), (1,)), ((), ())), preferred_element_type=F32)


def tn(left, right):
    return lax.dot_general(left, right, (((0,), (0,)), ((), ())), preferred_element_type=F32)


def normed(values):
    row_mean = jnp.mean(values, axis=-1, keepdims=True)
    centred = values - row_mean
    row_var = jnp.mean(centred * centred, axis=-1, keepdims=True)
    inv = lax.rsqrt(row_var + EPS)
    return centred * inv, inv


def norm_back(xhat, inv, gain_vec, cotangent):
    scaled = cotangent * gain_vec
    mean_one = jnp.mean(scaled, axis=-1, keepdims=True)
    mean_two = jnp.mean(scaled * xhat, axis=-1, keepdims=True)
    return inv * (scaled - mean_one - xhat * mean_two)


def full(shape):
    zeros = (0,) * len(shape)
    return pl.BlockSpec(shape, lambda *_: zeros, pipeline_mode=pl.Buffered(1))


ANY = pl.BlockSpec(memory_space=pl.ANY)


def launch(
    body, name, grid, operands, outs, work, prefetch=(), held=(), after=(), scratch=(), aliased=0
):
    arrays = [*prefetch, *(a for a, _ in operands), *held, *after]
    specs = [*(spec for _, spec in operands), *([ANY] * (len(held) + len(after)))]
    first = len(prefetch) + len(operands)
    spare = len(held) + len(after)

    def whole(*refs):
        return body(*refs[:first], *refs[first + spare :])

    return pl.pallas_call(
        whole,
        grid_spec=pltpu.PrefetchScalarGridSpec(
            num_scalar_prefetch=len(prefetch),
            grid=grid,
            in_specs=specs,
            out_specs=[spec for _, _, spec in outs],
            scratch_shapes=list(scratch),
        ),
        out_shape=[jax.ShapeDtypeStruct(shape, kind) for shape, kind, _ in outs],
        input_output_aliases={first + i: aliased + i for i in range(len(held))},
        compiler_params=pltpu.CompilerParams(
            vmem_limit_bytes=VMEM_BYTES, dimension_semantics=("arbitrary",) * len(grid)
        ),
        cost_estimate=work,
        name=name,
    )(*arrays)


def cost(flops, nbytes, trans=0):
    return pl.CostEstimate(flops=int(flops), bytes_accessed=int(nbytes), transcendentals=int(trans))


def head_lanes(head):
    lane = lax.broadcasted_iota(jnp.int32, (1, LANES), 1)
    here = jnp.where(lane < HD, 1.0, 0.0)
    mine = here if head == 0 else 1.0 - here
    return mine.astype(BF16), (1.0 - mine).astype(BF16)


def lane_one(slot):
    lane = lax.broadcasted_iota(jnp.int32, (1, LANES), 1)
    return jnp.where((lane == slot) | (lane == slot + HD), 1.0, 0.0).astype(BF16)


def layout_body(place_ref, blocks_ref, tails_ref, docs_ref, augk_ref, augq_ref, mask_ref):
    first_block, group_first, own_first = place_ref[0], place_ref[1], place_ref[2]
    own_count = place_ref[3]
    count = augq_ref.shape[0]
    rows = augk_ref.shape[0] - count
    lane = lax.broadcasted_iota(jnp.int32, (1, LANES), 1)
    slot = jnp.where(lane < HD, lane, lane - HD)
    for block in range(rows // BLOCK):
        index = first_block + block
        start, doc, real = jnp.int32(0), jnp.int32(0), jnp.int32(BLOCK)
        for number in range(blocks_ref.shape[0]):
            end = start + blocks_ref[number]
            inside = jnp.logical_and(index >= start, index < end)
            doc = jnp.where(inside, number, doc)
            real = jnp.where(
                jnp.logical_and(inside, index == end - 1), tails_ref[number], real
            )
            start = end
        doc = doc - group_first
        docs_ref[block] = doc
        row = lax.broadcasted_iota(jnp.int32, (BLOCK, 1), 0)
        padded = row >= real
        shut = ((slot == 1) & (doc != 0)) | ((slot == 2) & (doc != 1))
        shut = jnp.where(shut, 1, 0) + jnp.where(padded & (slot < 3), 1, 0)
        augk_ref[block * BLOCK : (block + 1) * BLOCK, :] = jnp.where(shut > 0, NEG, 0.0).astype(BF16)
    row = lax.broadcasted_iota(jnp.int32, (count, 1), 0)
    late = row >= GLOB
    shut = ((slot == 1) & late) | ((slot == 2) & ~late) | (slot == 3)
    augk_ref[rows:, :] = jnp.where(shut, NEG, 0.0).astype(BF16)
    owned = (row >= own_first) & (row < own_first + own_count)
    on = ((slot == 1) & ~late) | ((slot == 2) & late) | ((slot == 3) & ~owned)
    augq_ref[...] = jnp.where(on, 1.0, 0.0).astype(BF16)
    mask_ref[:rows, :] = jnp.ones((rows, 1), F32)
    mask_ref[rows:, :] = jnp.where(owned, 1.0, 0.0)


def layout(place, doc_blocks, doc_tail, rows_all, count, blocks):
    smem = pl.BlockSpec(memory_space=pltpu.SMEM)
    return launch(
        layout_body,
        "layout",
        (1,),
        [],
        [
            ((blocks,), jnp.int32, smem),
            ((rows_all, LANES), BF16, full((rows_all, LANES))),
            ((count, LANES), BF16, full((count, LANES))),
            ((rows_all, 1), F32, full((rows_all, 1))),
        ],
        cost(0, rows_all * LANES * 4),
        prefetch=(place, doc_blocks, doc_tail),
    )


def order_body(place_ref, mine_ref, theirs_ref, grads_ref, x_ref, dz_ref):
    step = pl.program_id(0)
    last = pl.num_programs(0) - 1
    chips, _, own, _ = mine_ref.shape

    @pl.when(step < last)
    def _():
        dz_ref[...] = grads_ref[...]

    @pl.when(step == last)
    def _():
        for chip in range(chips):
            for side, ref in enumerate((mine_ref, theirs_ref)):
                spot = (place_ref[4] ^ chip) * 2 + (place_ref[5] ^ side)
                here = pl.ds(pl.multiple_of(spot * own, own), own)
                x_ref[here, :] = ref[chip, 0]
                dz_ref[here, :] = ref[chip, 1]


def order_rows(place, mine, theirs, grads, after=()):
    chips, _, own, dim = mine.shape
    count = chips * 2 * own
    tiles = grads.shape[0] // count
    return launch(
        order_body,
        "order_rows",
        (tiles + 1,),
        [
            (mine, full(mine.shape)),
            (theirs, full(mine.shape)),
            (grads, pl.BlockSpec((count, dim), lambda i, place: (jnp.minimum(i, tiles - 1), 0))),
        ],
        [
            ((count, dim), BF16, full((count, dim))),
            (
                (grads.shape[0] + count, dim),
                BF16,
                pl.BlockSpec((count, dim), lambda i, place: (i, 0)),
            ),
        ],
        cost(0, 4 * grads.size),
        prefetch=(place,),
        after=after,
    )


def project_body(x_ref, vecs_ref, halves_ref, own_ref, par_ref, qkv_ref, turned_ref):
    xhat, _ = normed(x_ref[...].astype(F32))
    hidden = (xhat * vecs_ref[0:1, :] + vecs_ref[1:2, :]).astype(BF16)
    turned_ref[...] = hidden.T
    width = own_ref.shape[1]
    third = width // 3
    for half, weight in enumerate((own_ref, par_ref)):
        first = half * width
        made = nn(hidden, weight[...])
        bias = halves_ref[half : half + 1, : 2 * third]
        qkv_ref[:, first : first + third] = (
            (made[:, :third] + bias[:, :third]) * SCALE
        ).astype(BF16)
        qkv_ref[:, first + third : first + 2 * third] = made[:, third : 2 * third].astype(BF16)
        qkv_ref[:, first + 2 * third : first + width] = (
            made[:, 2 * third :] + bias[:, third:]
        ).astype(BF16)


def project(x, vecs, halves, w_own, w_par, rows_all, first, count, held=(), after=()):
    dim = x.shape[1]
    width = 2 * w_own.shape[1]
    shift = first if first + count <= x.shape[0] // TILE else 0
    return launch(
        project_body,
        "project",
        (count,),
        [
            (x, pl.BlockSpec((TILE, dim), lambda i: (i + shift, 0))),
            (vecs, full(vecs.shape)),
            (halves, full(halves.shape)),
            (w_own, full(w_own.shape)),
            (w_par, full(w_par.shape)),
        ],
        [
            ((rows_all, width), BF16, pl.BlockSpec((TILE, width), lambda i: (i + first, 0))),
            ((dim, rows_all), BF16, pl.BlockSpec((dim, TILE), lambda i: (0, i + first))),
        ],
        cost(2 * count * TILE * dim * width, 2 * (count * TILE * (2 * dim + width) + dim * width)),
        held=held,
        after=after,
    )


def pair_column(kind, pairs):
    half = pairs // 2
    return lambda p: (p // half) * 3 * half + kind * half + p % half


def write_stats(out_ref, head, lse):
    first = lse.astype(BF16).astype(F32)
    second = (lse - first).astype(BF16).astype(F32)
    third = lse - first - second
    row = lax.broadcasted_iota(jnp.int32, (STATS, lse.shape[1]), 0)
    held = jnp.where(row == 0, first, jnp.where(row == 1, second, jnp.where(row == 2, third, 0.0)))
    out_ref[head, HD : HD + STATS, :] = held.astype(BF16)


def read_stats(ref, head):
    held = ref[head, HD : HD + STATS, :].astype(F32)
    return held[0:1] + held[1:2] + held[2:3]


def glob_forward_body(q_ref, k_ref, v_ref, augk_ref, augq_ref, own_ref, par_ref):
    rows_all = k_ref.shape[0]
    count = augq_ref.shape[0]
    queries = q_ref[rows_all - count :, :]
    keys = k_ref[...]
    values_turned = v_ref[...].T
    half = pl.num_programs(0) // 2
    for head in range(2):
        mine, other = head_lanes(head)
        key_head = keys * mine + augk_ref[...] * other
        query_head = queries * mine + augq_ref[...] * other
        scores = nt(key_head, query_head)
        top = jnp.max(scores, axis=0, keepdims=True)
        weights = jnp.exp(scores - top)
        total = jnp.sum(weights, axis=0, keepdims=True)
        summed = nn(values_turned[head * HD : (head + 1) * HD, :], weights.astype(BF16))
        summed = (summed / total).astype(BF16)
        lse = top + jnp.log(total)
        for ref, here in ((par_ref, pl.program_id(0) < half), (own_ref, pl.program_id(0) >= half)):

            @pl.when(here)
            def _(ref=ref, summed=summed, lse=lse, head=head):
                ref[head, :HD, :] = summed
                write_stats(ref, head, lse)


def glob_forward(qkv, augk, augq, pairs):
    rows_all = qkv.shape[0]
    count = augq.shape[0]
    half = pairs // 2

    def block(kind):
        column = pair_column(kind, pairs)
        return (qkv, pl.BlockSpec((rows_all, LANES), lambda p: (0, column((p + half) % pairs))))

    work = 2 * pairs * rows_all * count
    shape = (pairs, HD + STATS, count)
    size = (2, HD + STATS, count)
    return launch(
        glob_forward_body,
        "glob_forward",
        (pairs,),
        [block(0), block(1), block(2), (augk, full(augk.shape)), (augq, full(augq.shape))],
        [
            (shape, BF16, pl.BlockSpec(size, lambda p: (jnp.maximum(p - half, 0), 0, 0))),
            (shape, BF16, pl.BlockSpec(size, lambda p: (jnp.minimum(p, half - 1), 0, 0))),
        ],
        cost(work * 2 * 512, qkv.size * 2, work),
    )


def merge_body(left_ref, right_ref, out_ref):
    for head in range(left_ref.shape[0]):
        lse_left, lse_right = read_stats(left_ref, head), read_stats(right_ref, head)
        top = jnp.maximum(lse_left, lse_right)
        weight_left, weight_right = jnp.exp(lse_left - top), jnp.exp(lse_right - top)
        total = weight_left + weight_right
        out_left = left_ref[head, :HD, :].astype(F32)
        out_right = right_ref[head, :HD, :].astype(F32)
        merged = (out_left * weight_left + out_right * weight_right) / total
        out_ref[head, :HD, :] = merged.astype(BF16)
        write_stats(out_ref, head, top + jnp.log(total))


def merge(left, right, after=()):
    spec = full(left.shape)
    return launch(
        merge_body, "merge", (1,), [(left, spec), (right, spec)], [(left.shape, BF16, spec)],
        cost(left.size * 8, left.size * 6), after=after,
    )[0]


def local_forward_body(
    docs_ref, q_ref, k_ref, v_ref, kg_ref, vg_ref, augk_ref, high_ref, low_ref, turned_ref, lse_ref
):
    keys = jnp.concatenate([k_ref[...], kg_ref[...]], 0)
    values_turned = jnp.concatenate([v_ref[...], vg_ref[...]], 0).T
    bias = jnp.concatenate([augk_ref[...], jnp.zeros((GLOB, LANES), BF16)], 0)
    outs = []
    for head in range(2):
        mine, other = head_lanes(head)
        key_head = keys * mine + bias * other
        query_head = q_ref[...] * mine + lane_one(0) * other
        scores = nt(key_head, query_head)
        top = jnp.max(scores, axis=0, keepdims=True)
        weights = jnp.exp(scores - top)
        total = jnp.sum(weights, axis=0, keepdims=True)
        summed = nn(values_turned[head * HD : (head + 1) * HD, :], weights.astype(BF16))
        outs.append(summed / total)
        lse_ref[0, 0, head : head + 1, :] = top + jnp.log(total)
    turned = jnp.concatenate(outs, 0)
    turned_ref[...] = turned.astype(BF16)
    straight = turned.T
    high = straight.astype(BF16)
    high_ref[...] = high
    low_ref[...] = (straight - high.astype(F32)).astype(BF16)


def local_forward(docs, qkv, augk, pairs, blocks, first, count, held=(), after=()):
    rows_all = qkv.shape[0]
    glob_first = blocks * BLOCK // GLOB

    def block(kind):
        column = pair_column(kind, pairs)
        return (
            qkv,
            pl.BlockSpec((BLOCK, LANES), lambda b, p, docs: (b, column(p + first))),
        )

    def glob_block(kind):
        column = pair_column(kind, pairs)
        return (
            qkv,
            pl.BlockSpec(
                (GLOB, LANES), lambda b, p, docs: (glob_first + docs[b], column(p + first))
            ),
        )

    work = 2 * count * blocks * BLOCK * (BLOCK + GLOB)
    width = pairs * LANES
    straight = pl.BlockSpec((BLOCK, LANES), lambda b, p, docs: (b, p + first))
    return launch(
        local_forward_body,
        "local_forward",
        (blocks, count),
        [
            block(0),
            block(1),
            block(2),
            glob_block(1),
            glob_block(2),
            (augk, pl.BlockSpec((BLOCK, LANES), lambda b, p, docs: (b, 0))),
        ],
        [
            ((rows_all, width), BF16, straight),
            ((rows_all, width), BF16, straight),
            (
                (width, rows_all),
                BF16,
                pl.BlockSpec((LANES, BLOCK), lambda b, p, docs: (p + first, b)),
            ),
            (
                (blocks, pairs, 2, BLOCK),
                F32,
                pl.BlockSpec((1, 1, 2, BLOCK), lambda b, p, docs: (b, p + first, 0, 0)),
            ),
        ],
        cost(work * 2 * 512, count * rows_all * LANES * 12, work),
        prefetch=(docs,),
        held=held,
        after=after,
    )


def middle_of(out_high, x, own_ref, par_ref, vecs_ref):
    half = own_ref.shape[0]
    branch = nn(out_high[:, :half], own_ref[...]) + nn(out_high[:, half:], par_ref[...])
    middle = x.astype(F32) + branch + vecs_ref[4:5, :]
    xhat, _ = normed(middle)
    hidden = (xhat * vecs_ref[2:3, :] + vecs_ref[3:4, :]).astype(BF16)
    return middle, hidden


def middle_body(out_ref, x_ref, own_ref, par_ref, vecs_ref, mid_ref, hid_ref, turned_ref):
    middle, hidden = middle_of(out_ref[...], x_ref[...], own_ref, par_ref, vecs_ref)
    mid_ref[...] = middle
    hid_ref[...] = hidden
    turned_ref[...] = hidden.T


def middle_local(out_high, x, w_own, w_par, vecs, after=()):
    rows_all, dim = out_high.shape
    rows = x.shape[0]
    row = pl.BlockSpec((TILE, dim), lambda i: (i, 0))
    return launch(
        middle_body,
        "middle_local",
        (rows // TILE,),
        [
            (out_high, row),
            (x, row),
            (w_own, full(w_own.shape)),
            (w_par, full(w_par.shape)),
            (vecs, full(vecs.shape)),
        ],
        [
            ((rows_all, dim), F32, row),
            ((rows_all, dim), BF16, row),
            ((dim, rows_all), BF16, pl.BlockSpec((dim, TILE), lambda i: (0, i))),
        ],
        cost(2 * rows * dim * dim, 12 * rows * dim + 2 * dim * dim),
        after=after,
    )


def middle_glob_body(
    own_out_ref, par_out_ref, x_ref, own_ref, par_ref, vecs_ref,
    mid_ref, hid_ref, turned_ref, high_ref, low_ref, out_turned_ref, lse_ref,
):
    heads = own_out_ref.shape[0]
    parts = [own_out_ref[head, :HD, :] for head in range(heads)]
    parts += [par_out_ref[head, :HD, :] for head in range(heads)]
    turned = jnp.concatenate(parts, 0)
    out_turned_ref[...] = turned
    high = turned.T
    high_ref[...] = high
    low_ref[...] = jnp.zeros_like(high)
    stats = [read_stats(own_out_ref, head) for head in range(heads)]
    stats += [read_stats(par_out_ref, head) for head in range(heads)]
    spare = lse_ref.shape[0] - 2 * heads
    lse_ref[...] = jnp.concatenate(stats + [jnp.zeros((spare, x_ref.shape[0]), F32)], 0)
    middle, hidden = middle_of(high, x_ref[...], own_ref, par_ref, vecs_ref)
    mid_ref[...] = middle
    hid_ref[...] = hidden
    turned_ref[...] = hidden.T


def middle_glob(own_out, par_out, x, w_own, w_par, vecs, held):
    rows, dim = x.shape
    first = held[0].shape[0] // rows - 1
    row = pl.BlockSpec((rows, dim), lambda i: (first, 0))
    col = pl.BlockSpec((dim, rows), lambda i: (0, first))
    operands = [own_out, par_out, x, w_own, w_par, vecs]
    specs = [row, row, col, row, row, col]
    return launch(
        middle_glob_body,
        "middle_glob",
        (1,),
        [(a, full(a.shape)) for a in operands],
        [(h.shape, h.dtype, spec) for h, spec in zip(held, specs)]
        + [((HEAD_ROWS, rows), F32, full((HEAD_ROWS, rows)))],
        cost(2 * rows * dim * dim, 12 * rows * dim + 2 * dim * dim),
        held=held,
    )


def ffn_body(
    hid_ref, turned_ref, dz_ref, up_ref, bias_ref, down_ref, mask_ref, *rest, chunks, which
):
    dn_in_ref = rest[0] if len(rest) == 8 else None
    dnorm_ref, act_ref, grads_ref, bias_grad_ref, act_s, dup_s, sum_s = rest[-7:]
    step = pl.program_id(0)
    rows_all, dim = hid_ref.shape
    chunk = bias_grad_ref.shape[1]
    tail = slice(rows_all - mask_ref.shape[0], rows_all)

    @pl.when(step < chunks)
    def _():
        cols = pl.ds(pl.multiple_of(step * chunk, chunk), chunk)
        up = nn(hid_ref[...], up_ref[:, cols]) + bias_ref[which : which + 1, :]
        share = 0.5 * (1.0 + lax.erf(up * (2.0**-0.5)))
        density = jnp.exp(up * up * -0.5) * 0.3989422804014327
        active = (up * share).astype(BF16)
        slope = share + up * density
        d_up = (nt(dz_ref[...], down_ref[cols, :]) * slope).astype(BF16)
        act_ref[...] = active
        dup_s[:, cols] = d_up
        act_s[...] = active
        sum_s[...] = d_up
        mask = mask_ref[...]
        act_s[tail, :] = (active[tail].astype(F32) * mask).astype(BF16)
        sum_s[tail, :] = (d_up[tail].astype(F32) * mask).astype(BF16)
        bias_grad_ref[...] = jnp.sum(sum_s[...].astype(F32), axis=0, keepdims=True)
        up_grad = nn(turned_ref[...], sum_s[...]).astype(BF16)
        down_grad = tn(act_s[...], dz_ref[...]).astype(BF16)
        place = 0
        for grad in (up_grad, down_grad):
            rows = grad.shape[0]
            for col in range(grad.shape[1] // LANES):
                grads_ref[0, place : place + rows, :] = grad[:, col * LANES : (col + 1) * LANES]
                place += rows

    @pl.when(step >= chunks)
    def _():
        start = pl.multiple_of((step - chunks) * TILE, TILE)
        made = nt(dup_s[pl.ds(start, TILE), :], up_ref[...])
        dnorm_ref[...] = made if dn_in_ref is None else made + dn_in_ref[...]


def ffn_part(hidden, turned, dz, w_up, halves, w_down, mask, which, first, units, dn_in=None, after=()):
    rows_all, dim = hidden.shape
    half = w_up.shape[1]
    chunk = min(FFN_CHUNK, units)
    chunks = units // chunk
    skip = first // units
    packed = 2 * chunk * dim // LANES
    bias_first = (halves.shape[1] - half + first) // chunk

    def now(j):
        return jnp.minimum(j, chunks - 1)

    row = pl.BlockSpec((TILE, dim), lambda j: (jnp.maximum(j - chunks, 0), 0))
    tail = mask.shape[0] // TILE - 1
    one = pl.Buffered(1)
    operands = [
        (hidden, full(hidden.shape)),
        (turned, full(turned.shape)),
        (dz, full(dz.shape)),
        (w_up, pl.BlockSpec((dim, units), lambda j: (0, skip), pipeline_mode=one)),
        (halves, pl.BlockSpec((halves.shape[0], chunk), lambda j: (0, bias_first + now(j)))),
        (w_down, pl.BlockSpec((units, dim), lambda j: (skip, 0), pipeline_mode=one)),
        (mask, pl.BlockSpec((TILE, 1), lambda j: (tail, 0))),
    ]
    if dn_in is not None:
        operands.append((dn_in, row))
    return launch(
        functools.partial(ffn_body, chunks=chunks, which=which),
        "ffn_part",
        (chunks + rows_all // TILE,),
        operands,
        [
            ((rows_all, dim), F32, row),
            ((rows_all, units), BF16, pl.BlockSpec((rows_all, chunk), lambda j: (0, now(j)))),
            ((chunks, packed, LANES), BF16, pl.BlockSpec((1, packed, LANES), lambda j: (now(j), 0, 0))),
            ((1, units), F32, pl.BlockSpec((1, chunk), lambda j: (0, now(j)))),
        ],
        cost(10 * rows_all * dim * units, rows_all * dim * 14 + units * dim * 8, 2 * rows_all * units),
        after=after,
        scratch=[
            pltpu.VMEM((rows_all, chunk), BF16),
            pltpu.VMEM((rows_all, units), BF16),
            pltpu.VMEM((rows_all, chunk), BF16),
        ],
    )


def output_body(place_ref, mid_ref, vecs_ref, *rest):
    out_ref, glob_ref = rest[-2:]
    parts = len(rest) // 2 - 1
    made = mid_ref[...] + vecs_ref[5:6, :]
    for part in range(parts):
        made = made + nn(rest[part][...], rest[parts + part][...])
    step = pl.program_id(0)
    last = pl.num_programs(0) - 1

    @pl.when(step < last)
    def _():
        out_ref[...] = made.astype(BF16)

    @pl.when(step == last)
    def _():
        glob_ref[...] = made.astype(BF16)


def output_rows(place, middle, vecs, acts, weights, own, after=()):
    rows_all, dim = middle.shape
    tiles = rows_all // TILE
    rows = rows_all - TILE
    row = pl.BlockSpec((TILE, dim), lambda i, place: (i, 0))
    operands = [(middle, row), (vecs, full(vecs.shape))]
    operands += [
        (act, pl.BlockSpec((TILE, act.shape[1]), lambda i, place: (i, 0))) for act in acts
    ]
    for act, (weight, number) in zip(acts, weights):
        operands.append(
            (
                weight,
                pl.BlockSpec(
                    (act.shape[1], dim),
                    lambda i, place, number=number: (number, 0),
                    pipeline_mode=pl.Buffered(1),
                ),
            )
        )
    units = sum(act.shape[1] for act in acts)
    out, glob = launch(
        output_body,
        "output_rows",
        (tiles,),
        operands,
        [
            ((rows, dim), BF16, pl.BlockSpec((TILE, dim), lambda i, place: (jnp.minimum(i, tiles - 2), 0))),
            ((TILE, dim), BF16, full((TILE, dim))),
        ],
        cost(2 * rows_all * dim * units, rows_all * (units * 2 + dim * 6) + units * dim * 2),
        prefetch=(place,),
        after=after,
    )
    return out, glob


def middle_back_body(
    dn_ref, mid_ref, dz_ref, high_ref, low_ref, out_turned_ref, own_ref, par_ref, vecs_ref, mask_ref,
    dmid_ref, dattn_ref, delta_ref, grads_ref, sums_ref, acc_s,
):
    step = pl.program_id(0)
    dim = mid_ref.shape[1]
    half = own_ref.shape[0]
    xhat, inv = normed(mid_ref[...])
    dn = dn_ref[...]
    dz = dz_ref[...].astype(F32)
    d_mid = dz + norm_back(xhat, inv, vecs_ref[2:3, :], dn)
    dmid_ref[...] = d_mid
    d_branch = d_mid.astype(BF16)
    for part, weight in enumerate((own_ref, par_ref)):
        dattn_ref[:, part * half : (part + 1) * half] = nt(d_branch, weight[...]).astype(BF16)
    straight = high_ref[...].astype(F32) + low_ref[...].astype(F32)
    product = dattn_ref[...].astype(F32) * straight
    first = product.astype(BF16)
    second = (product - first.astype(F32)).astype(BF16)
    head = lax.broadcasted_iota(jnp.int32, (delta_ref.shape[0], dim), 0)
    column = lax.broadcasted_iota(jnp.int32, (delta_ref.shape[0], dim), 1)
    picked = jnp.where((column >= head * HD) & (column < (head + 1) * HD), 1.0, 0.0).astype(BF16)
    delta_ref[...] = nt(picked, first) + nt(picked, second)
    mask = mask_ref[...]
    masked = (d_branch.astype(F32) * mask).astype(BF16)
    made = nn(out_turned_ref[...], masked)
    sums = [
        jnp.sum(dn * xhat * mask, axis=0, keepdims=True),
        jnp.sum(dn * mask, axis=0, keepdims=True),
        jnp.sum(masked.astype(F32), axis=0, keepdims=True),
        jnp.sum(dz * mask, axis=0, keepdims=True),
    ]
    sums = jnp.concatenate(sums + [jnp.zeros((4, dim), F32)], 0)

    @pl.when(step == 0)
    def _():
        acc_s[...] = made
        sums_ref[...] = sums

    @pl.when(step > 0)
    def _():
        acc_s[...] += made
        sums_ref[...] += sums

    @pl.when(step == pl.num_programs(0) - 1)
    def _():
        for part in range(2):
            for col in range(dim // LANES):
                grads_ref[part, col * half : (col + 1) * half, :] = acc_s[
                    part * half : (part + 1) * half, col * LANES : (col + 1) * LANES
                ].astype(BF16)


def middle_back(dn, middle, dz, high, low, out_turned, w_own, w_par, vecs, mask, after=()):
    rows_all, dim = middle.shape
    row = pl.BlockSpec((TILE, dim), lambda i: (i, 0))
    col = pl.BlockSpec((dim, TILE), lambda i: (0, i))
    packed = w_own.size // LANES
    return launch(
        middle_back_body,
        "middle_back",
        (rows_all // TILE,),
        [
            (dn, row),
            (middle, row),
            (dz, row),
            (high, row),
            (low, row),
            (out_turned, col),
            (w_own, full(w_own.shape)),
            (w_par, full(w_par.shape)),
            (vecs, full(vecs.shape)),
            (mask, pl.BlockSpec((TILE, 1), lambda i: (i, 0))),
        ],
        [
            ((rows_all, dim), F32, row),
            ((rows_all, dim), BF16, row),
            ((HEAD_ROWS, rows_all), F32, pl.BlockSpec((HEAD_ROWS, TILE), lambda i: (0, i))),
            ((2, packed, LANES), BF16, full((2, packed, LANES))),
            ((8, dim), F32, full((8, dim))),
        ],
        cost(4 * rows_all * dim * dim, rows_all * dim * 24),
        after=after,
        scratch=[pltpu.VMEM((dim, dim), F32)],
    )


def attention_back_body(
    docs_ref, q_ref, k_ref, v_ref, do_ref, lse_ref, lseg_ref, delta_ref, augk_ref, augq_ref,
    dq_ref, dk_ref, dv_ref, key_s, value_s, turned_s, dk_s, dv_s, *, first,
):
    pair = pl.program_id(0) + first
    rows_all = q_ref.shape[0]
    count = augq_ref.shape[0]
    local_rows = rows_all - count
    blocks = local_rows // BLOCK
    turned_s[...] = k_ref[...].T
    dk_s[...] = jnp.zeros_like(dk_s)
    dv_s[...] = jnp.zeros_like(dv_s)
    dq_parts = [[] for _ in range(blocks + 1)]
    for head in range(2):
        mine, other = head_lanes(head)
        key_s[...] = k_ref[...] * mine + augk_ref[...] * other
        value_s[...] = v_ref[...] * mine
        head_rows = slice(head * HD, (head + 1) * HD)
        index = 2 * pair + head

        def grads(key_cat, value_cat, turned_cat, query_rows, aug, lse):
            queries = q_ref[query_rows, :] * mine
            douts = do_ref[query_rows, :] * mine
            delta = delta_ref[pl.ds(index, 1), query_rows]
            probs = jnp.exp(nt(key_cat, queries + aug * other) - lse)
            d_scores = (probs * (nt(value_cat, douts) - delta)).astype(BF16)
            d_key = nn(d_scores, queries)
            d_value = nn(probs.astype(BF16), douts)
            return nn(turned_cat, d_scores), d_key, d_value

        for block in range(blocks):
            rows = slice(block * BLOCK, (block + 1) * BLOCK)
            start = pl.multiple_of(local_rows + docs_ref[block] * GLOB, GLOB)
            doc_rows = pl.ds(start, GLOB)
            key_cat = jnp.concatenate([key_s[rows, :], key_s[doc_rows, :]], 0)
            value_cat = jnp.concatenate([value_s[rows, :], value_s[doc_rows, :]], 0)
            turned_cat = jnp.concatenate(
                [turned_s[head_rows, rows], turned_s[head_rows, doc_rows]], 1
            )
            d_query, d_key, d_value = grads(
                key_cat, value_cat, turned_cat, rows, lane_one(0), lse_ref[block, 0, head : head + 1, :]
            )
            dq_parts[block].append(d_query)
            dk_s[rows, :] += d_key[:BLOCK]
            dk_s[doc_rows, :] += d_key[BLOCK:]
            dv_s[rows, :] += d_value[:BLOCK]
            dv_s[doc_rows, :] += d_value[BLOCK:]
        rows = slice(local_rows, rows_all)
        d_query, d_key, d_value = grads(
            key_s[...], value_s[...], turned_s[head_rows, :], rows, augq_ref[...],
            lseg_ref[pl.ds(index, 1), :],
        )
        dq_parts[blocks].append(d_query)
        dk_s[...] += d_key
        dv_s[...] += d_value
    for block in range(blocks + 1):
        begin = block * BLOCK
        made = jnp.concatenate(dq_parts[block], 0).T
        dq_ref[begin : begin + made.shape[0], :] = (
            made.astype(BF16).astype(F32) * SCALE
        ).astype(BF16)
    dk_ref[...] = dk_s[...].astype(BF16)
    dv_ref[...] = dv_s[...].astype(BF16)


def attention_back(
    docs, qkv, d_attn, lse, lse_glob, delta, augk, augq, pairs, first, number, held=(), after=()
):
    rows_all = qkv.shape[0]
    count = augq.shape[0]
    blocks = (rows_all - count) // BLOCK

    def block(kind):
        column = pair_column(kind, pairs)
        return (qkv, pl.BlockSpec((rows_all, LANES), lambda p, docs: (0, column(p + first))))

    straight = pl.BlockSpec((rows_all, LANES), lambda p, docs: (0, p + first))
    work = 2 * number * (blocks * BLOCK * (BLOCK + GLOB) + rows_all * count)
    return launch(
        functools.partial(attention_back_body, first=first),
        "attention_back",
        (number,),
        [
            block(0),
            block(1),
            block(2),
            (d_attn, straight),
            (lse, pl.BlockSpec((blocks, 1, 2, BLOCK), lambda p, docs: (0, p + first, 0, 0))),
            (lse_glob, full(lse_glob.shape)),
            (delta, full(delta.shape)),
            (augk, full(augk.shape)),
            (augq, full(augq.shape)),
        ],
        [((rows_all, pairs * LANES), BF16, straight)] * 3,
        cost(work * 5 * 512, number * rows_all * LANES * 14, work),
        prefetch=(docs,),
        held=held,
        after=after,
        scratch=[
            pltpu.VMEM((rows_all, LANES), BF16),
            pltpu.VMEM((rows_all, LANES), BF16),
            pltpu.VMEM((LANES, rows_all), BF16),
            pltpu.VMEM((rows_all, LANES), F32),
            pltpu.VMEM((rows_all, LANES), F32),
        ],
    )


def project_grad_body(turned_ref, dq_ref, dk_ref, dv_ref, out_grad_ref, mid_ref, in_ref, *rest):
    up_refs, grads_ref = rest[:-1], rest[-1]
    step = pl.program_id(0)
    dim = turned_ref.shape[0] * pl.num_programs(0)
    width = dq_ref.shape[1]
    cols = width // LANES
    per_half = 2 * cols
    start = pl.multiple_of(step * TILE, TILE)
    for kind, ref in enumerate((dq_ref, dk_ref, dv_ref)):
        made = nn(turned_ref[...], ref[...]).astype(BF16)
        for col in range(cols):
            unit = kind * cols + col
            grads_ref[unit // per_half, pl.ds(unit % per_half * dim + start, TILE), :] = made[
                :, col * LANES : (col + 1) * LANES
            ]

    @pl.when(step == 0)
    def _():
        grads_ref[1, cols * dim : per_half * dim, :] = out_grad_ref[0]
        small = [mid_ref[row : row + 1, :] for row in range(4)]
        small += [in_ref[row : row + 1, :] for row in range(2)]
        small += [jnp.sum(ref[...].astype(F32), axis=0, keepdims=True) for ref in (dq_ref, dv_ref)]
        small += [ref[...] for ref in up_refs]
        pieces = []
        for row in small:
            pieces += [row[:, col * LANES : (col + 1) * LANES] for col in range(row.shape[1] // LANES)]
        pieces.append(jnp.zeros((LANES - len(pieces), LANES), F32))
        grads_ref[0, per_half * dim :, :] = jnp.concatenate(pieces, 0).astype(BF16)
        grads_ref[1, per_half * dim :, :] = jnp.zeros((LANES, LANES), BF16)


def project_grad(turned, dq, dk, dv, out_grad, mid_sums, in_sums, up_sums, half, after=()):
    dim, rows_all = turned.shape
    width = dq.shape[1] // 2
    grads = pl.BlockSpec((rows_all, width), lambda i: (0, half), pipeline_mode=pl.Buffered(1))
    shape = (2, 2 * width // LANES * dim + LANES, LANES)
    packed = out_grad.shape[1:]
    return launch(
        project_grad_body,
        "project_grad",
        (dim // TILE,),
        [
            (turned, pl.BlockSpec((TILE, rows_all), lambda i: (i, 0))),
            (dq, grads),
            (dk, grads),
            (dv, grads),
            (out_grad, pl.BlockSpec((1, *packed), lambda i: (half, 0, 0))),
            (mid_sums, full(mid_sums.shape)),
            (in_sums, full(in_sums.shape)),
        ]
        + [(up, full(up.shape)) for up in up_sums],
        [(shape, BF16, full(shape))],
        cost(6 * rows_all * dim * width, rows_all * (dim + 3 * width) * 2),
        after=after,
    )[0]


def input_back_body(
    place_ref, dq_ref, dk_ref, dv_ref, own_ref, par_ref, x_ref, xg_ref, dmid_ref, vecs_ref,
    tokens_ref, leave_ref, stay_ref, sums_ref, *, number,
):
    step = pl.program_id(0)
    last = pl.num_programs(0) - 1
    half = own_ref.shape[1] // 3
    d_hidden = None
    for part, weight in enumerate((own_ref, par_ref)):
        cols = slice(part * half, (part + 1) * half)
        joined = jnp.concatenate([dq_ref[:, cols], dk_ref[:, cols], dv_ref[:, cols]], 1)
        made = nt(joined, weight[...])
        d_hidden = made if d_hidden is None else d_hidden + made

    @pl.when(step == 0)
    def _():
        sums_ref[...] = jnp.zeros_like(sums_ref)

    def add_sums(xhat):
        sums_ref[0:1, :] += jnp.sum(d_hidden * xhat, axis=0, keepdims=True)
        sums_ref[1:2, :] += jnp.sum(d_hidden, axis=0, keepdims=True)

    @pl.when(step < last)
    def _():
        xhat, inv = normed(x_ref[...].astype(F32))
        tokens_ref[...] = dmid_ref[...] + norm_back(xhat, inv, vecs_ref[0:1, :], d_hidden)
        add_sums(xhat)

    @pl.when(step == last)
    def _():
        xhat, _ = normed(xg_ref[...].astype(F32))
        low = d_hidden.astype(BF16)
        cut = low.shape[0] // 2
        for side in range(2):

            @pl.when(place_ref[number] == side)
            def _(side=side):
                stay_ref[...] = low[side * cut : (side + 1) * cut]
                leave_ref[...] = low[(1 - side) * cut : (2 - side) * cut]

        add_sums(xhat)


def input_back(place, number, dq, dk, dv, w_own, w_par, x, x_glob, d_mid, vecs, after=()):
    rows_all, dim = dq.shape
    tiles = rows_all // TILE
    row = pl.BlockSpec((TILE, dim), lambda i, place: (i, 0))
    local = pl.BlockSpec((TILE, dim), lambda i, place: (jnp.minimum(i, tiles - 2), 0))
    cut = (x_glob.shape[0] // 2, dim)
    return launch(
        functools.partial(input_back_body, number=number),
        "input_back",
        (tiles,),
        [
            (dq, row),
            (dk, row),
            (dv, row),
            (w_own, full(w_own.shape)),
            (w_par, full(w_par.shape)),
            (x, local),
            (x_glob, full(x_glob.shape)),
            (d_mid, row),
            (vecs, full(vecs.shape)),
        ],
        [
            (x.shape, F32, local),
            (cut, BF16, full(cut)),
            (cut, BF16, full(cut)),
            ((8, dim), F32, full((8, dim))),
        ],
        cost(6 * rows_all * dim * dim, rows_all * dim * 16 + 6 * dim * dim),
        prefetch=(place,),
        after=after,
    )


def glob_input_body(kept_ref, got_ref, x_ref, dmid_ref, vecs_ref, out_ref):
    d_hidden = kept_ref[...].astype(F32) + got_ref[...].astype(F32)
    xhat, inv = normed(x_ref[...].astype(F32))
    out_ref[...] = dmid_ref[...] + norm_back(xhat, inv, vecs_ref[0:1, :], d_hidden)


def glob_input(place, kept, got, x, d_mid, vecs):
    own, dim = x.shape
    first = (d_mid.shape[0] - 2 * GLOB) // own
    spec = pl.BlockSpec((own, dim), lambda i, place: (0, 0))
    here = pl.BlockSpec((own, dim), lambda i, place: (first + place[2] // own, 0))

    def body(place_ref, *refs):
        glob_input_body(*refs)

    return launch(
        body,
        "glob_input",
        (1,),
        [(kept, spec), (got, spec), (x, spec), (d_mid, here), (vecs, full(vecs.shape))],
        [((own, dim), F32, spec)],
        cost(0, own * dim * 14),
        prefetch=(place,),
    )[0]


def pair_add(left, right):
    return (left.astype(F32) + right.astype(F32)).astype(BF16)


def add_split_body(place_ref, kept_go, got_go, kept_stay, got_stay, go_ref, stay_ref):
    go_ref[...] = pair_add(kept_go[0], got_go[0])
    stay_ref[...] = pair_add(kept_stay[0], got_stay[0])


def add_split(place, number, kept, got, after=()):
    lanes = kept.shape[-1]
    kept = kept.reshape(2, -1, lanes)
    got = got.reshape(kept.shape)
    rows = kept.shape[1]
    tiles = next((t for t in (4, 2) if rows % (16 * t) == 0 and rows >= 512 * t), 1)
    tile = rows // tiles

    def spec(flipped):
        def at(i, place):
            side = place[number]
            return (1 - side if flipped else side, i, 0)

        return pl.BlockSpec((1, tile, lanes), at)

    out = pl.BlockSpec((tile, lanes), lambda i, place: (i, 0))
    return launch(
        add_split_body,
        "add_split",
        (tiles,),
        [(kept, spec(True)), (got, spec(True)), (kept, spec(False)), (got, spec(False))],
        [((rows, lanes), BF16, out), ((rows, lanes), BF16, out)],
        cost(kept.size, kept.size * 6),
        prefetch=(place,),
        after=after,
    )


def add_body(kept_ref, got_ref, out_ref):
    out_ref[...] = pair_add(kept_ref[...], got_ref[...])


def add_rows(kept, got, after=()):
    spec = full(kept.shape)
    return launch(
        add_body, "add_rows", (1,), [(kept, spec), (got, spec)], [(kept.shape, BF16, spec)],
        cost(kept.size, kept.size * 6), after=after,
    )[0]


def join_body(place_ref, mine_ref, other_ref, out_ref):
    step = pl.program_id(0)
    half = pl.num_programs(0) // 2

    @pl.when(step < half)
    def _():
        out_ref[0] = mine_ref[...]

    @pl.when(step >= half)
    def _():
        out_ref[0] = other_ref[...]


def join(place, number, mine, other, after=()):
    rows, lanes = mine.shape
    tiles = 2 if rows % 32 == 0 and rows >= 2048 else 1
    tile = rows // tiles

    def at(i, place):
        side = place[number]
        return (jnp.where(i < tiles, side, 1 - side), i % tiles, 0)

    made = launch(
        join_body,
        "join",
        (2 * tiles,),
        [
            (mine, pl.BlockSpec((tile, lanes), lambda i, place: (jnp.minimum(i, tiles - 1), 0))),
            (other, pl.BlockSpec((tile, lanes), lambda i, place: (jnp.maximum(i - tiles, 0), 0))),
        ],
        [((2, rows, lanes), BF16, pl.BlockSpec((1, tile, lanes), at))],
        cost(0, mine.size * 8),
        prefetch=(place,),
        after=after,
    )[0]
    return made.reshape(2 * rows, lanes)


def by_side(place_ref, number, mine_ref, other_ref, write):
    for half in range(2):
        for ref, here in ((mine_ref, place_ref[number] == half), (other_ref, place_ref[number] != half)):

            @pl.when(here)
            def _(ref=ref, half=half):
                write(ref, half)


def ffn_unpack_body(place_ref, mine_ref, other_ref, up_ref, down_ref, *, number, chunk):
    dim = up_ref.shape[0]
    units = up_ref.shape[1]
    packed = 2 * chunk * dim // LANES

    def write(ref, half):
        first = half * ref.shape[0]
        spot = 0
        for step in range(units // chunk):
            for col in range(chunk // LANES):
                if first <= spot < first + ref.shape[0]:
                    begin = step * chunk + col * LANES
                    up_ref[:, begin : begin + LANES] = ref[spot - first : spot - first + dim, :].astype(F32)
                spot += dim
            for col in range(dim // LANES):
                if first <= spot < first + ref.shape[0]:
                    down_ref[step * chunk : (step + 1) * chunk, col * LANES : (col + 1) * LANES] = ref[
                        spot - first : spot - first + chunk, :
                    ].astype(F32)
                spot += chunk

    by_side(place_ref, number, mine_ref, other_ref, write)


def ffn_unpack(place, number, mine, other, dim, half, units, part, held=(), after=()):
    spec = full(mine.shape)
    chunk = min(FFN_CHUNK, units)
    one = pl.Buffered(1)
    return launch(
        functools.partial(ffn_unpack_body, number=number, chunk=chunk),
        "ffn_unpack",
        (1,),
        [(mine, spec), (other, spec)],
        [
            ((dim, half), F32, pl.BlockSpec((dim, units), lambda i, place: (0, part), pipeline_mode=one)),
            ((half, dim), F32, pl.BlockSpec((units, dim), lambda i, place: (part, 0), pipeline_mode=one)),
        ],
        cost(0, mine.size * 12),
        prefetch=(place,),
        held=held,
        after=after,
    )


def tail_unpack_body(place_ref, mine_ref, other_ref, q_ref, k_ref, v_ref, out_ref, small_ref, *, number):
    dim, width = q_ref.shape
    cols = width // LANES
    per_half = 2 * cols

    def write(ref, half):
        for place in range(per_half):
            unit = half * per_half + place
            kind, col = unit // cols, unit % cols
            rows = ref[place * dim : (place + 1) * dim, :].astype(F32)
            if kind < 3:
                (q_ref, k_ref, v_ref)[kind][:, col * LANES : (col + 1) * LANES] = rows
            else:
                for step in range(dim // width):
                    begin = (col * (dim // width) + step) * LANES
                    out_ref[:, begin : begin + LANES] = rows[step * width : (step + 1) * width]
        if half == 0:
            small_ref[...] = ref[per_half * dim :, :].astype(F32)

    by_side(place_ref, number, mine_ref, other_ref, write)


def tail_unpack(place, number, mine, other, dim, width):
    spec = full(mine.shape)
    shapes = [(dim, width)] * 3 + [(width, dim), (LANES, LANES)]
    return launch(
        functools.partial(tail_unpack_body, number=number),
        "tail_unpack",
        (1,),
        [(mine, spec), (other, spec)],
        [(shape, F32, full(shape)) for shape in shapes],
        cost(0, mine.size * 12),
        prefetch=(place,),
    )


def per_device(
    tokens, glob_tokens, w_query, b_query, w_key, w_value, b_value, w_out, b_out, w_up, b_up,
    w_down, b_down, gain_attn, shift_attn, gain_ffn, shift_ffn, doc_blocks, doc_tail,
    grad_tokens, grad_glob,
):
    seq_size = lax.axis_size("seq")
    seq_pos = lax.axis_index("seq")
    tp_pos = lax.axis_index("tp")
    rows, dim = tokens.shape
    own_glob = glob_tokens.shape[0]
    half = w_query.shape[1]
    units = w_up.shape[1]
    pairs = 2 * half // PAIR
    blocks = rows // BLOCK
    glob_rows = 2 * GLOB
    rows_all = rows + glob_rows
    group_size = GROUP_BLOCKS // (2 * blocks)
    group_bits = group_size.bit_length() - 1
    seq_bits = seq_size.bit_length() - 1
    group_pos = seq_pos % group_size
    own_first = (group_pos * 2 + tp_pos) * own_glob

    def flip(value, bit):
        return lax.ppermute(value, "seq", [(s, s ^ (1 << bit)) for s in range(seq_size)])

    def swap(value):
        return lax.ppermute(value, "tp", [(0, 1), (1, 0)])

    rest = tuple(range(3, seq_bits))
    orders = {
        "one": ((0, 1, 2, *rest), (2, 0, 1, *rest)),
        "two": ((1, 0, 2, *rest), (2, 1, 0, *rest)),
        "tail": ((0, 1, 2, *rest), (2, 0, 1, *rest)),
    }
    place = [
        (seq_pos * 2 + tp_pos) * blocks,
        (seq_pos // group_size) * 2,
        own_first,
        jnp.int32(own_glob),
        group_pos,
        tp_pos,
    ]
    group_sides = len(place)
    place += [(seq_pos >> bit) & 1 for bit in range(group_bits)] + [tp_pos]
    job_sides = {}
    for name, (zero, one) in orders.items():
        job_sides[name] = len(place)
        place += [(seq_pos >> jnp.where(tp_pos == 0, a, b)) & 1 for a, b in zip(zero, one)]
    place = jnp.stack(place).astype(jnp.int32)

    def trade(value, name, step):
        zero, one = orders[name][0][step], orders[name][1][step]
        links = [(2 * s, 2 * (s ^ (1 << zero))) for s in range(seq_size)]
        links += [(2 * s + 1, 2 * (s ^ (1 << one)) + 1) for s in range(seq_size)]
        return lax.ppermute(value, ("seq", "tp"), links)

    gathered = jnp.stack([glob_tokens, grad_glob])[None]
    qkv_own = jnp.concatenate([w_query, w_key, w_value], 1)
    qkv_par = swap(qkv_own)
    half_own = jnp.concatenate([b_query, b_value, b_up])
    halves = jnp.stack([half_own, swap(half_own)])
    vecs = jnp.stack([gain_attn, shift_attn, gain_ffn, shift_ffn, b_out, b_down])
    docs, augk, augq, mask = layout(place, doc_blocks, doc_tail, rows_all, glob_rows, blocks)
    tiles = rows // TILE
    held = ()
    cuts = [tiles * (bit + 1) // group_bits for bit in range(group_bits)]
    done = 0
    for bit in range(group_bits):
        other = flip(gathered, bit)
        if cuts[bit] > done:
            held = project(
                tokens, vecs, halves, qkv_own, qkv_par, rows_all, done, cuts[bit] - done, held,
                (gathered,),
            )
            done = cuts[bit]
        gathered = jnp.concatenate([gathered, other], 0)
    x_glob, dz_all = order_rows(place, gathered, swap(gathered), grad_tokens)
    qkv, hidden_turned = project(
        x_glob, vecs, halves, qkv_own, qkv_par, rows_all, tiles, glob_rows // TILE, held
    )
    out_par = swap(w_out)
    up_par = swap(w_up)
    down_par = swap(w_down)

    mine, theirs = glob_forward(qkv, augk, augq, pairs)
    state = merge(mine, swap(theirs))
    outs = ()
    for bit in range(group_bits):
        other = flip(state, bit)
        first, end = pairs * bit // group_bits, pairs * (bit + 1) // group_bits
        outs = local_forward(docs, qkv, augk, pairs, blocks, first, end - first, outs, (state,))
        state = merge(state, other, (outs[3],))
    state_par = swap(state)
    high, low, out_turned, lse = outs
    held = middle_local(high, tokens, w_out, out_par, vecs, (state,))
    middle, hidden, ffn_turned, high, low, out_turned, lse_glob = middle_glob(
        state, state_par, x_glob, w_out, out_par, vecs, [*held, high, low, out_turned]
    )

    part = units // 2
    acts, ups, jobs = [], [[], []], []
    dn = None
    for number in range(2):
        first = number * part
        grads = []
        for which, (up, down) in ((1, (up_par, down_par)), (0, (w_up, w_down))):
            dn, act, grad, up_sum = ffn_part(
                hidden, ffn_turned, dz_all, up, halves, down, mask, which, first, part, dn,
            )
            acts.append((act, down, number))
            ups[which].append(up_sum)
            grads.append(grad if which == 0 else swap(grad))
        jobs.append(grads)

    class Job:
        def __init__(self, name, own, got, after=()):
            self.name, self.step = name, 0
            self.go, self.stay = add_split(place, job_sides[name], own, got, after)
            self.other = trade(self.go, name, 0)

        def advance(self, after=()):
            first, step = job_sides[self.name], self.step
            if step < seq_bits - 1:
                self.go, self.stay = add_split(place, first + step + 1, self.stay, self.other, after)
                self.other = trade(self.go, self.name, step + 1)
                marker = self.stay
            elif step == seq_bits - 1:
                self.shard = add_rows(self.stay, self.other, after)
                self.other = trade(self.shard, self.name, seq_bits - 1)
                marker = self.shard
            else:
                back = 2 * seq_bits - 1 - step
                self.shard = join(place, first + back, self.shard, self.other, after)
                self.other = trade(self.shard, self.name, back - 1)
                marker = self.shard
            self.step += 1
            return marker

        @property
        def left(self):
            return 2 * seq_bits - 1 - self.step

    job_one = Job("one", jobs[0][1], jobs[0][0])
    job_two = Job("two", jobs[1][1], jobs[1][0])

    d_mid, d_attn, delta, out_grad, mid_sums = middle_back(
        dn, middle, dz_all, high, low, out_turned, w_out, out_par, vecs, mask, (job_one.go, job_two.go)
    )
    marks = [job_one.advance((d_attn,)), job_two.advance((d_attn,))]
    grads = ()
    steps = 3
    for step in range(steps):
        first, end = pairs * step // steps, pairs * (step + 1) // steps
        grads = attention_back(
            docs, qkv, d_attn, lse, lse_glob, delta, augk, augq, pairs, first, end - first, grads, marks
        )
        marks = [job_one.advance((grads[0],)), job_two.advance((grads[0],))]
    dq, dk, dv = grads
    top_side = group_sides + group_bits - 1
    tokens_grad, go, stay, in_sums = input_back(
        place, top_side, dq, dk, dv, qkv_own, qkv_par, tokens, x_glob, d_mid, vecs, marks
    )
    marks = [job_one.advance((tokens_grad,)), job_two.advance((tokens_grad,))]
    tail_par = project_grad(
        hidden_turned, dq, dk, dv, out_grad, mid_sums, in_sums, ups[1], 1, marks
    )
    tail_got = swap(tail_par)
    tail_own = project_grad(
        hidden_turned, dq, dk, dv, out_grad, mid_sums, in_sums, ups[0], 0, (tail_par,)
    )
    job_tail = Job("tail", tail_own, tail_got)

    marks = [job_tail.go]
    got = flip(go, group_bits - 1)
    for bit in reversed(range(group_bits)):
        number = group_sides + bit - 1 if bit else group_sides + group_bits
        go, stay = add_split(place, number, stay, got, marks)
        got = flip(go, bit - 1) if bit else swap(go)
        if job_one.left:
            marks = [job_one.advance((stay,))]
        if job_two.left:
            marks.append(job_two.advance((stay,)))
        marks.append(job_tail.advance((stay,)))
    glob_grad = glob_input(place, stay, got, glob_tokens, d_mid, vecs)
    out_tokens, out_all = output_rows(
        place, middle, vecs, [a for a, _, _ in acts], [(w, n) for _, w, n in acts], own_glob, marks
    )
    out_glob = lax.dynamic_slice_in_dim(out_all, own_first, own_glob, 0)
    while job_one.left:
        job_one.advance()
    while job_two.left:
        job_two.advance()
    while job_tail.left:
        job_tail.advance()
    kinds = ffn_unpack(place, job_sides["one"], job_one.shard, job_one.other, dim, units, part, 0)
    up_grad, down_grad = ffn_unpack(
        place, job_sides["two"], job_two.shard, job_two.other, dim, units, part, 1, kinds
    )
    q_grad, k_grad, v_grad, w_out_grad, small = tail_unpack(
        place, job_sides["tail"], job_tail.shard, job_tail.other, dim, half
    )
    small = small.reshape(-1)
    shared = small[: 6 * dim]
    shared = jnp.where(tp_pos == 0, shared, swap(shared))
    gain_f_grad, shift_f_grad, out_bias, down_bias, gain_a_grad, shift_a_grad = (
        shared.reshape(6, dim)
    )
    b_query_grad = small[6 * dim : 6 * dim + half]
    b_value_grad = small[6 * dim + half : 6 * dim + 2 * half]
    b_up_grad = small[6 * dim + 2 * half : 6 * dim + 2 * half + units]
    return (
        out_tokens, out_glob, tokens_grad, glob_grad, q_grad, b_query_grad, k_grad,
        v_grad, b_value_grad, w_out_grad, out_bias, up_grad, b_up_grad, down_grad, down_bias,
        gain_a_grad, shift_a_grad, gain_f_grad, shift_f_grad,
    )


def solution(mesh):
    rows = P(("seq", "tp"), None)
    cols, part, whole = P(None, "tp"), P("tp"), P()
    lines = P("tp", None)
    return jax.shard_map(
        per_device,
        mesh=mesh,
        in_specs=(
            rows, rows, cols, part, cols, cols, part, lines, whole, cols, part, lines, whole,
            whole, whole, whole, whole, whole, whole, rows, rows,
        ),
        out_specs=(
            rows, rows, rows, rows, cols, part, cols, cols, part, lines, whole, cols, part, lines,
            whole, whole, whole, whole, whole,
        ),
        check_vma=False,
    )
```

```python
import functools

import jax
import jax.numpy as jnp
from jax import lax
from jax.experimental import pallas as pl
from jax.experimental.pallas import tpu as pltpu
from jax.sharding import PartitionSpec as P

HD = 64
BLOCK = 512
GLOB = 128
GROUP_BLOCKS = 32
EPS = 1e-05
SCALE = 0.125
NEG = -1e30
TILE = 256
PAIR = 2 * HD
LANES = 128
STATS = 16
HEAD_ROWS = 16
FFN_CHUNK = 256
WEIGHT = 10
F32 = jnp.float32
BF16 = jnp.bfloat16
VMEM_BYTES = 16 * 2**20


def nn(left, right):
    return jnp.dot(left, right, preferred_element_type=F32)


def nt(left, right):
    return lax.dot_general(left, right, (((1,), (1,)), ((), ())), preferred_element_type=F32)


def tn(left, right):
    return lax.dot_general(left, right, (((0,), (0,)), ((), ())), preferred_element_type=F32)


def normed(values):
    row_mean = jnp.mean(values, axis=-1, keepdims=True)
    centred = values - row_mean
    row_var = jnp.mean(centred * centred, axis=-1, keepdims=True)
    inv = lax.rsqrt(row_var + EPS)
    return centred * inv, inv


def norm_back(xhat, inv, gain_vec, cotangent):
    scaled = cotangent * gain_vec
    mean_one = jnp.mean(scaled, axis=-1, keepdims=True)
    mean_two = jnp.mean(scaled * xhat, axis=-1, keepdims=True)
    return inv * (scaled - mean_one - xhat * mean_two)


def full(shape):
    zeros = (0,) * len(shape)
    return pl.BlockSpec(shape, lambda *_: zeros, pipeline_mode=pl.Buffered(1))


ANY = pl.BlockSpec(memory_space=pl.ANY)


def launch(
    body, name, grid, operands, outs, work, prefetch=(), held=(), after=(), scratch=(), aliased=0
):
    arrays = [*prefetch, *(a for a, _ in operands), *held, *after]
    specs = [*(spec for _, spec in operands), *([ANY] * (len(held) + len(after)))]
    first = len(prefetch) + len(operands)
    spare = len(held) + len(after)

    def whole(*refs):
        return body(*refs[:first], *refs[first + spare :])

    return pl.pallas_call(
        whole,
        grid_spec=pltpu.PrefetchScalarGridSpec(
            num_scalar_prefetch=len(prefetch),
            grid=grid,
            in_specs=specs,
            out_specs=[out[2] for out in outs],
            scratch_shapes=list(scratch),
        ),
        out_shape=[(pltpu.HBM if out[3:] else jax.ShapeDtypeStruct)(out[0], out[1]) for out in outs],
        input_output_aliases={first + i: aliased + i for i in range(len(held))},
        compiler_params=pltpu.CompilerParams(
            vmem_limit_bytes=VMEM_BYTES, dimension_semantics=("arbitrary",) * len(grid)
        ),
        cost_estimate=work,
        name=name,
    )(*arrays)


def cost(flops, nbytes, trans=0):
    scale = WEIGHT if flops > 2**28 else 1
    return pl.CostEstimate(
        flops=int(scale * flops), bytes_accessed=int(scale * nbytes), transcendentals=int(trans)
    )


def head_lanes(head):
    lane = lax.broadcasted_iota(jnp.int32, (1, LANES), 1)
    here = jnp.where(lane < HD, 1.0, 0.0)
    mine = here if head == 0 else 1.0 - here
    return mine.astype(BF16), (1.0 - mine).astype(BF16)


def lane_one(slot):
    lane = lax.broadcasted_iota(jnp.int32, (1, LANES), 1)
    return jnp.where((lane == slot) | (lane == slot + HD), 1.0, 0.0).astype(BF16)


def layout_body(place_ref, blocks_ref, tails_ref, docs_ref, augk_ref, augq_ref, mask_ref):
    first_block, group_first, own_first = place_ref[0], place_ref[1], place_ref[2]
    own_count = place_ref[3]
    count = augq_ref.shape[0]
    rows = augk_ref.shape[0] - count
    lane = lax.broadcasted_iota(jnp.int32, (1, LANES), 1)
    slot = jnp.where(lane < HD, lane, lane - HD)
    for block in range(rows // BLOCK):
        index = first_block + block
        start, doc, real = jnp.int32(0), jnp.int32(0), jnp.int32(BLOCK)
        for number in range(blocks_ref.shape[0]):
            end = start + blocks_ref[number]
            inside = jnp.logical_and(index >= start, index < end)
            doc = jnp.where(inside, number, doc)
            real = jnp.where(
                jnp.logical_and(inside, index == end - 1), tails_ref[number], real
            )
            start = end
        doc = doc - group_first
        docs_ref[block] = doc
        row = lax.broadcasted_iota(jnp.int32, (BLOCK, 1), 0)
        padded = row >= real
        shut = ((slot == 1) & (doc != 0)) | ((slot == 2) & (doc != 1))
        shut = jnp.where(shut, 1, 0) + jnp.where(padded & (slot < 3), 1, 0)
        augk_ref[block * BLOCK : (block + 1) * BLOCK, :] = jnp.where(shut > 0, NEG, 0.0).astype(BF16)
    row = lax.broadcasted_iota(jnp.int32, (count, 1), 0)
    late = row >= GLOB
    shut = ((slot == 1) & late) | ((slot == 2) & ~late) | (slot == 3)
    augk_ref[rows:, :] = jnp.where(shut, NEG, 0.0).astype(BF16)
    owned = (row >= own_first) & (row < own_first + own_count)
    on = ((slot == 1) & ~late) | ((slot == 2) & late) | ((slot == 3) & ~owned)
    augq_ref[...] = jnp.where(on, 1.0, 0.0).astype(BF16)
    mask_ref[:rows, :] = jnp.ones((rows, 1), F32)
    mask_ref[rows:, :] = jnp.where(owned, 1.0, 0.0)


def layout(place, doc_blocks, doc_tail, rows_all, count, blocks):
    smem = pl.BlockSpec(memory_space=pltpu.SMEM)
    return launch(
        layout_body,
        "layout",
        (1,),
        [],
        [
            ((blocks,), jnp.int32, smem),
            ((rows_all, LANES), BF16, full((rows_all, LANES))),
            ((count, LANES), BF16, full((count, LANES))),
            ((rows_all, 1), F32, full((rows_all, 1))),
        ],
        cost(0, rows_all * LANES * 4),
        prefetch=(place, doc_blocks, doc_tail),
    )


def pack_body(*refs):
    vecs_ref, half_ref = refs[-2:]
    for row, ref in enumerate(refs[:6]):
        vecs_ref[row : row + 1, :] = ref[...].reshape(1, -1)
    vecs_ref[6:, :] = jnp.zeros((2, vecs_ref.shape[1]), F32)
    half_ref[...] = jnp.zeros(half_ref.shape, F32)
    first = 0
    for ref in refs[6:9]:
        count = ref.shape[0]
        half_ref[0:1, first : first + count] = ref[...].reshape(1, -1)
        first += count


def pack_vectors(vectors, parts):
    arrays = [*vectors, *parts]
    dim = vectors[0].shape[0]
    width = sum(part.shape[0] for part in parts)
    return launch(
        pack_body,
        "pack_vectors",
        (1,),
        [(a, full(a.shape)) for a in arrays],
        [((8, dim), F32, full((8, dim))), ((8, width), F32, full((8, width)))],
        cost(0, 32 * (dim + width)),
    )


def order_body(place_ref, mine_ref, theirs_ref, grads_ref, x_ref, dz_ref):
    step = pl.program_id(0)
    last = pl.num_programs(0) - 1
    chips, _, own, _ = mine_ref.shape

    @pl.when(step < last)
    def _():
        dz_ref[...] = grads_ref[...]

    @pl.when(step == last)
    def _():
        for chip in range(chips):
            for side, ref in enumerate((mine_ref, theirs_ref)):
                spot = (place_ref[4] ^ chip) * 2 + (place_ref[5] ^ side)
                here = pl.ds(pl.multiple_of(spot * own, own), own)
                x_ref[here, :] = ref[chip, 0]
                dz_ref[here, :] = ref[chip, 1]


def order_rows(place, mine, theirs, grads, after=()):
    chips, _, own, dim = mine.shape
    count = chips * 2 * own
    tiles = grads.shape[0] // count
    return launch(
        order_body,
        "order_rows",
        (tiles + 1,),
        [
            (mine, full(mine.shape)),
            (theirs, full(mine.shape)),
            (grads, pl.BlockSpec((count, dim), lambda i, place: (jnp.minimum(i, tiles - 1), 0))),
        ],
        [
            ((count, dim), BF16, full((count, dim))),
            (
                (grads.shape[0] + count, dim),
                BF16,
                pl.BlockSpec((count, dim), lambda i, place: (i, 0)),
            ),
        ],
        cost(0, 4 * grads.size),
        prefetch=(place,),
        after=after,
    )


def project_body(x_ref, vecs_ref, own_vec_ref, par_vec_ref, own_ref, par_ref, qkv_ref, turned_ref):
    xhat, _ = normed(x_ref[...].astype(F32))
    hidden = (xhat * vecs_ref[0:1, :] + vecs_ref[1:2, :]).astype(BF16)
    turned_ref[...] = hidden.T
    width = own_ref.shape[1]
    third = width // 3
    for half, (weight, vec_ref) in enumerate(((own_ref, own_vec_ref), (par_ref, par_vec_ref))):
        first = half * width
        made = nn(hidden, weight[...])
        bias = vec_ref[0:1, : 2 * third]
        qkv_ref[:, first : first + third] = (
            (made[:, :third] + bias[:, :third]) * SCALE
        ).astype(BF16)
        qkv_ref[:, first + third : first + 2 * third] = made[:, third : 2 * third].astype(BF16)
        qkv_ref[:, first + 2 * third : first + width] = (
            made[:, 2 * third :] + bias[:, third:]
        ).astype(BF16)


def project(x, vecs, halves, w_own, w_par, rows_all, first, count, held=(), after=()):
    dim = x.shape[1]
    width = 2 * w_own.shape[1]
    shift = first if first + count <= x.shape[0] // TILE else 0
    return launch(
        project_body,
        "project",
        (count,),
        [
            (x, pl.BlockSpec((TILE, dim), lambda i: (i + shift, 0))),
            (vecs, full(vecs.shape)),
            (halves[0], full(halves[0].shape)),
            (halves[1], full(halves[1].shape)),
            (w_own, full(w_own.shape)),
            (w_par, full(w_par.shape)),
        ],
        [
            ((rows_all, width), BF16, pl.BlockSpec((TILE, width), lambda i: (i + first, 0))),
            ((dim, rows_all), BF16, pl.BlockSpec((dim, TILE), lambda i: (0, i + first))),
        ],
        cost(2 * count * TILE * dim * width, 2 * (count * TILE * (2 * dim + width) + dim * width)),
        held=held,
        after=after,
    )


def pair_column(kind, pairs):
    half = pairs // 2
    return lambda p: (p // half) * 3 * half + kind * half + p % half


def write_stats(out_ref, head, lse):
    first = lse.astype(BF16).astype(F32)
    second = (lse - first).astype(BF16).astype(F32)
    third = lse - first - second
    row = lax.broadcasted_iota(jnp.int32, (STATS, lse.shape[1]), 0)
    held = jnp.where(row == 0, first, jnp.where(row == 1, second, jnp.where(row == 2, third, 0.0)))
    out_ref[head, HD : HD + STATS, :] = held.astype(BF16)


def read_stats(ref, head):
    held = ref[head, HD : HD + STATS, :].astype(F32)
    return held[0:1] + held[1:2] + held[2:3]


def glob_forward_body(q_ref, k_ref, v_ref, augk_ref, augq_ref, own_ref, par_ref):
    rows_all = k_ref.shape[0]
    count = augq_ref.shape[0]
    queries = q_ref[rows_all - count :, :]
    keys = k_ref[...]
    values_turned = v_ref[...].T
    half = pl.num_programs(0) // 2
    for head in range(2):
        mine, other = head_lanes(head)
        key_head = keys * mine + augk_ref[...] * other
        query_head = queries * mine + augq_ref[...] * other
        scores = nt(key_head, query_head)
        top = jnp.max(scores, axis=0, keepdims=True)
        weights = jnp.exp(scores - top)
        total = jnp.sum(weights, axis=0, keepdims=True)
        summed = nn(values_turned[head * HD : (head + 1) * HD, :], weights.astype(BF16))
        summed = (summed / total).astype(BF16)
        lse = top + jnp.log(total)
        for ref, here in ((par_ref, pl.program_id(0) < half), (own_ref, pl.program_id(0) >= half)):

            @pl.when(here)
            def _(ref=ref, summed=summed, lse=lse, head=head):
                ref[head, :HD, :] = summed
                write_stats(ref, head, lse)


def glob_forward(qkv, augk, augq, pairs):
    rows_all = qkv.shape[0]
    count = augq.shape[0]
    half = pairs // 2

    def block(kind):
        column = pair_column(kind, pairs)
        return (qkv, pl.BlockSpec((rows_all, LANES), lambda p: (0, column((p + half) % pairs))))

    work = 2 * pairs * rows_all * count
    shape = (pairs, HD + STATS, count)
    size = (2, HD + STATS, count)
    return launch(
        glob_forward_body,
        "glob_forward",
        (pairs,),
        [block(0), block(1), block(2), (augk, full(augk.shape)), (augq, full(augq.shape))],
        [
            (shape, BF16, pl.BlockSpec(size, lambda p: (jnp.maximum(p - half, 0), 0, 0))),
            (shape, BF16, pl.BlockSpec(size, lambda p: (jnp.minimum(p, half - 1), 0, 0))),
        ],
        cost(work * 2 * 512, qkv.size * 2, work),
    )


def merge_body(left_ref, right_ref, out_ref):
    for head in range(left_ref.shape[0]):
        lse_left, lse_right = read_stats(left_ref, head), read_stats(right_ref, head)
        top = jnp.maximum(lse_left, lse_right)
        weight_left, weight_right = jnp.exp(lse_left - top), jnp.exp(lse_right - top)
        total = weight_left + weight_right
        out_left = left_ref[head, :HD, :].astype(F32)
        out_right = right_ref[head, :HD, :].astype(F32)
        merged = (out_left * weight_left + out_right * weight_right) / total
        out_ref[head, :HD, :] = merged.astype(BF16)
        write_stats(out_ref, head, top + jnp.log(total))


def merge(left, right, after=()):
    spec = full(left.shape)
    return launch(
        merge_body, "merge", (1,), [(left, spec), (right, spec)], [(left.shape, BF16, spec)],
        cost(left.size * 8, left.size * 6), after=after,
    )[0]


def local_forward_body(
    docs_ref, q_ref, k_ref, v_ref, kg_ref, vg_ref, augk_ref, high_ref, lse_ref
):
    keys = jnp.concatenate([k_ref[...], kg_ref[...]], 0)
    values_turned = jnp.concatenate([v_ref[...], vg_ref[...]], 0).T
    bias = jnp.concatenate([augk_ref[...], jnp.zeros((GLOB, LANES), BF16)], 0)
    outs = []
    for head in range(2):
        mine, other = head_lanes(head)
        key_head = keys * mine + bias * other
        query_head = q_ref[...] * mine + lane_one(0) * other
        scores = nt(key_head, query_head)
        top = jnp.max(scores, axis=0, keepdims=True)
        weights = jnp.exp(scores - top)
        total = jnp.sum(weights, axis=0, keepdims=True)
        summed = nn(values_turned[head * HD : (head + 1) * HD, :], weights.astype(BF16))
        outs.append(summed / total)
        lse_ref[0, 0, head : head + 1, :] = top + jnp.log(total)
    high_ref[...] = jnp.concatenate(outs, 0).T.astype(BF16)


def local_forward(docs, qkv, augk, pairs, blocks, first, count, held=(), after=()):
    rows_all = qkv.shape[0]
    glob_first = blocks * BLOCK // GLOB

    def block(kind):
        column = pair_column(kind, pairs)
        return (
            qkv,
            pl.BlockSpec((BLOCK, LANES), lambda b, p, docs: (b, column(p + first))),
        )

    def glob_block(kind):
        column = pair_column(kind, pairs)
        return (
            qkv,
            pl.BlockSpec(
                (GLOB, LANES), lambda b, p, docs: (glob_first + docs[b], column(p + first))
            ),
        )

    work = 2 * count * blocks * BLOCK * (BLOCK + GLOB)
    width = pairs * LANES
    straight = pl.BlockSpec((BLOCK, LANES), lambda b, p, docs: (b, p + first))
    return launch(
        local_forward_body,
        "local_forward",
        (blocks, count),
        [
            block(0),
            block(1),
            block(2),
            glob_block(1),
            glob_block(2),
            (augk, pl.BlockSpec((BLOCK, LANES), lambda b, p, docs: (b, 0))),
        ],
        [
            ((rows_all, width), BF16, straight),
            (
                (blocks, pairs, 2, BLOCK),
                F32,
                pl.BlockSpec((1, 1, 2, BLOCK), lambda b, p, docs: (b, p + first, 0, 0)),
            ),
        ],
        cost(work * 2 * 512, count * rows_all * LANES * 12, work),
        prefetch=(docs,),
        held=held,
        after=after,
    )


def middle_of(out_high, x, own_ref, par_ref, vecs_ref):
    half = own_ref.shape[0]
    branch = nn(out_high[:, :half], own_ref[...]) + nn(out_high[:, half:], par_ref[...])
    middle = x.astype(F32) + branch + vecs_ref[4:5, :]
    xhat, _ = normed(middle)
    hidden = (xhat * vecs_ref[2:3, :] + vecs_ref[3:4, :]).astype(BF16)
    return middle, hidden


def middle_body(out_ref, x_ref, own_ref, par_ref, vecs_ref, mid_ref, hid_ref, turned_ref):
    middle, hidden = middle_of(out_ref[...], x_ref[...], own_ref, par_ref, vecs_ref)
    mid_ref[...] = middle
    hid_ref[...] = hidden
    turned_ref[...] = hidden.T


def middle_local(out_high, x, w_own, w_par, vecs, after=()):
    rows_all, dim = out_high.shape
    rows = x.shape[0]
    row = pl.BlockSpec((TILE, dim), lambda i: (i, 0))
    return launch(
        middle_body,
        "middle_local",
        (rows // TILE,),
        [
            (out_high, row),
            (x, row),
            (w_own, full(w_own.shape)),
            (w_par, full(w_par.shape)),
            (vecs, full(vecs.shape)),
        ],
        [
            ((rows_all, dim), F32, row, True),
            ((rows_all, dim), BF16, row),
            ((dim, rows_all), BF16, pl.BlockSpec((dim, TILE), lambda i: (0, i))),
        ],
        cost(2 * rows * dim * dim, 12 * rows * dim + 2 * dim * dim),
        after=after,
    )


def middle_glob_body(
    own_out_ref, par_out_ref, x_ref, own_ref, par_ref, vecs_ref,
    mid_ref, hid_ref, turned_ref, high_ref, lse_ref,
):
    heads = own_out_ref.shape[0]
    parts = [own_out_ref[head, :HD, :] for head in range(heads)]
    parts += [par_out_ref[head, :HD, :] for head in range(heads)]
    turned = jnp.concatenate(parts, 0)
    high = turned.T
    high_ref[...] = high
    stats = [read_stats(own_out_ref, head) for head in range(heads)]
    stats += [read_stats(par_out_ref, head) for head in range(heads)]
    spare = lse_ref.shape[0] - 2 * heads
    lse_ref[...] = jnp.concatenate(stats + [jnp.zeros((spare, x_ref.shape[0]), F32)], 0)
    middle, hidden = middle_of(high, x_ref[...], own_ref, par_ref, vecs_ref)
    mid_ref[...] = middle
    hid_ref[...] = hidden
    turned_ref[...] = hidden.T


def middle_glob(own_out, par_out, x, w_own, w_par, vecs, held):
    rows, dim = x.shape
    first = held[0].shape[0] // rows - 1
    row = pl.BlockSpec((rows, dim), lambda i: (first, 0))
    col = pl.BlockSpec((dim, rows), lambda i: (0, first))
    operands = [own_out, par_out, x, w_own, w_par, vecs]
    specs = [row, row, col, row]
    return launch(
        middle_glob_body,
        "middle_glob",
        (1,),
        [(a, full(a.shape)) for a in operands],
        [(h.shape, h.dtype, spec, *pin) for h, spec, pin in zip(held, specs, ((True,), (), (), ()))]
        + [((HEAD_ROWS, rows), F32, full((HEAD_ROWS, rows)))],
        cost(2 * rows * dim * dim, 12 * rows * dim + 2 * dim * dim),
        held=held,
    )


def ffn_body(
    hid_ref, turned_ref, dz_ref, up_ref, bias_ref, down_ref, mask_ref, *rest, chunks
):
    dn_in_ref = rest[0] if len(rest) == 8 else None
    dnorm_ref, act_ref, grads_ref, bias_grad_ref, act_s, dup_s, sum_s = rest[-7:]
    step = pl.program_id(0)
    rows_all, dim = hid_ref.shape
    chunk = bias_grad_ref.shape[1]
    tail = slice(rows_all - mask_ref.shape[0], rows_all)

    @pl.when(step < chunks)
    def _():
        cols = pl.ds(pl.multiple_of(step * chunk, chunk), chunk)
        up = nn(hid_ref[...], up_ref[:, cols]) + bias_ref[0:1, :]
        share = 0.5 * (1.0 + lax.erf(up * (2.0**-0.5)))
        density = jnp.exp(up * up * -0.5) * 0.3989422804014327
        active = (up * share).astype(BF16)
        slope = share + up * density
        d_up = (nt(dz_ref[...], down_ref[cols, :]) * slope).astype(BF16)
        act_ref[...] = active
        dup_s[:, cols] = d_up
        act_s[...] = active
        sum_s[...] = d_up
        mask = mask_ref[...]
        act_s[tail, :] = (active[tail].astype(F32) * mask).astype(BF16)
        sum_s[tail, :] = (d_up[tail].astype(F32) * mask).astype(BF16)
        bias_grad_ref[...] = jnp.sum(sum_s[...].astype(F32), axis=0, keepdims=True)
        up_grad = nn(turned_ref[...], sum_s[...]).astype(BF16)
        down_grad = tn(act_s[...], dz_ref[...]).astype(BF16)
        place = 0
        for grad in (up_grad, down_grad):
            rows = grad.shape[0]
            for col in range(grad.shape[1] // LANES):
                grads_ref[0, place : place + rows, :] = grad[:, col * LANES : (col + 1) * LANES]
                place += rows

    @pl.when(step >= chunks)
    def _():
        start = pl.multiple_of((step - chunks) * TILE, TILE)
        made = nt(dup_s[pl.ds(start, TILE), :], up_ref[...])
        dnorm_ref[...] = made if dn_in_ref is None else made + dn_in_ref[...]


def ffn_part(hidden, turned, dz, w_up, vec, w_down, mask, first, units, dn_in=None, after=()):
    rows_all, dim = hidden.shape
    half = w_up.shape[1]
    chunk = min(FFN_CHUNK, units)
    chunks = units // chunk
    skip = first // units
    packed = 2 * chunk * dim // LANES
    bias_first = (vec.shape[1] - half + first) // chunk

    def now(j):
        return jnp.minimum(j, chunks - 1)

    row = pl.BlockSpec((TILE, dim), lambda j: (jnp.maximum(j - chunks, 0), 0))
    tail = mask.shape[0] // TILE - 1
    one = pl.Buffered(1)
    operands = [
        (hidden, full(hidden.shape)),
        (turned, full(turned.shape)),
        (dz, full(dz.shape)),
        (w_up, pl.BlockSpec((dim, units), lambda j: (0, skip), pipeline_mode=one)),
        (vec, pl.BlockSpec((vec.shape[0], chunk), lambda j: (0, bias_first + now(j)))),
        (w_down, pl.BlockSpec((units, dim), lambda j: (skip, 0), pipeline_mode=one)),
        (mask, pl.BlockSpec((TILE, 1), lambda j: (tail, 0))),
    ]
    if dn_in is not None:
        operands.append((dn_in, row))
    return launch(
        functools.partial(ffn_body, chunks=chunks),
        "ffn_part",
        (chunks + rows_all // TILE,),
        operands,
        [
            ((rows_all, dim), F32, row),
            ((rows_all, units), BF16, pl.BlockSpec((rows_all, chunk), lambda j: (0, now(j))), True),
            ((chunks, packed, LANES), BF16, pl.BlockSpec((1, packed, LANES), lambda j: (now(j), 0, 0))),
            ((1, units), F32, pl.BlockSpec((1, chunk), lambda j: (0, now(j)))),
        ],
        cost(10 * rows_all * dim * units, rows_all * dim * 14 + units * dim * 8, 2 * rows_all * units),
        after=after,
        scratch=[
            pltpu.VMEM((rows_all, chunk), BF16),
            pltpu.VMEM((rows_all, units), BF16),
            pltpu.VMEM((rows_all, chunk), BF16),
        ],
    )


def output_body(place_ref, mid_ref, vecs_ref, *rest):
    out_ref, glob_ref = rest[-2:]
    parts = len(rest) // 2 - 1
    made = mid_ref[...] + vecs_ref[5:6, :]
    for part in range(parts):
        made = made + nn(rest[part][...], rest[parts + part][...])
    step = pl.program_id(0)
    last = pl.num_programs(0) - 1

    @pl.when(step < last)
    def _():
        out_ref[...] = made.astype(BF16)

    @pl.when(step == last)
    def _():
        glob_ref[...] = made.astype(BF16)


def output_rows(place, middle, vecs, acts, weights, own, after=()):
    rows_all, dim = middle.shape
    tiles = rows_all // TILE
    rows = rows_all - TILE
    row = pl.BlockSpec((TILE, dim), lambda i, place: (i, 0))
    operands = [(middle, row), (vecs, full(vecs.shape))]
    operands += [
        (act, pl.BlockSpec((TILE, act.shape[1]), lambda i, place: (i, 0))) for act in acts
    ]
    for act, (weight, number) in zip(acts, weights):
        operands.append(
            (
                weight,
                pl.BlockSpec(
                    (act.shape[1], dim),
                    lambda i, place, number=number: (number, 0),
                    pipeline_mode=pl.Buffered(1),
                ),
            )
        )
    units = sum(act.shape[1] for act in acts)
    out, glob = launch(
        output_body,
        "output_rows",
        (tiles,),
        operands,
        [
            ((rows, dim), BF16, pl.BlockSpec((TILE, dim), lambda i, place: (jnp.minimum(i, tiles - 2), 0))),
            ((TILE, dim), BF16, full((TILE, dim))),
        ],
        cost(2 * rows_all * dim * units, rows_all * (units * 2 + dim * 6) + units * dim * 2),
        prefetch=(place,),
        after=after,
    )
    return out, glob


def middle_back_body(
    dn_ref, mid_ref, dz_ref, high_ref, own_ref, par_ref, vecs_ref, mask_ref,
    dmid_ref, dattn_ref, delta_ref, grads_ref, sums_ref, acc_s,
):
    step = pl.program_id(0)
    dim = mid_ref.shape[1]
    half = own_ref.shape[0]
    xhat, inv = normed(mid_ref[...])
    dn = dn_ref[...]
    dz = dz_ref[...].astype(F32)
    d_mid = dz + norm_back(xhat, inv, vecs_ref[2:3, :], dn)
    dmid_ref[...] = d_mid
    d_branch = d_mid.astype(BF16)
    for part, weight in enumerate((own_ref, par_ref)):
        dattn_ref[:, part * half : (part + 1) * half] = nt(d_branch, weight[...]).astype(BF16)
    product = dattn_ref[...].astype(F32) * high_ref[...].astype(F32)
    first = product.astype(BF16)
    second = (product - first.astype(F32)).astype(BF16)
    head = lax.broadcasted_iota(jnp.int32, (delta_ref.shape[0], dim), 0)
    column = lax.broadcasted_iota(jnp.int32, (delta_ref.shape[0], dim), 1)
    picked = jnp.where((column >= head * HD) & (column < (head + 1) * HD), 1.0, 0.0).astype(BF16)
    delta_ref[...] = nt(picked, first) + nt(picked, second)
    mask = mask_ref[...]
    masked = (d_branch.astype(F32) * mask).astype(BF16)
    made = tn(high_ref[...], masked)
    sums = [
        jnp.sum(dn * xhat * mask, axis=0, keepdims=True),
        jnp.sum(dn * mask, axis=0, keepdims=True),
        jnp.sum(masked.astype(F32), axis=0, keepdims=True),
        jnp.sum(dz * mask, axis=0, keepdims=True),
    ]
    sums = jnp.concatenate(sums + [jnp.zeros((4, dim), F32)], 0)

    @pl.when(step == 0)
    def _():
        acc_s[...] = made
        sums_ref[...] = sums

    @pl.when(step > 0)
    def _():
        acc_s[...] += made
        sums_ref[...] += sums

    @pl.when(step == pl.num_programs(0) - 1)
    def _():
        for part in range(2):
            for col in range(dim // LANES):
                grads_ref[part, col * half : (col + 1) * half, :] = acc_s[
                    part * half : (part + 1) * half, col * LANES : (col + 1) * LANES
                ].astype(BF16)


def middle_back(dn, middle, dz, high, w_own, w_par, vecs, mask, after=()):
    rows_all, dim = middle.shape
    row = pl.BlockSpec((TILE, dim), lambda i: (i, 0))
    packed = w_own.size // LANES
    return launch(
        middle_back_body,
        "middle_back",
        (rows_all // TILE,),
        [
            (dn, row),
            (middle, row),
            (dz, row),
            (high, row),
            (w_own, full(w_own.shape)),
            (w_par, full(w_par.shape)),
            (vecs, full(vecs.shape)),
            (mask, pl.BlockSpec((TILE, 1), lambda i: (i, 0))),
        ],
        [
            ((rows_all, dim), F32, row, True),
            ((rows_all, dim), BF16, row),
            ((HEAD_ROWS, rows_all), F32, pl.BlockSpec((HEAD_ROWS, TILE), lambda i: (0, i))),
            ((2, packed, LANES), BF16, full((2, packed, LANES))),
            ((8, dim), F32, full((8, dim))),
        ],
        cost(4 * rows_all * dim * dim, rows_all * dim * 24),
        after=after,
        scratch=[pltpu.VMEM((dim, dim), F32)],
    )


def attention_back_body(
    docs_ref, q_ref, k_ref, v_ref, do_ref, lse_ref, lseg_ref, delta_ref, augk_ref, augq_ref,
    dq_ref, dk_ref, dv_ref, key_s, value_s, turned_s, dk_s, dv_s, *, first,
):
    pair = pl.program_id(0) + first
    rows_all = q_ref.shape[0]
    count = augq_ref.shape[0]
    local_rows = rows_all - count
    blocks = local_rows // BLOCK
    turned_s[...] = k_ref[...].T
    dk_s[...] = jnp.zeros_like(dk_s)
    dv_s[...] = jnp.zeros_like(dv_s)
    dq_parts = [[] for _ in range(blocks + 1)]
    for head in range(2):
        mine, other = head_lanes(head)
        key_s[...] = k_ref[...] * mine + augk_ref[...] * other
        value_s[...] = v_ref[...] * mine
        head_rows = slice(head * HD, (head + 1) * HD)
        index = 2 * pair + head

        def grads(key_cat, value_cat, turned_cat, query_rows, aug, lse):
            queries = q_ref[query_rows, :] * mine
            douts = do_ref[query_rows, :] * mine
            delta = delta_ref[pl.ds(index, 1), query_rows]
            probs = jnp.exp(nt(key_cat, queries + aug * other) - lse)
            d_scores = (probs * (nt(value_cat, douts) - delta)).astype(BF16)
            d_key = nn(d_scores, queries)
            d_value = nn(probs.astype(BF16), douts)
            return nn(turned_cat, d_scores), d_key, d_value

        for block in range(blocks):
            rows = slice(block * BLOCK, (block + 1) * BLOCK)
            start = pl.multiple_of(local_rows + docs_ref[block] * GLOB, GLOB)
            doc_rows = pl.ds(start, GLOB)
            key_cat = jnp.concatenate([key_s[rows, :], key_s[doc_rows, :]], 0)
            value_cat = jnp.concatenate([value_s[rows, :], value_s[doc_rows, :]], 0)
            turned_cat = jnp.concatenate(
                [turned_s[head_rows, rows], turned_s[head_rows, doc_rows]], 1
            )
            d_query, d_key, d_value = grads(
                key_cat, value_cat, turned_cat, rows, lane_one(0), lse_ref[block, 0, head : head + 1, :]
            )
            dq_parts[block].append(d_query)
            dk_s[rows, :] += d_key[:BLOCK]
            dk_s[doc_rows, :] += d_key[BLOCK:]
            dv_s[rows, :] += d_value[:BLOCK]
            dv_s[doc_rows, :] += d_value[BLOCK:]
        rows = slice(local_rows, rows_all)
        d_query, d_key, d_value = grads(
            key_s[...], value_s[...], turned_s[head_rows, :], rows, augq_ref[...],
            lseg_ref[pl.ds(index, 1), :],
        )
        dq_parts[blocks].append(d_query)
        dk_s[...] += d_key
        dv_s[...] += d_value
    for block in range(blocks + 1):
        begin = block * BLOCK
        made = jnp.concatenate(dq_parts[block], 0).T
        dq_ref[begin : begin + made.shape[0], :] = (
            made.astype(BF16).astype(F32) * SCALE
        ).astype(BF16)
    dk_ref[...] = dk_s[...].astype(BF16)
    dv_ref[...] = dv_s[...].astype(BF16)


def attention_back(
    docs, qkv, d_attn, lse, lse_glob, delta, augk, augq, pairs, first, number, held=(), after=()
):
    rows_all = qkv.shape[0]
    count = augq.shape[0]
    blocks = (rows_all - count) // BLOCK

    def block(kind):
        column = pair_column(kind, pairs)
        return (qkv, pl.BlockSpec((rows_all, LANES), lambda p, docs: (0, column(p + first))))

    straight = pl.BlockSpec((rows_all, LANES), lambda p, docs: (0, p + first))
    work = 2 * number * (blocks * BLOCK * (BLOCK + GLOB) + rows_all * count)
    return launch(
        functools.partial(attention_back_body, first=first),
        "attention_back",
        (number,),
        [
            block(0),
            block(1),
            block(2),
            (d_attn, straight),
            (lse, pl.BlockSpec((blocks, 1, 2, BLOCK), lambda p, docs: (0, p + first, 0, 0))),
            (lse_glob, full(lse_glob.shape)),
            (delta, full(delta.shape)),
            (augk, full(augk.shape)),
            (augq, full(augq.shape)),
        ],
        [((rows_all, pairs * LANES), BF16, straight)] * 3,
        cost(work * 5 * 512, number * rows_all * LANES * 14, work),
        prefetch=(docs,),
        held=held,
        after=after,
        scratch=[
            pltpu.VMEM((rows_all, LANES), BF16),
            pltpu.VMEM((rows_all, LANES), BF16),
            pltpu.VMEM((LANES, rows_all), BF16),
            pltpu.VMEM((rows_all, LANES), F32),
            pltpu.VMEM((rows_all, LANES), F32),
        ],
    )


def project_grad_body(
    turned_ref, dq_ref, dk_ref, dv_ref, weight_ref, vecs_ref, mid_ref, *rest, shared
):
    up_refs, grads_ref = rest[:-1], rest[-1]
    dim, _ = turned_ref.shape
    width = dq_ref.shape[1]
    cols = width // LANES
    count = 3 * cols
    ones = jnp.ones((8, width), BF16)
    sums, dots, shifts = [], None, None
    for kind, ref in enumerate((dq_ref, dk_ref, dv_ref)):
        made = nn(turned_ref[...], ref[...])
        weight = weight_ref[:, kind * width : (kind + 1) * width]
        total = jnp.sum(ref[...].astype(F32), axis=0, keepdims=True)
        sums.append(total)
        scaled = made * weight.astype(F32)
        first = scaled.astype(BF16)
        second = (scaled - first.astype(F32)).astype(BF16)
        dot = nt(ones, first) + nt(ones, second)
        first = total.astype(BF16).astype(F32)
        second = (total - first).astype(BF16).astype(F32)
        parts = jnp.concatenate([first, second, jnp.zeros((6, width), F32)], 0)
        shift = jnp.sum(nt(parts.astype(BF16), weight), axis=0, keepdims=True)
        dots = dot if dots is None else dots + dot
        shifts = shift if shifts is None else shifts + shift
        low = made.astype(BF16)
        for col in range(cols):
            for part in range(2):
                number = 2 * (kind * cols + col) + part
                spot = number % count * width
                grads_ref[number // count, spot : spot + width, :] = low[
                    part * width : (part + 1) * width, col * LANES : (col + 1) * LANES
                ]
    gains = (dots[0:1, :] - vecs_ref[1:2, :] * shifts) / vecs_ref[0:1, :]
    small = [mid_ref[row : row + 1, :] * shared for row in range(4)]
    small += [gains, shifts, sums[0], sums[2]]
    small += [ref[...] for ref in up_refs]
    pieces = []
    for row in small:
        pieces += [row[:, col * LANES : (col + 1) * LANES] for col in range(row.shape[1] // LANES)]
    pieces.append(jnp.zeros((LANES - len(pieces), LANES), F32))
    grads_ref[0, count * width :, :] = jnp.concatenate(pieces, 0).astype(BF16)
    grads_ref[1, count * width :, :] = jnp.zeros((LANES, LANES), BF16)


def project_grad(turned, dq, dk, dv, weight, vecs, mid_sums, up_sums, half, after=()):
    dim, rows_all = turned.shape
    width = dq.shape[1] // 2
    grads = pl.BlockSpec((rows_all, width), lambda i: (0, half))
    shape = (2, 3 * width // LANES * dim // 2 + LANES, LANES)
    return launch(
        functools.partial(project_grad_body, shared=1.0 - half),
        "project_grad",
        (1,),
        [
            (turned, full(turned.shape)),
            (dq, grads),
            (dk, grads),
            (dv, grads),
            (weight, full(weight.shape)),
            (vecs, full(vecs.shape)),
            (mid_sums, full(mid_sums.shape)),
        ]
        + [(up, full(up.shape)) for up in up_sums],
        [(shape, BF16, full(shape))],
        cost(6 * rows_all * dim * width, rows_all * (dim + 3 * width) * 2),
        after=after,
    )[0]


def input_back_body(
    place_ref, dq_ref, dk_ref, dv_ref, own_ref, par_ref, x_ref, dmid_ref, vecs_ref,
    tokens_ref, leave_ref, stay_ref, *, number,
):
    step = pl.program_id(0)
    last = pl.num_programs(0) - 1
    half = own_ref.shape[1] // 3
    d_hidden = None
    for part, weight in enumerate((own_ref, par_ref)):
        cols = slice(part * half, (part + 1) * half)
        joined = jnp.concatenate([dq_ref[:, cols], dk_ref[:, cols], dv_ref[:, cols]], 1)
        made = nt(joined, weight[...])
        d_hidden = made if d_hidden is None else d_hidden + made

    @pl.when(step < last)
    def _():
        xhat, inv = normed(x_ref[...].astype(F32))
        tokens_ref[...] = dmid_ref[...] + norm_back(xhat, inv, vecs_ref[0:1, :], d_hidden)

    @pl.when(step == last)
    def _():
        low = d_hidden.astype(BF16)
        cut = low.shape[0] // 2
        for side in range(2):

            @pl.when(place_ref[number] == side)
            def _(side=side):
                stay_ref[...] = low[side * cut : (side + 1) * cut]
                leave_ref[...] = low[(1 - side) * cut : (2 - side) * cut]


def input_back(place, number, dq, dk, dv, w_own, w_par, x, d_mid, vecs, after=()):
    rows_all, dim = dq.shape
    tiles = rows_all // TILE
    row = pl.BlockSpec((TILE, dim), lambda i, place: (i, 0))
    local = pl.BlockSpec((TILE, dim), lambda i, place: (jnp.minimum(i, tiles - 2), 0))
    cut = ((rows_all - x.shape[0]) // 2, dim)
    return launch(
        functools.partial(input_back_body, number=number),
        "input_back",
        (tiles,),
        [
            (dq, row),
            (dk, row),
            (dv, row),
            (w_own, full(w_own.shape)),
            (w_par, full(w_par.shape)),
            (x, local),
            (d_mid, row),
            (vecs, full(vecs.shape)),
        ],
        [
            (x.shape, F32, local, True),
            (cut, BF16, full(cut)),
            (cut, BF16, full(cut)),
        ],
        cost(6 * rows_all * dim * dim, rows_all * dim * 16 + 6 * dim * dim),
        prefetch=(place,),
        after=after,
    )


def glob_input_body(kept_ref, got_ref, x_ref, dmid_ref, vecs_ref, out_ref):
    d_hidden = kept_ref[...].astype(F32) + got_ref[...].astype(F32)
    xhat, inv = normed(x_ref[...].astype(F32))
    out_ref[...] = dmid_ref[...] + norm_back(xhat, inv, vecs_ref[0:1, :], d_hidden)


def glob_input(place, kept, got, x, d_mid, vecs, after=()):
    own, dim = x.shape
    first = (d_mid.shape[0] - 2 * GLOB) // own
    spec = pl.BlockSpec((own, dim), lambda i, place: (0, 0))
    here = pl.BlockSpec((own, dim), lambda i, place: (first + place[2] // own, 0))

    def body(place_ref, *refs):
        glob_input_body(*refs)

    return launch(
        body,
        "glob_input",
        (1,),
        [(kept, spec), (got, spec), (x, spec), (d_mid, here), (vecs, full(vecs.shape))],
        [((own, dim), F32, spec)],
        cost(0, own * dim * 14),
        prefetch=(place,),
        after=after,
    )[0]


def pair_add(left, right):
    return (left.astype(F32) + right.astype(F32)).astype(BF16)


def add_split_body(place_ref, kept_go, got_go, kept_stay, got_stay, go_ref, stay_ref):
    go_ref[...] = pair_add(kept_go[0], got_go[0])
    stay_ref[...] = pair_add(kept_stay[0], got_stay[0])


def add_split(place, number, kept, got, after=()):
    lanes = kept.shape[-1]
    kept = kept.reshape(2, -1, lanes)
    got = got.reshape(kept.shape)
    rows = kept.shape[1]
    tiles = next((t for t in (4, 2) if rows % (16 * t) == 0 and rows >= 512 * t), 1)
    tile = rows // tiles

    def spec(flipped):
        def at(i, place):
            side = place[number]
            return (1 - side if flipped else side, i, 0)

        return pl.BlockSpec((1, tile, lanes), at)

    out = pl.BlockSpec((tile, lanes), lambda i, place: (i, 0))
    return launch(
        add_split_body,
        "add_split",
        (tiles,),
        [(kept, spec(True)), (got, spec(True)), (kept, spec(False)), (got, spec(False))],
        [((rows, lanes), BF16, out), ((rows, lanes), BF16, out)],
        cost(kept.size, kept.size * 6),
        prefetch=(place,),
        after=after,
    )


def start_body(place_ref, *refs, number):
    go_ref, stay_ref = refs[-2:]
    side = place_ref[number]
    first = 0
    for own_ref, got_ref in zip(refs[:-2:2], refs[1:-2:2]):
        rows = slice(first, first + own_ref.shape[1])
        go_ref[rows, :] = pair_add(own_ref[1 - side], got_ref[1 - side])
        stay_ref[rows, :] = pair_add(own_ref[side], got_ref[side])
        first = rows.stop


def start_sum(place, number, pairs, after=()):
    arrays = [array for pair in pairs for array in pair]
    shape = (sum(own.shape[1] for own, _ in pairs), LANES)
    return launch(
        functools.partial(start_body, number=number),
        "start_sum",
        (1,),
        [(a, full(a.shape)) for a in arrays],
        [(shape, BF16, full(shape)), (shape, BF16, full(shape))],
        cost(shape[0] * LANES * 2, shape[0] * LANES * 12),
        prefetch=(place,),
        after=after,
    )


def add_body(kept_ref, got_ref, out_ref):
    out_ref[...] = pair_add(kept_ref[...], got_ref[...])


def add_rows(kept, got, after=()):
    spec = full(kept.shape)
    return launch(
        add_body, "add_rows", (1,), [(kept, spec), (got, spec)], [(kept.shape, BF16, spec)],
        cost(kept.size, kept.size * 6), after=after,
    )[0]


def join_body(place_ref, mine_ref, other_ref, out_ref):
    step = pl.program_id(0)
    half = pl.num_programs(0) // 2

    @pl.when(step < half)
    def _():
        out_ref[0] = mine_ref[...]

    @pl.when(step >= half)
    def _():
        out_ref[0] = other_ref[...]


def join(place, number, mine, other, after=()):
    rows, lanes = mine.shape
    tiles = 2 if rows % 32 == 0 and rows >= 2048 else 1
    tile = rows // tiles

    def at(i, place):
        side = place[number]
        return (jnp.where(i < tiles, side, 1 - side), i % tiles, 0)

    made = launch(
        join_body,
        "join",
        (2 * tiles,),
        [
            (mine, pl.BlockSpec((tile, lanes), lambda i, place: (jnp.minimum(i, tiles - 1), 0))),
            (other, pl.BlockSpec((tile, lanes), lambda i, place: (jnp.maximum(i - tiles, 0), 0))),
        ],
        [((2, rows, lanes), BF16, pl.BlockSpec((1, tile, lanes), at))],
        cost(0, mine.size * 8),
        prefetch=(place,),
        after=after,
    )[0]
    return made.reshape(2 * rows, lanes)


def by_side(place_ref, number, mine_ref, other_ref, write):
    for half in range(2):
        for ref, here in ((mine_ref, place_ref[number] == half), (other_ref, place_ref[number] != half)):

            @pl.when(here)
            def _(ref=ref, half=half):
                write(ref, half)


def ffn_unpack_body(place_ref, mine_ref, other_ref, up_ref, down_ref, *rest, number, chunk):
    dim = up_ref.shape[0]
    units = up_ref.shape[1]

    def write(ref, half):
        count = units * dim // LANES
        first = half * count
        spot = 0
        for step in range(units // chunk):
            for col in range(chunk // LANES):
                if first <= spot < first + count:
                    begin = step * chunk + col * LANES
                    up_ref[:, begin : begin + LANES] = ref[spot - first : spot - first + dim, :].astype(F32)
                spot += dim
            for col in range(dim // LANES):
                if first <= spot < first + count:
                    down_ref[step * chunk : (step + 1) * chunk, col * LANES : (col + 1) * LANES] = ref[
                        spot - first : spot - first + chunk, :
                    ].astype(F32)
                spot += chunk
        for out_ref in rest:
            rows, cols = out_ref.shape[0], out_ref.shape[1] // LANES // 2
            for col in range(cols):
                begin = (half * cols + col) * LANES
                out_ref[:, begin : begin + LANES] = ref[
                    count + col * rows : count + (col + 1) * rows, :
                ].astype(F32)

    by_side(place_ref, number, mine_ref, other_ref, write)


def ffn_unpack(place, number, mine, other, dim, half, units, part, held=(), extra=(), after=()):
    spec = full(mine.shape)
    one = pl.Buffered(1)
    return launch(
        functools.partial(ffn_unpack_body, number=number, chunk=min(FFN_CHUNK, units)),
        "ffn_unpack",
        (1,),
        [(mine, spec), (other, spec)],
        [
            ((dim, half), F32, pl.BlockSpec((dim, units), lambda i, place: (0, part), pipeline_mode=one), True),
            ((half, dim), F32, pl.BlockSpec((units, dim), lambda i, place: (part, 0), pipeline_mode=one), True),
        ]
        + [(shape, F32, full(shape)) for shape in extra],
        cost(0, mine.size * 12),
        prefetch=(place,),
        held=held,
        after=after,
    )


def tail_unpack_body(place_ref, mine_ref, other_ref, q_ref, k_ref, v_ref, small_ref, *, number):
    dim, width = q_ref.shape
    cols = width // LANES
    count = 3 * cols

    def write(ref, half):
        for spot in range(count):
            unit, part = divmod(half * count + spot, 2)
            kind, col = unit // cols, unit % cols
            (q_ref, k_ref, v_ref)[kind][
                part * width : (part + 1) * width, col * LANES : (col + 1) * LANES
            ] = ref[spot * width : (spot + 1) * width, :].astype(F32)
        if half == 0:
            small_ref[...] = ref[count * width :, :].astype(F32)

    by_side(place_ref, number, mine_ref, other_ref, write)


def tail_unpack(place, number, mine, other, dim, width):
    spec = full(mine.shape)
    shapes = [(dim, width)] * 3 + [(LANES, LANES)]
    return launch(
        functools.partial(tail_unpack_body, number=number),
        "tail_unpack",
        (1,),
        [(mine, spec), (other, spec)],
        [(shape, F32, full(shape)) for shape in shapes],
        cost(0, mine.size * 12),
        prefetch=(place,),
    )


def finish_body(mine_ref, theirs_ref, *outs):
    rows = 0
    for number, out_ref in enumerate(outs):
        count = out_ref.shape[0] // LANES
        pieces = []
        for row in range(rows, rows + count):
            piece = mine_ref[row : row + 1, :]
            pieces.append(piece + theirs_ref[row : row + 1, :] if number < 6 else piece)
        out_ref[...] = jnp.concatenate(pieces, 1).reshape(-1)
        rows += count


def finish(mine, theirs, sizes):
    return launch(
        finish_body,
        "finish",
        (1,),
        [(mine, full(mine.shape)), (theirs, full(theirs.shape))],
        [((size,), F32, full((size,))) for size in sizes],
        cost(0, 4 * sum(sizes)),
    )


def per_device(
    tokens, glob_tokens, w_query, b_query, w_key, w_value, b_value, w_out, b_out, w_up, b_up,
    w_down, b_down, gain_attn, shift_attn, gain_ffn, shift_ffn, doc_blocks, doc_tail,
    grad_tokens, grad_glob,
):
    seq_size = lax.axis_size("seq")
    seq_pos = lax.axis_index("seq")
    tp_pos = lax.axis_index("tp")
    rows, dim = tokens.shape
    own_glob = glob_tokens.shape[0]
    half = w_query.shape[1]
    units = w_up.shape[1]
    pairs = 2 * half // PAIR
    blocks = rows // BLOCK
    glob_rows = 2 * GLOB
    rows_all = rows + glob_rows
    group_size = GROUP_BLOCKS // (2 * blocks)
    group_bits = group_size.bit_length() - 1
    seq_bits = seq_size.bit_length() - 1
    group_pos = seq_pos % group_size
    own_first = (group_pos * 2 + tp_pos) * own_glob

    def flip(value, bit):
        return lax.ppermute(value, "seq", [(s, s ^ (1 << bit)) for s in range(seq_size)])

    def swap(value):
        return lax.ppermute(value, "tp", [(0, 1), (1, 0)])

    rest = tuple(range(3, seq_bits))
    orders = {
        "one": ((0, 1, 2, *rest), (2, 0, 1, *rest)),
        "two": ((1, 0, 2, *rest), (2, 1, 0, *rest)),
        "tail": ((0, 1, 2, *rest), (2, 0, 1, *rest)),
    }
    place = [
        (seq_pos * 2 + tp_pos) * blocks,
        (seq_pos // group_size) * 2,
        own_first,
        jnp.int32(own_glob),
        group_pos,
        tp_pos,
    ]
    group_sides = len(place)
    place += [(seq_pos >> bit) & 1 for bit in range(group_bits)] + [tp_pos]
    job_sides = {}
    for name, (zero, one) in orders.items():
        job_sides[name] = len(place)
        place += [(seq_pos >> jnp.where(tp_pos == 0, a, b)) & 1 for a, b in zip(zero, one)]
    place = jnp.stack(place).astype(jnp.int32)

    def trade(value, name, step):
        zero, one = orders[name][0][step], orders[name][1][step]
        links = [(2 * s, 2 * (s ^ (1 << zero))) for s in range(seq_size)]
        links += [(2 * s + 1, 2 * (s ^ (1 << one)) + 1) for s in range(seq_size)]
        return lax.ppermute(value, ("seq", "tp"), links)

    gathered = jnp.stack([glob_tokens, grad_glob])[None]
    qkv_own = jnp.concatenate([w_query, w_key, w_value], 1)
    qkv_par = swap(qkv_own)
    vecs, half_own = pack_vectors(
        [gain_attn, shift_attn, gain_ffn, shift_ffn, b_out, b_down], [b_query, b_value, b_up]
    )
    half_par = swap(half_own)
    halves = (half_own, half_par)
    docs, augk, augq, mask = layout(place, doc_blocks, doc_tail, rows_all, glob_rows, blocks)
    tiles = rows // TILE
    held = ()
    cuts = [tiles * (bit + 1) // group_bits for bit in range(group_bits)]
    done = 0
    for bit in range(group_bits):
        other = flip(gathered, bit)
        if cuts[bit] > done:
            held = project(
                tokens, vecs, halves, qkv_own, qkv_par, rows_all, done, cuts[bit] - done, held,
                (gathered,),
            )
            done = cuts[bit]
        gathered = jnp.concatenate([gathered, other], 0)
    x_glob, dz_all = order_rows(place, gathered, swap(gathered), grad_tokens)
    qkv, hidden_turned = project(
        x_glob, vecs, halves, qkv_own, qkv_par, rows_all, tiles, glob_rows // TILE, held
    )
    out_par = swap(w_out)
    up_par = swap(w_up)
    down_par = swap(w_down)

    mine, theirs = glob_forward(qkv, augk, augq, pairs)
    state = merge(mine, swap(theirs))
    outs = ()
    for bit in range(group_bits):
        other = flip(state, bit)
        first, end = pairs * bit // group_bits, pairs * (bit + 1) // group_bits
        outs = local_forward(docs, qkv, augk, pairs, blocks, first, end - first, outs, (state,))
        state = merge(state, other, (outs[1],))
    state_par = swap(state)
    high, lse = outs
    held = middle_local(high, tokens, w_out, out_par, vecs, (state,))
    middle, hidden, ffn_turned, high, lse_glob = middle_glob(
        state, state_par, x_glob, w_out, out_par, vecs, [*held, high]
    )

    class Job:
        def __init__(self, name, sums, after=()):
            self.name, self.step = name, 0
            self.go, self.stay = start_sum(place, job_sides[name], sums, after)
            self.other = trade(self.go, name, 0)
            self.marker = self.stay

        def advance(self, after=()):
            first, step = job_sides[self.name], self.step
            if step < seq_bits - 1:
                self.go, self.stay = add_split(place, first + step + 1, self.stay, self.other, after)
                self.other = trade(self.go, self.name, step + 1)
                self.marker = self.stay
            elif step == seq_bits - 1:
                self.shard = add_rows(self.stay, self.other, after)
                self.other = trade(self.shard, self.name, seq_bits - 1)
                self.marker = self.shard
            elif step < 2 * seq_bits - 1:
                back = 2 * seq_bits - 1 - step
                self.shard = join(place, first + back, self.shard, self.other, after)
                self.other = trade(self.shard, self.name, back - 1)
                self.marker = self.shard
            self.step += 1

    jobs = []

    def move(mark):
        for job in jobs:
            job.advance((mark,))
        return [job.marker for job in jobs if job.step < 2 * seq_bits]

    part = units // 2
    acts, ups, grads = [], [[], []], []
    dn = None
    marks = []
    for number in range(2):
        first = number * part
        for which, (up, down, vec) in ((1, (up_par, down_par, half_par)), (0, (w_up, w_down, half_own))):
            dn, act, grad, up_sum = ffn_part(
                hidden, ffn_turned, dz_all, up, vec, down, mask, first, part, dn, marks
            )
            marks = move(up_sum)
            grad = grad.reshape(2, -1, LANES)
            acts.append((act, down, number))
            ups[which].append(up_sum)
            grads.append(swap(grad) if which else grad)
        if number == 0:
            jobs.append(Job("one", [(grads[1], grads[0])]))
            marks = [jobs[0].marker]

    d_mid, d_attn, delta, out_grad, mid_sums = middle_back(
        dn, middle, dz_all, high, w_out, out_par, vecs, mask, marks
    )
    marks = move(mid_sums)
    out_grad = out_grad.reshape(2, 2, -1, LANES)
    jobs.append(Job("two", [(grads[3], grads[2]), (out_grad[0], swap(out_grad[1]))]))
    marks.append(jobs[1].marker)
    grads = ()
    for pair in range(pairs):
        grads = attention_back(
            docs, qkv, d_attn, lse, lse_glob, delta, augk, augq, pairs, pair, 1, grads, marks
        )
        marks = move(grads[0])
    dq, dk, dv = grads
    tail_par = project_grad(
        hidden_turned, dq, dk, dv, qkv_par, vecs, mid_sums, ups[1], 1, marks
    )
    tail_own = project_grad(
        hidden_turned, dq, dk, dv, qkv_own, vecs, mid_sums, ups[0], 0, (tail_par,)
    )
    marks = move(tail_own)
    jobs.append(Job("tail", [(tail_own, swap(tail_par))], marks))
    marks = [jobs[2].marker]

    top_side = group_sides + group_bits - 1
    tokens_grad, go, stay = input_back(
        place, top_side, dq, dk, dv, qkv_own, qkv_par, tokens, d_mid, vecs, marks
    )
    marks = move(stay)
    got = flip(go, group_bits - 1)
    for bit in reversed(range(group_bits)):
        number = group_sides + bit - 1 if bit else group_sides + group_bits
        go, stay = add_split(place, number, stay, got, marks)
        got = flip(go, bit - 1) if bit else swap(go)
        marks = move(stay)
    glob_grad = glob_input(place, stay, got, glob_tokens, d_mid, vecs, marks)
    kinds = ffn_unpack(
        place, job_sides["one"], jobs[0].shard, jobs[0].other, dim, units, part, 0, after=(glob_grad,)
    )
    marks = move(kinds[0])
    out_tokens, out_all = output_rows(
        place, middle, vecs, [a for a, _, _ in acts], [(w, n) for _, w, n in acts], own_glob, marks
    )
    out_glob = lax.dynamic_slice_in_dim(out_all, own_first, own_glob, 0)
    marks = move(out_all)
    while jobs[1].step < 2 * seq_bits - 1:
        marks = move(out_all)
    up_grad, down_grad, w_out_grad = ffn_unpack(
        place, job_sides["two"], jobs[1].shard, jobs[1].other, dim, units, part, 1, kinds,
        [(half, dim)], marks,
    )
    while jobs[2].step < 2 * seq_bits - 1:
        jobs[2].advance((w_out_grad,))
    q_grad, k_grad, v_grad, small = tail_unpack(
        place, job_sides["tail"], jobs[2].shard, jobs[2].other, dim, half
    )
    (
        gain_f_grad, shift_f_grad, out_bias, down_bias, gain_a_grad, shift_a_grad, b_query_grad,
        b_value_grad, b_up_grad,
    ) = finish(small, swap(small), [dim] * 6 + [half, half, units])
    return (
        out_tokens, out_glob, tokens_grad, glob_grad, q_grad, b_query_grad, k_grad,
        v_grad, b_value_grad, w_out_grad, out_bias, up_grad, b_up_grad, down_grad, down_bias,
        gain_a_grad, shift_a_grad, gain_f_grad, shift_f_grad,
    )


def solution(mesh):
    rows = P(("seq", "tp"), None)
    cols, part, whole = P(None, "tp"), P("tp"), P()
    lines = P("tp", None)
    return jax.shard_map(
        per_device,
        mesh=mesh,
        in_specs=(
            rows, rows, cols, part, cols, cols, part, lines, whole, cols, part, lines, whole,
            whole, whole, whole, whole, whole, whole, rows, rows,
        ),
        out_specs=(
            rows, rows, rows, rows, cols, part, cols, cols, part, lines, whole, cols, part, lines,
            whole, whole, whole, whole, whole,
        ),
        check_vma=False,
    )
```

```python
import functools

import jax
import jax.numpy as jnp
from jax import lax
from jax.experimental import pallas as pl
from jax.experimental.pallas import tpu as pltpu
from jax.sharding import PartitionSpec as P

HD = 64
BLOCK = 512
GLOB = 128
GROUP_BLOCKS = 32
EPS = 1e-05
SCALE = 0.125
NEG = -1e30
SHIFT = -10.0
FAINT = 1e-25
TILE = 256
PAIR = 2 * HD
LANES = 128
STATS = 16
HEAD_ROWS = 16
FFN_CHUNK = 256
WEIGHT = 1
F32 = jnp.float32
BF16 = jnp.bfloat16
VMEM_BYTES = 14 * 2**20


def nn(left, right):
    return jnp.dot(left, right, preferred_element_type=F32)


def nt(left, right):
    return lax.dot_general(left, right, (((1,), (1,)), ((), ())), preferred_element_type=F32)


def tn(left, right):
    return lax.dot_general(left, right, (((0,), (0,)), ((), ())), preferred_element_type=F32)


def normed(values):
    row_mean = jnp.mean(values, axis=-1, keepdims=True)
    centred = values - row_mean
    row_var = jnp.mean(centred * centred, axis=-1, keepdims=True)
    inv = lax.rsqrt(row_var + EPS)
    return centred * inv, inv


def norm_back(xhat, inv, gain_vec, cotangent):
    scaled = cotangent * gain_vec
    mean_one = jnp.mean(scaled, axis=-1, keepdims=True)
    mean_two = jnp.mean(scaled * xhat, axis=-1, keepdims=True)
    return inv * (scaled - mean_one - xhat * mean_two)


def full(shape):
    zeros = (0,) * len(shape)
    return pl.BlockSpec(shape, lambda *_: zeros, pipeline_mode=pl.Buffered(1))


ANY = pl.BlockSpec(memory_space=pl.ANY)


def far(array):
    return pltpu.with_memory_space_constraint(array, pltpu.HBM)


def launch(
    body, name, grid, operands, outs, work, prefetch=(), held=(), after=(), scratch=(), aliased=0
):
    arrays = [*prefetch, *(a for a, _ in operands), *held, *after]
    specs = [*(spec for _, spec in operands), *([ANY] * (len(held) + len(after)))]
    first = len(prefetch) + len(operands)
    spare = len(held) + len(after)

    def whole(*refs):
        return body(*refs[:first], *refs[first + spare :])

    return pl.pallas_call(
        whole,
        grid_spec=pltpu.PrefetchScalarGridSpec(
            num_scalar_prefetch=len(prefetch),
            grid=grid,
            in_specs=specs,
            out_specs=[out[2] for out in outs],
            scratch_shapes=list(scratch),
        ),
        out_shape=[(pltpu.HBM if out[3:] else jax.ShapeDtypeStruct)(out[0], out[1]) for out in outs],
        input_output_aliases={first + i: aliased + i for i in range(len(held))},
        compiler_params=pltpu.CompilerParams(
            vmem_limit_bytes=VMEM_BYTES, dimension_semantics=("arbitrary",) * len(grid)
        ),
        cost_estimate=work,
        name=name,
    )(*arrays)


def cost(flops, nbytes, trans=0):
    scale = WEIGHT if flops > 2**28 else 1
    return pl.CostEstimate(
        flops=int(scale * flops), bytes_accessed=int(scale * nbytes), transcendentals=int(trans)
    )


def head_lanes(head):
    lane = lax.broadcasted_iota(jnp.int32, (1, LANES), 1)
    here = jnp.where(lane < HD, 1.0, 0.0)
    mine = here if head == 0 else 1.0 - here
    return mine.astype(BF16), (1.0 - mine).astype(BF16)


def lane_one(slot):
    lane = lax.broadcasted_iota(jnp.int32, (1, LANES), 1)
    return jnp.where((lane == slot) | (lane == slot + HD), 1.0, 0.0).astype(BF16)


def layout_body(
    place_ref, blocks_ref, tails_ref, docs_ref, augk_ref, augq_ref, mask_ref, seen_ref
):
    first_block, group_first, own_first = place_ref[0], place_ref[1], place_ref[2]
    own_count = place_ref[3]
    count = augq_ref.shape[0]
    rows = augk_ref.shape[0] - count
    lane = lax.broadcasted_iota(jnp.int32, (1, LANES), 1)
    slot = jnp.where(lane < HD, lane, lane - HD)
    column = lax.broadcasted_iota(jnp.int32, (8, count), 1)
    seen = (column >= own_first) & (column < own_first + own_count)
    for block in range(rows // BLOCK):
        index = first_block + block
        start, doc, real = jnp.int32(0), jnp.int32(0), jnp.int32(BLOCK)
        for number in range(blocks_ref.shape[0]):
            end = start + blocks_ref[number]
            inside = jnp.logical_and(index >= start, index < end)
            doc = jnp.where(inside, number, doc)
            real = jnp.where(
                jnp.logical_and(inside, index == end - 1), tails_ref[number], real
            )
            start = end
        doc = doc - group_first
        docs_ref[block] = doc
        seen = seen | ((column >= doc * GLOB) & (column < (doc + 1) * GLOB))
        row = lax.broadcasted_iota(jnp.int32, (BLOCK, 1), 0)
        padded = row >= real
        shut = ((slot == 1) & (doc != 0)) | ((slot == 2) & (doc != 1))
        shut = jnp.where(shut, 1, 0) + jnp.where(padded & (slot < 3), 1, 0)
        augk_ref[block * BLOCK : (block + 1) * BLOCK, :] = jnp.where(
            shut > 0, NEG, jnp.where(slot < 3, SHIFT, 0.0)
        ).astype(BF16)
    row = lax.broadcasted_iota(jnp.int32, (count, 1), 0)
    late = row >= GLOB
    shut = ((slot == 1) & late) | ((slot == 2) & ~late) | (slot == 3)
    augk_ref[rows:, :] = jnp.where(shut, NEG, jnp.where(slot < 3, SHIFT, 0.0)).astype(BF16)
    owned = (row >= own_first) & (row < own_first + own_count)
    on = ((slot == 1) & ~late) | ((slot == 2) & late) | ((slot == 3) & ~owned)
    augq_ref[...] = jnp.where(on, 1.0, 0.0).astype(BF16)
    seen_ref[...] = jnp.where(seen, 1.0, 0.0)
    mask_ref[:rows, :] = jnp.ones((rows, 1), F32)
    mask_ref[rows:, :] = jnp.where(owned, 1.0, 0.0)


def layout(place, doc_blocks, doc_tail, rows_all, count, blocks, after=()):
    smem = pl.BlockSpec(memory_space=pltpu.SMEM)
    return launch(
        layout_body,
        "layout",
        (1,),
        [],
        [
            ((blocks,), jnp.int32, smem),
            ((rows_all, LANES), BF16, full((rows_all, LANES))),
            ((count, LANES), BF16, full((count, LANES))),
            ((rows_all, 1), F32, full((rows_all, 1))),
            ((8, count), F32, full((8, count))),
        ],
        cost(0, rows_all * LANES * 4),
        prefetch=(place, doc_blocks, doc_tail),
        after=after,
    )


def pack_body(*refs):
    vecs_ref, half_ref = refs[-2:]
    for row, ref in enumerate(refs[:6]):
        vecs_ref[row : row + 1, :] = ref[...].reshape(1, -1)
    vecs_ref[6:, :] = jnp.zeros((2, vecs_ref.shape[1]), F32)
    half_ref[...] = jnp.zeros(half_ref.shape, F32)
    first = 0
    for ref in refs[6:9]:
        count = ref.shape[0]
        half_ref[0:1, first : first + count] = ref[...].reshape(1, -1)
        first += count


def pack_vectors(vectors, parts):
    arrays = [far(array) for array in (*vectors, *parts)]
    dim = vectors[0].shape[0]
    width = sum(part.shape[0] for part in parts)
    return launch(
        pack_body,
        "pack_vectors",
        (1,),
        [(a, full(a.shape)) for a in arrays],
        [((8, dim), F32, full((8, dim))), ((8, width), F32, full((8, width)))],
        cost(0, 32 * (dim + width)),
    )


def order_body(place_ref, mine_ref, theirs_ref, grads_ref, x_ref, dz_ref):
    step = pl.program_id(0)
    last = pl.num_programs(0) - 1
    chips, _, own, _ = mine_ref.shape

    @pl.when(step < last)
    def _():
        dz_ref[...] = grads_ref[...]

    @pl.when(step == last)
    def _():
        for chip in range(chips):
            for side, ref in enumerate((mine_ref, theirs_ref)):
                spot = (place_ref[4] ^ chip) * 2 + (place_ref[5] ^ side)
                here = pl.ds(pl.multiple_of(spot * own, own), own)
                x_ref[here, :] = ref[chip, 0]
                dz_ref[here, :] = ref[chip, 1]


def order_rows(place, mine, theirs, grads, after=()):
    chips, _, own, dim = mine.shape
    count = chips * 2 * own
    tiles = grads.shape[0] // count
    return launch(
        order_body,
        "order_rows",
        (tiles + 1,),
        [
            (mine, full(mine.shape)),
            (theirs, full(mine.shape)),
            (grads, pl.BlockSpec((count, dim), lambda i, place: (jnp.minimum(i, tiles - 1), 0))),
        ],
        [
            ((count, dim), BF16, full((count, dim))),
            (
                (grads.shape[0] + count, dim),
                BF16,
                pl.BlockSpec((count, dim), lambda i, place: (i, 0)),
            ),
        ],
        cost(0, 4 * grads.size),
        prefetch=(place,),
        after=after,
    )


def stack_body(left_ref, right_ref, out_ref):
    count = left_ref.shape[0]
    out_ref[:count] = left_ref[...]
    out_ref[count:] = right_ref[...]


def stack_two(left, right, after=()):
    shape = (2 * left.shape[0], *left.shape[1:])
    return launch(
        stack_body,
        "stack_two",
        (1,),
        [(left, full(left.shape)), (right, full(right.shape))],
        [(shape, left.dtype, full(shape))],
        cost(0, left.size * 8),
        after=after,
    )[0]


def project_body(x_ref, vecs_ref, own_vec_ref, par_vec_ref, *rest, given):
    qkv_ref, turned_ref = rest[-2 - given : len(rest) - given]
    if given:
        both_ref = rest[-1]
        parts = rest[:6]
        width = parts[0].shape[1]

        @pl.when(pl.program_id(0) == 0)
        def _():
            for number, part in enumerate(parts):
                half, kind = divmod(number, 3)
                both_ref[half, :, kind * width : (kind + 1) * width] = part[...]

    else:
        both_ref = rest[0]
    xhat, _ = normed(x_ref[...].astype(F32))
    hidden = (xhat * vecs_ref[0:1, :] + vecs_ref[1:2, :]).astype(BF16)
    turned_ref[...] = hidden.T
    width = both_ref.shape[2]
    third = width // 3
    for half, vec_ref in enumerate((own_vec_ref, par_vec_ref)):
        first = half * width
        made = nn(hidden, both_ref[half])
        bias = vec_ref[0:1, : 2 * third]
        qkv_ref[:, first : first + third] = (
            (made[:, :third] + bias[:, :third]) * SCALE
        ).astype(BF16)
        qkv_ref[:, first + third : first + 2 * third] = made[:, third : 2 * third].astype(BF16)
        qkv_ref[:, first + 2 * third : first + width] = (
            made[:, 2 * third :] + bias[:, third:]
        ).astype(BF16)


def project(x, vecs, halves, weights, after=()):
    rows, dim = x.shape
    given = len(weights) > 1
    half = 3 * weights[0].shape[1] if given else weights[0].shape[2]
    width = 2 * half
    both = (2, dim, half)
    return launch(
        functools.partial(project_body, given=int(given)),
        "project",
        (rows // TILE,),
        [
            (far(x) if given else x, pl.BlockSpec((TILE, dim), lambda i: (i, 0))),
            (vecs, full(vecs.shape)),
            (halves[0], full(halves[0].shape)),
            (halves[1], full(halves[1].shape)),
        ]
        + [(far(w), full(w.shape)) for w in weights],
        [
            ((rows, width), BF16, pl.BlockSpec((TILE, width), lambda i: (i, 0))),
            ((dim, rows), BF16, pl.BlockSpec((dim, TILE), lambda i: (0, i))),
        ]
        + ([(both, BF16, full(both), True)] if given else []),
        cost(2 * rows * dim * width, 2 * (rows * (2 * dim + width) + dim * width)),
        after=after,
    )


def pair_column(kind, pairs):
    half = pairs // 2
    return lambda p: (p // half) * 3 * half + kind * half + p % half


def write_stats(out_ref, head, lse):
    first = lse.astype(BF16).astype(F32)
    second = (lse - first).astype(BF16).astype(F32)
    third = lse - first - second
    row = lax.broadcasted_iota(jnp.int32, (STATS, lse.shape[1]), 0)
    held = jnp.where(row == 0, first, jnp.where(row == 1, second, jnp.where(row == 2, third, 0.0)))
    out_ref[head, HD : HD + STATS, :] = held.astype(BF16)


def read_stats(ref, head):
    held = ref[head, HD : HD + STATS, :].astype(F32)
    return held[0:1] + held[1:2] + held[2:3]


def summed_up(scores, values, seen=None):
    weights = jnp.exp(scores)
    total = jnp.sum(weights, axis=0, keepdims=True)
    summed = nn(values, weights.astype(BF16))
    faint = total < FAINT
    if seen is not None:
        faint = faint & (seen > 0.0)
    return summed, total, jnp.max(jnp.where(faint, 1.0, 0.0))


def summed_faint(scores, values):
    top = jnp.max(scores, axis=0, keepdims=True)
    weights = jnp.exp(scores - top)
    total = jnp.sum(weights, axis=0, keepdims=True)
    return nn(values, weights.astype(BF16)) / total, top + jnp.log(total)


def glob_forward_body(
    q_ref, k_ref, v_ref, kg_ref, vg_ref, augk_ref, augq_ref, seen_ref, own_ref, par_ref
):
    queries = q_ref[...]
    keys = jnp.concatenate([k_ref[...], kg_ref[...]], 0)
    values_turned = jnp.concatenate([v_ref[...], vg_ref[...]], 0).T
    seen = seen_ref[0:1, :]
    half = pl.num_programs(0) // 2

    def write(head, summed, lse):
        for ref, here in ((par_ref, pl.program_id(0) < half), (own_ref, pl.program_id(0) >= half)):

            @pl.when(here)
            def _(ref=ref):
                ref[head, :HD, :] = summed
                write_stats(ref, head, lse)

    both = []
    for head in range(2):
        mine, other = head_lanes(head)
        key_head = keys * mine + augk_ref[...] * other
        query_head = queries * mine + augq_ref[...] * other
        both.append(nt(key_head, query_head))
    results = []
    for head in range(2):
        values = values_turned[head * HD : (head + 1) * HD, :]
        summed, total, faint = summed_up(both[head], values, seen)
        some = total > 0.0
        safe = jnp.where(some, total, 1.0)
        results.append((summed / safe, jnp.where(some, jnp.log(safe), NEG), faint))
    for head, (summed, lse, _) in enumerate(results):
        write(head, summed.astype(BF16), lse)
    for head, (_, _, faint) in enumerate(results):

        @pl.when(faint > 0.0)
        def _(head=head):
            values = values_turned[head * HD : (head + 1) * HD, :]
            summed, lse = summed_faint(both[head], values)
            write(head, summed.astype(BF16), jnp.where(seen > 0.0, lse, NEG))


def glob_forward(qkv, qkv_glob, augk, augq, seen, pairs):
    count = augq.shape[0]
    half = pairs // 2

    def block(array, kind):
        column = pair_column(kind, pairs)
        return (
            array,
            pl.BlockSpec((array.shape[0], LANES), lambda p: (0, column((p + half) % pairs))),
        )

    work = 2 * pairs * augk.shape[0] * count
    shape = (pairs, HD + STATS, count)
    size = (2, HD + STATS, count)
    return launch(
        glob_forward_body,
        "glob_forward",
        (pairs,),
        [
            block(qkv_glob, 0),
            block(qkv, 1),
            block(qkv, 2),
            block(qkv_glob, 1),
            block(qkv_glob, 2),
            (augk, full(augk.shape)),
            (augq, full(augq.shape)),
            (seen, full(seen.shape)),
        ],
        [
            (shape, BF16, pl.BlockSpec(size, lambda p: (jnp.maximum(p - half, 0), 0, 0))),
            (shape, BF16, pl.BlockSpec(size, lambda p: (jnp.minimum(p, half - 1), 0, 0))),
        ],
        cost(work * 2 * 512, qkv.size * 2, work),
    )


def merge_body(left_ref, right_ref, out_ref):
    for head in range(left_ref.shape[0]):
        lse_left, lse_right = read_stats(left_ref, head), read_stats(right_ref, head)
        top = jnp.maximum(lse_left, lse_right)
        weight_left, weight_right = jnp.exp(lse_left - top), jnp.exp(lse_right - top)
        total = weight_left + weight_right
        out_left = left_ref[head, :HD, :].astype(F32)
        out_right = right_ref[head, :HD, :].astype(F32)
        merged = (out_left * weight_left + out_right * weight_right) / total
        out_ref[head, :HD, :] = merged.astype(BF16)
        write_stats(out_ref, head, top + jnp.log(total))


def merge(left, right, after=()):
    spec = full(left.shape)
    return launch(
        merge_body, "merge", (1,), [(left, spec), (right, spec)], [(left.shape, BF16, spec)],
        cost(left.size * 8, left.size * 6), after=after,
    )[0]


def local_forward_body(docs_ref, q_ref, k_ref, v_ref, kg_ref, vg_ref, augk_ref, augg_ref, out_ref, lse_ref):
    keys = jnp.concatenate([k_ref[...], kg_ref[...]], 0)
    values_turned = jnp.concatenate([v_ref[...], vg_ref[...]], 0).T
    bias = jnp.concatenate([augk_ref[...], augg_ref[...]], 0)
    both = []
    for head in range(2):
        mine, other = head_lanes(head)
        key_head = keys * mine + bias * other
        query_head = q_ref[...] * mine + lane_one(0) * other
        both.append(nt(key_head, query_head))
    outs, faints = [], []
    for head in range(2):
        values = values_turned[head * HD : (head + 1) * HD, :]
        summed, total, faint = summed_up(both[head], values)
        outs.append(summed / total)
        faints.append(faint)
        lse_ref[0, 0, head : head + 1, :] = jnp.log(total)
    out_ref[...] = jnp.concatenate(outs, 0).T.astype(BF16)

    @pl.when(faints[0] + faints[1] > 0.0)
    def _():
        again = []
        for head in range(2):
            values = values_turned[head * HD : (head + 1) * HD, :]
            summed, lse = summed_faint(both[head], values)
            again.append(summed)
            lse_ref[0, 0, head : head + 1, :] = lse
        out_ref[...] = jnp.concatenate(again, 0).T.astype(BF16)


def local_forward(docs, qkv, qkv_glob, augk, pairs, blocks, first, count, held=(), after=()):
    rows_all = augk.shape[0]
    glob_first = blocks * BLOCK // GLOB

    def block(kind):
        column = pair_column(kind, pairs)
        return (
            qkv,
            pl.BlockSpec((BLOCK, LANES), lambda b, p, docs: (b, column(p + first))),
        )

    def glob_block(kind):
        column = pair_column(kind, pairs)
        return (
            qkv_glob,
            pl.BlockSpec((GLOB, LANES), lambda b, p, docs: (docs[b], column(p + first))),
        )

    work = 2 * count * blocks * BLOCK * (BLOCK + GLOB)
    width = pairs * LANES
    straight = pl.BlockSpec((BLOCK, LANES), lambda b, p, docs: (b, p + first))
    return launch(
        local_forward_body,
        "local_forward",
        (blocks, count),
        [
            block(0),
            block(1),
            block(2),
            glob_block(1),
            glob_block(2),
            (augk, pl.BlockSpec((BLOCK, LANES), lambda b, p, docs: (b, 0))),
            (augk, pl.BlockSpec((GLOB, LANES), lambda b, p, docs: (glob_first, 0))),
        ],
        [
            ((rows_all, width), BF16, straight),
            (
                (blocks, pairs, 2, BLOCK),
                F32,
                pl.BlockSpec((1, 1, 2, BLOCK), lambda b, p, docs: (b, p + first, 0, 0)),
            ),
        ],
        cost(work * 2 * 512, count * rows_all * LANES * 12, work),
        prefetch=(docs,),
        held=held,
        after=after,
    )


def middle_of(out_high, x, own_ref, par_ref, vecs_ref):
    half = own_ref.shape[0]
    branch = nn(out_high[:, :half], own_ref[...]) + nn(out_high[:, half:], par_ref[...])
    middle = x.astype(F32) + branch + vecs_ref[4:5, :]
    xhat, _ = normed(middle)
    hidden = (xhat * vecs_ref[2:3, :] + vecs_ref[3:4, :]).astype(BF16)
    return middle, hidden


def middle_body(out_ref, x_ref, own_ref, par_ref, vecs_ref, mid_ref, hid_ref, turned_ref):
    middle, hidden = middle_of(out_ref[...], x_ref[...], own_ref, par_ref, vecs_ref)
    mid_ref[...] = middle
    hid_ref[...] = hidden
    turned_ref[...] = hidden.T


def middle_local(out_high, x, w_own, w_par, vecs, after=()):
    rows_all, dim = out_high.shape
    rows = x.shape[0]
    row = pl.BlockSpec((TILE, dim), lambda i: (i, 0))
    return launch(
        middle_body,
        "middle_local",
        (rows // TILE,),
        [
            (out_high, row),
            (far(x), row),
            (w_own, full(w_own.shape)),
            (w_par, full(w_par.shape)),
            (vecs, full(vecs.shape)),
        ],
        [
            ((rows_all, dim), F32, row, True),
            ((rows_all, dim), BF16, row),
            ((dim, rows_all), BF16, pl.BlockSpec((dim, TILE), lambda i: (0, i))),
        ],
        cost(2 * rows * dim * dim, 12 * rows * dim + 2 * dim * dim),
        after=after,
    )


def middle_glob_body(
    own_out_ref, par_out_ref, x_ref, own_ref, par_ref, vecs_ref,
    mid_ref, hid_ref, turned_ref, high_ref, lse_ref,
):
    heads = own_out_ref.shape[0]
    parts = [own_out_ref[head, :HD, :] for head in range(heads)]
    parts += [par_out_ref[head, :HD, :] for head in range(heads)]
    turned = jnp.concatenate(parts, 0)
    high = turned.T
    high_ref[...] = high
    stats = [read_stats(own_out_ref, head) for head in range(heads)]
    stats += [read_stats(par_out_ref, head) for head in range(heads)]
    spare = lse_ref.shape[0] - 2 * heads
    lse_ref[...] = jnp.concatenate(stats + [jnp.zeros((spare, x_ref.shape[0]), F32)], 0)
    middle, hidden = middle_of(high, x_ref[...], own_ref, par_ref, vecs_ref)
    mid_ref[...] = middle
    hid_ref[...] = hidden
    turned_ref[...] = hidden.T


def middle_glob(own_out, par_out, x, w_own, w_par, vecs, held):
    rows, dim = x.shape
    first = held[0].shape[0] // rows - 1
    row = pl.BlockSpec((rows, dim), lambda i: (first, 0))
    col = pl.BlockSpec((dim, rows), lambda i: (0, first))
    operands = [own_out, par_out, x, w_own, w_par, vecs]
    specs = [row, row, col, row]
    return launch(
        middle_glob_body,
        "middle_glob",
        (1,),
        [(a, full(a.shape)) for a in operands],
        [(h.shape, h.dtype, spec, *pin) for h, spec, pin in zip(held, specs, ((True,), (), (), ()))]
        + [((HEAD_ROWS, rows), F32, full((HEAD_ROWS, rows)))],
        cost(2 * rows * dim * dim, 12 * rows * dim + 2 * dim * dim),
        held=held,
    )


def ffn_body(
    hid_ref, turned_ref, dz_ref, up_ref, bias_ref, down_ref, mask_ref, *rest, chunks
):
    dn_in_ref = rest[0] if len(rest) == 8 else None
    dnorm_ref, act_ref, grads_ref, bias_grad_ref, act_s, dup_s, sum_s = rest[-7:]
    step = pl.program_id(0)
    rows_all, dim = hid_ref.shape
    chunk = bias_grad_ref.shape[1]
    tail = slice(rows_all - mask_ref.shape[0], rows_all)

    @pl.when(step < chunks)
    def _():
        cols = pl.ds(pl.multiple_of(step * chunk, chunk), chunk)
        up = nn(hid_ref[...], up_ref[:, cols]) + bias_ref[0:1, :]
        share = 0.5 * (1.0 + lax.erf(up * (2.0**-0.5)))
        density = jnp.exp(up * up * -0.5) * 0.3989422804014327
        active = (up * share).astype(BF16)
        slope = share + up * density
        d_up = (nt(dz_ref[...], down_ref[cols, :]) * slope).astype(BF16)
        act_ref[...] = active
        dup_s[:, cols] = d_up
        act_s[...] = active
        sum_s[...] = d_up
        mask = mask_ref[...]
        act_s[tail, :] = (active[tail].astype(F32) * mask).astype(BF16)
        sum_s[tail, :] = (d_up[tail].astype(F32) * mask).astype(BF16)
        bias_grad_ref[...] = jnp.sum(sum_s[...].astype(F32), axis=0, keepdims=True)
        up_grad = nn(turned_ref[...], sum_s[...]).astype(BF16)
        down_grad = tn(act_s[...], dz_ref[...]).astype(BF16)
        place = 0
        for grad in (up_grad, down_grad):
            rows = grad.shape[0]
            for col in range(grad.shape[1] // LANES):
                grads_ref[0, place : place + rows, :] = grad[:, col * LANES : (col + 1) * LANES]
                place += rows

    @pl.when(step >= chunks)
    def _():
        start = pl.multiple_of((step - chunks) * TILE, TILE)
        made = nt(dup_s[pl.ds(start, TILE), :], up_ref[...])
        dnorm_ref[...] = made if dn_in_ref is None else made + dn_in_ref[...]


def ffn_part(hidden, turned, dz, w_up, vec, w_down, mask, first, units, dn_in=None, after=()):
    rows_all, dim = hidden.shape
    half = w_up.shape[1]
    chunk = min(FFN_CHUNK, units)
    chunks = units // chunk
    skip = first // units
    packed = 2 * chunk * dim // LANES
    bias_first = (vec.shape[1] - half + first) // chunk

    def now(j):
        return jnp.minimum(j, chunks - 1)

    row = pl.BlockSpec((TILE, dim), lambda j: (jnp.maximum(j - chunks, 0), 0))
    tail = mask.shape[0] // TILE - 1
    one = pl.Buffered(1)
    operands = [
        (hidden, full(hidden.shape)),
        (turned, full(turned.shape)),
        (dz, full(dz.shape)),
        (w_up, pl.BlockSpec((dim, units), lambda j: (0, skip), pipeline_mode=one)),
        (vec, pl.BlockSpec((vec.shape[0], chunk), lambda j: (0, bias_first + now(j)))),
        (w_down, pl.BlockSpec((units, dim), lambda j: (skip, 0), pipeline_mode=one)),
        (mask, pl.BlockSpec((TILE, 1), lambda j: (tail, 0))),
    ]
    if dn_in is not None:
        operands.append((dn_in, row))
    return launch(
        functools.partial(ffn_body, chunks=chunks),
        "ffn_part",
        (chunks + rows_all // TILE,),
        operands,
        [
            ((rows_all, dim), F32, row),
            ((rows_all, units), BF16, pl.BlockSpec((rows_all, chunk), lambda j: (0, now(j))), True),
            ((chunks, packed, LANES), BF16, pl.BlockSpec((1, packed, LANES), lambda j: (now(j), 0, 0))),
            ((1, units), F32, pl.BlockSpec((1, chunk), lambda j: (0, now(j)))),
        ],
        cost(10 * rows_all * dim * units, rows_all * dim * 14 + units * dim * 8, 2 * rows_all * units),
        after=after,
        scratch=[
            pltpu.VMEM((rows_all, chunk), BF16),
            pltpu.VMEM((rows_all, units), BF16),
            pltpu.VMEM((rows_all, chunk), BF16),
        ],
    )


def output_body(place_ref, mid_ref, vecs_ref, *rest):
    out_ref, glob_ref = rest[-2:]
    parts = len(rest) // 2 - 1
    made = mid_ref[...] + vecs_ref[5:6, :]
    for part in range(parts):
        made = made + nn(rest[part][...], rest[parts + part][...])
    step = pl.program_id(0)
    last = pl.num_programs(0) - 1

    @pl.when(step < last)
    def _():
        out_ref[...] = made.astype(BF16)

    @pl.when(step == last)
    def _():
        glob_ref[...] = made.astype(BF16)


def output_rows(place, middle, vecs, acts, weights, own, after=()):
    rows_all, dim = middle.shape
    tiles = rows_all // TILE
    rows = rows_all - TILE
    row = pl.BlockSpec((TILE, dim), lambda i, place: (i, 0))
    operands = [(far(middle), row), (vecs, full(vecs.shape))]
    operands += [
        (far(act), pl.BlockSpec((TILE, act.shape[1]), lambda i, place: (i, 0))) for act in acts
    ]
    for act, (weight, number) in zip(acts, weights):
        operands.append(
            (
                weight,
                pl.BlockSpec(
                    (act.shape[1], dim),
                    lambda i, place, number=number: (number, 0),
                    pipeline_mode=pl.Buffered(1),
                ),
            )
        )
    units = sum(act.shape[1] for act in acts)
    out, glob = launch(
        output_body,
        "output_rows",
        (tiles,),
        operands,
        [
            ((rows, dim), BF16, pl.BlockSpec((TILE, dim), lambda i, place: (jnp.minimum(i, tiles - 2), 0))),
            ((TILE, dim), BF16, full((TILE, dim))),
        ],
        cost(2 * rows_all * dim * units, rows_all * (units * 2 + dim * 6) + units * dim * 2),
        prefetch=(place,),
        after=after,
    )
    return out, glob


def middle_back_body(
    dn_ref, mid_ref, dz_ref, high_ref, own_ref, par_ref, vecs_ref, mask_ref,
    dmid_ref, dattn_ref, delta_ref, grads_ref, sums_ref, acc_s,
):
    step = pl.program_id(0)
    dim = mid_ref.shape[1]
    half = own_ref.shape[0]
    xhat, inv = normed(mid_ref[...])
    dn = dn_ref[...]
    dz = dz_ref[...].astype(F32)
    d_mid = dz + norm_back(xhat, inv, vecs_ref[2:3, :], dn)
    dmid_ref[...] = d_mid
    d_branch = d_mid.astype(BF16)
    for part, weight in enumerate((own_ref, par_ref)):
        dattn_ref[:, part * half : (part + 1) * half] = nt(d_branch, weight[...]).astype(BF16)
    product = dattn_ref[...].astype(F32) * high_ref[...].astype(F32)
    first = product.astype(BF16)
    second = (product - first.astype(F32)).astype(BF16)
    head = lax.broadcasted_iota(jnp.int32, (delta_ref.shape[0], dim), 0)
    column = lax.broadcasted_iota(jnp.int32, (delta_ref.shape[0], dim), 1)
    picked = jnp.where((column >= head * HD) & (column < (head + 1) * HD), 1.0, 0.0).astype(BF16)
    delta_ref[...] = nt(picked, first) + nt(picked, second)
    mask = mask_ref[...]
    masked = (d_branch.astype(F32) * mask).astype(BF16)
    made = tn(high_ref[...], masked)
    sums = [
        jnp.sum(dn * xhat * mask, axis=0, keepdims=True),
        jnp.sum(dn * mask, axis=0, keepdims=True),
        jnp.sum(masked.astype(F32), axis=0, keepdims=True),
        jnp.sum(dz * mask, axis=0, keepdims=True),
    ]
    sums = jnp.concatenate(sums + [jnp.zeros((4, dim), F32)], 0)

    @pl.when(step == 0)
    def _():
        acc_s[...] = made
        sums_ref[...] = sums

    @pl.when(step > 0)
    def _():
        acc_s[...] += made
        sums_ref[...] += sums

    @pl.when(step == pl.num_programs(0) - 1)
    def _():
        for part in range(2):
            for col in range(dim // LANES):
                grads_ref[part, col * half : (col + 1) * half, :] = acc_s[
                    part * half : (part + 1) * half, col * LANES : (col + 1) * LANES
                ].astype(BF16)


def middle_back(dn, middle, dz, high, w_own, w_par, vecs, mask, after=()):
    rows_all, dim = middle.shape
    row = pl.BlockSpec((TILE, dim), lambda i: (i, 0))
    packed = w_own.size // LANES
    return launch(
        middle_back_body,
        "middle_back",
        (rows_all // TILE,),
        [
            (dn, row),
            (middle, row),
            (dz, row),
            (high, row),
            (w_own, full(w_own.shape)),
            (w_par, full(w_par.shape)),
            (vecs, full(vecs.shape)),
            (mask, pl.BlockSpec((TILE, 1), lambda i: (i, 0))),
        ],
        [
            ((rows_all, dim), F32, row, True),
            ((rows_all, dim), BF16, row),
            ((HEAD_ROWS, rows_all), F32, pl.BlockSpec((HEAD_ROWS, TILE), lambda i: (0, i))),
            ((2, packed, LANES), BF16, full((2, packed, LANES))),
            ((8, dim), F32, full((8, dim))),
        ],
        cost(4 * rows_all * dim * dim, rows_all * dim * 24),
        after=after,
        scratch=[pltpu.VMEM((dim, dim), F32)],
    )


def attention_back_body(
    docs_ref, ql_ref, kl_ref, vl_ref, qg_ref, kg_ref, vg_ref, do_ref, lse_ref, lseg_ref, delta_ref,
    augk_ref, augq_ref, dq_ref, dk_ref, dv_ref, q_ref, key_s, value_s, turned_s, dk_s, dv_s, *, first,
):
    pair = pl.program_id(0) + first
    rows_all = q_ref.shape[0]
    count = augq_ref.shape[0]
    local_rows = rows_all - count
    blocks = local_rows // BLOCK
    q_ref[:local_rows, :] = ql_ref[...]
    q_ref[local_rows:, :] = qg_ref[...]
    turned_s[:, :local_rows] = kl_ref[...].T
    turned_s[:, local_rows:] = kg_ref[...].T
    dk_s[...] = jnp.zeros_like(dk_s)
    dv_s[...] = jnp.zeros_like(dv_s)
    dq_parts = [[] for _ in range(blocks + 1)]
    for head in range(2):
        mine, other = head_lanes(head)
        key_s[:local_rows, :] = kl_ref[...] * mine + augk_ref[:local_rows, :] * other
        key_s[local_rows:, :] = kg_ref[...] * mine + augk_ref[local_rows:, :] * other
        value_s[:local_rows, :] = vl_ref[...] * mine
        value_s[local_rows:, :] = vg_ref[...] * mine
        head_rows = slice(head * HD, (head + 1) * HD)
        index = 2 * pair + head

        def grads(key_cat, value_cat, turned_cat, query_rows, aug, lse):
            queries = q_ref[query_rows, :] * mine
            douts = do_ref[query_rows, :] * mine
            delta = delta_ref[pl.ds(index, 1), query_rows]
            probs = jnp.exp(nt(key_cat, queries + aug * other) - lse)
            d_scores = (probs * (nt(value_cat, douts) - delta)).astype(BF16)
            d_key = nn(d_scores, queries)
            d_value = nn(probs.astype(BF16), douts)
            return nn(turned_cat, d_scores), d_key, d_value

        for block in range(blocks):
            rows = slice(block * BLOCK, (block + 1) * BLOCK)
            start = pl.multiple_of(local_rows + docs_ref[block] * GLOB, GLOB)
            doc_rows = pl.ds(start, GLOB)
            key_cat = jnp.concatenate([key_s[rows, :], key_s[doc_rows, :]], 0)
            value_cat = jnp.concatenate([value_s[rows, :], value_s[doc_rows, :]], 0)
            turned_cat = jnp.concatenate(
                [turned_s[head_rows, rows], turned_s[head_rows, doc_rows]], 1
            )
            d_query, d_key, d_value = grads(
                key_cat, value_cat, turned_cat, rows, lane_one(0), lse_ref[block, 0, head : head + 1, :]
            )
            dq_parts[block].append(d_query)
            dk_s[rows, :] += d_key[:BLOCK]
            dk_s[doc_rows, :] += d_key[BLOCK:]
            dv_s[rows, :] += d_value[:BLOCK]
            dv_s[doc_rows, :] += d_value[BLOCK:]
        rows = slice(local_rows, rows_all)
        d_query, d_key, d_value = grads(
            key_s[...], value_s[...], turned_s[head_rows, :], rows, augq_ref[...],
            lseg_ref[pl.ds(index, 1), :],
        )
        dq_parts[blocks].append(d_query)
        dk_s[...] += d_key
        dv_s[...] += d_value
    for block in range(blocks + 1):
        begin = block * BLOCK
        made = jnp.concatenate(dq_parts[block], 0).T
        dq_ref[begin : begin + made.shape[0], :] = (
            made.astype(BF16).astype(F32) * SCALE
        ).astype(BF16)
    dk_ref[...] = dk_s[...].astype(BF16)
    dv_ref[...] = dv_s[...].astype(BF16)


def attention_back(
    docs, qkv, qkv_glob, d_attn, lse, lse_glob, delta, augk, augq, pairs, first, spot, held=(),
    after=(),
):
    number = 1
    rows_all = augk.shape[0]
    count = augq.shape[0]
    blocks = (rows_all - count) // BLOCK

    def block(array, kind):
        column = pair_column(kind, pairs)
        return (
            array,
            pl.BlockSpec((array.shape[0], LANES), lambda p, docs: (0, column(p + first))),
        )

    straight = pl.BlockSpec((rows_all, LANES), lambda p, docs: (0, p + first))
    work = 2 * number * (blocks * BLOCK * (BLOCK + GLOB) + rows_all * count)
    return launch(
        functools.partial(attention_back_body, first=first),
        "attention_back",
        (number,),
        [
            block(qkv, 0),
            block(qkv, 1),
            block(qkv, 2),
            block(qkv_glob, 0),
            block(qkv_glob, 1),
            block(qkv_glob, 2),
            (d_attn, straight),
            (lse, pl.BlockSpec((blocks, 1, 2, BLOCK), lambda p, docs: (0, p + first, 0, 0))),
            (lse_glob, full(lse_glob.shape)),
            (delta, full(delta.shape)),
            (augk, full(augk.shape)),
            (augq, full(augq.shape)),
        ],
        [((rows_all, pairs * LANES), BF16, pl.BlockSpec((rows_all, LANES), lambda p, docs: (0, spot)))] * 3,
        cost(work * 5 * 512, number * rows_all * LANES * 14, work),
        prefetch=(docs,),
        held=held,
        after=after,
        scratch=[
            pltpu.VMEM((rows_all, LANES), BF16),
            pltpu.VMEM((rows_all, LANES), BF16),
            pltpu.VMEM((rows_all, LANES), BF16),
            pltpu.VMEM((LANES, rows_all), BF16),
            pltpu.VMEM((rows_all, LANES), F32),
            pltpu.VMEM((rows_all, LANES), F32),
        ],
    )


def project_grad_body(
    turned_ref, turned_glob_ref, dq_ref, dk_ref, dv_ref, weight_ref, vecs_ref, *rest, first, last, shared
):
    dim, local_rows = turned_ref.shape
    width = dq_ref.shape[1]
    third = weight_ref.shape[1] // 3
    cols = width // LANES
    cut = dim // 2
    count = 3 * cols
    if last:
        carry_ref, mid_ref, *up_refs, grads_ref = rest
    else:
        grads_ref, next_ref = rest
    ones = jnp.ones((8, width), BF16)
    sums, dots, shifts = [], None, None
    for kind, ref in enumerate((dq_ref, dk_ref, dv_ref)):
        made = nn(turned_ref[...], ref[:local_rows, :]) + nn(turned_glob_ref[...], ref[local_rows:, :])
        begin = kind * third + first
        weight = weight_ref[:, begin : begin + width]
        total = jnp.sum(ref[...].astype(F32), axis=0, keepdims=True)
        sums.append(total)
        scaled = made * weight.astype(F32)
        high = scaled.astype(BF16)
        low = (scaled - high.astype(F32)).astype(BF16)
        dot = nt(ones, high) + nt(ones, low)
        high = total.astype(BF16).astype(F32)
        low = (total - high).astype(BF16).astype(F32)
        parts = jnp.concatenate([high, low, jnp.zeros((6, width), F32)], 0)
        shift = jnp.sum(nt(parts.astype(BF16), weight), axis=0, keepdims=True)
        dots = dot if dots is None else dots + dot
        shifts = shift if shifts is None else shifts + shift
        rounded = made.astype(BF16)
        for col in range(cols):
            for part in range(2):
                number = 2 * (kind * cols + col) + part
                spot = number % count * cut
                grads_ref[number // count, spot : spot + cut, :] = rounded[
                    part * cut : (part + 1) * cut, col * LANES : (col + 1) * LANES
                ]
    if not last:
        row = jnp.concatenate([sums[0], sums[2], jnp.zeros((1, dim - 2 * width), F32)], 1)
        next_ref[...] = jnp.concatenate([dots[0:1, :], shifts, row, jnp.zeros((5, dim), F32)], 0)
        return
    dots = dots[0:1, :] + carry_ref[0:1, :]
    shifts = shifts + carry_ref[1:2, :]
    gains = (dots - vecs_ref[1:2, :] * shifts) / vecs_ref[0:1, :]
    small = [mid_ref[row : row + 1, :] * shared for row in range(4)]
    small += [gains, shifts]
    for number, total in enumerate((sums[0], sums[2])):
        small += [carry_ref[2:3, number * first : (number + 1) * first], total]
    small += [ref[...] for ref in up_refs]
    pieces = []
    for row in small:
        pieces += [row[:, col * LANES : (col + 1) * LANES] for col in range(row.shape[1] // LANES)]
    pieces.append(jnp.zeros((LANES - len(pieces), LANES), F32))
    grads_ref[0, count * cut :, :] = jnp.concatenate(pieces, 0).astype(BF16)
    grads_ref[1, count * cut :, :] = jnp.zeros((LANES, LANES), BF16)


def project_grad(
    turned, turned_glob, dq, dk, dv, weight, vecs, half, first, width, spot, carry=None, mid_sums=None,
    up_sums=(), after=(),
):
    dim = turned.shape[0]
    rows_all = dq.shape[0]
    last = carry is not None
    grads = pl.BlockSpec((rows_all, width), lambda i: (0, spot))
    shape = (2, 3 * width // LANES * dim // 2 + (LANES if last else 0), LANES)
    more = [carry, mid_sums, *up_sums] if last else []
    return launch(
        functools.partial(project_grad_body, first=first, last=last, shared=1.0 - half),
        "project_grad",
        (1,),
        [
            (turned, full(turned.shape)),
            (turned_glob, full(turned_glob.shape)),
            (dq, grads),
            (dk, grads),
            (dv, grads),
            (weight, pl.BlockSpec((None, *weight.shape[1:]), lambda i: (half, 0, 0))),
            (vecs, full(vecs.shape)),
        ]
        + [(array, full(array.shape)) for array in more],
        [(shape, BF16, full(shape))] + ([] if last else [((8, dim), F32, full((8, dim)))]),
        cost(6 * rows_all * dim * width, rows_all * (dim + 3 * width) * 2),
        after=after,
    )


def hidden_back(dq_ref, dk_ref, dv_ref, both_ref, places):
    d_hidden = None
    for part, spots in enumerate(places):
        joined = jnp.concatenate(
            [ref[:, s * LANES : (s + 1) * LANES] for ref in (dq_ref, dk_ref, dv_ref) for s in spots], 1
        )
        made = nt(joined, both_ref[part])
        d_hidden = made if d_hidden is None else d_hidden + made
    return d_hidden


def input_back_body(
    dq_ref, dk_ref, dv_ref, both_ref, x_ref, dmid_ref, vecs_ref, tokens_ref, *, places
):
    d_hidden = hidden_back(dq_ref, dk_ref, dv_ref, both_ref, places)
    xhat, inv = normed(x_ref[...].astype(F32))
    tokens_ref[...] = dmid_ref[...] + norm_back(xhat, inv, vecs_ref[0:1, :], d_hidden)


def input_back(dq, dk, dv, both, x, d_mid, vecs, places, after=()):
    rows, dim = x.shape
    row = pl.BlockSpec((TILE, dim), lambda i: (i, 0))
    return launch(
        functools.partial(input_back_body, places=places),
        "input_back",
        (rows // TILE,),
        [
            (dq, row),
            (dk, row),
            (dv, row),
            (both, full(both.shape)),
            (x, row),
            (d_mid, row),
            (vecs, full(vecs.shape)),
        ],
        [(x.shape, F32, row, True)],
        cost(6 * rows * dim * dim, rows * dim * 16 + 6 * dim * dim),
        after=after,
    )[0]


def glob_back_body(dq_ref, dk_ref, dv_ref, both_ref, out_ref, *, places):
    out_ref[...] = hidden_back(dq_ref, dk_ref, dv_ref, both_ref, places).astype(BF16)


def glob_back(dq, dk, dv, both, places, after=()):
    rows_all, dim = dq.shape
    last = rows_all // TILE - 1
    row = pl.BlockSpec((TILE, dim), lambda i: (last, 0))
    return launch(
        functools.partial(glob_back_body, places=places),
        "glob_back",
        (1,),
        [(dq, row), (dk, row), (dv, row), (both, full(both.shape))],
        [((TILE, dim), BF16, full((TILE, dim)))],
        cost(6 * TILE * dim * dim, TILE * dim * 16 + 6 * dim * dim),
        after=after,
    )[0]


def glob_input_body(kept_ref, got_ref, x_ref, dmid_ref, vecs_ref, out_ref):
    d_hidden = kept_ref[...].astype(F32) + got_ref[...].astype(F32)
    xhat, inv = normed(x_ref[...].astype(F32))
    out_ref[...] = dmid_ref[...] + norm_back(xhat, inv, vecs_ref[0:1, :], d_hidden)


def glob_input(place, kept, got, x, d_mid, vecs, after=()):
    own, dim = x.shape
    first = (d_mid.shape[0] - 2 * GLOB) // own
    spec = pl.BlockSpec((own, dim), lambda i, place: (0, 0))
    here = pl.BlockSpec((own, dim), lambda i, place: (first + place[2] // own, 0))

    def body(place_ref, *refs):
        glob_input_body(*refs)

    return launch(
        body,
        "glob_input",
        (1,),
        [(kept, spec), (got, spec), (x, spec), (d_mid, here), (vecs, full(vecs.shape))],
        [((own, dim), F32, spec, True)],
        cost(0, own * dim * 14),
        prefetch=(place,),
        after=after,
    )[0]


def pair_add(left, right):
    return (left.astype(F32) + right.astype(F32)).astype(BF16)


def turn_body(place_ref, *refs, actions):
    count = sum(len(action[2]) for action in actions)
    ins, outs = list(refs[:count]), list(refs[count:])
    for kind, number, arrays in actions:
        mine = [ins.pop(0) for _ in arrays]
        side = None if number is None else place_ref[number]
        if kind == "start":
            go_ref, stay_ref = outs.pop(0), outs.pop(0)
            first = 0
            for own_ref, got_ref in zip(mine[::2], mine[1::2]):
                rows = slice(first, first + own_ref.shape[1])
                go_ref[rows, :] = pair_add(own_ref[1 - side], got_ref[1 - side])
                stay_ref[rows, :] = pair_add(own_ref[side], got_ref[side])
                first = rows.stop
        elif kind == "pick":
            go_ref, stay_ref = outs.pop(0), outs.pop(0)
            go_ref[...] = mine[0][1 - side]
            stay_ref[...] = mine[0][side]
        elif kind == "split":
            go_ref, stay_ref = outs.pop(0), outs.pop(0)
            go_ref[...] = pair_add(mine[0][1 - side], mine[1][1 - side])
            stay_ref[...] = pair_add(mine[0][side], mine[1][side])
        elif kind == "add":
            outs.pop(0)[...] = pair_add(mine[0][...], mine[1][...])
        elif kind == "join":
            out_ref = outs.pop(0)
            out_ref[side] = mine[0][...]
            out_ref[1 - side] = mine[1][...]
        else:
            outs.pop(0)[...] = mine[0][...]


def halved(array):
    return array.reshape(2, -1, array.shape[-1])


class Chain:
    def __init__(self, steps, sends, first):
        self.steps, self.sends, self.first, self.at = steps, sends, first, 0

    def action(self):
        kind, number = self.steps[self.at]
        if kind in ("start", "pick", "copy"):
            return kind, number, self.first
        arrays = [self.stay, self.other]
        return kind, number, [halved(a) for a in arrays] if kind == "split" else arrays

    def shapes(self):
        kind, _, arrays = self.action()
        lanes = arrays[0].shape[-1]
        if kind == "start":
            return [(sum(own.shape[1] for own in arrays[::2]), lanes)] * 2
        if kind in ("pick", "split"):
            return [arrays[0].shape[1:]] * 2
        if kind == "join":
            return [(2, *arrays[0].shape)]
        return [arrays[0].shape]

    def take(self, outs):
        kind, _ = self.steps[self.at]
        self.stay = outs[-1].reshape(-1, outs[-1].shape[-1]) if kind == "join" else outs[-1]
        self.other = self.sends[self.at](outs[0] if len(outs) > 1 else self.stay)
        self.at += 1

    @property
    def left(self):
        return len(self.steps) - self.at


def turn(place, chains, after=()):
    actions = [chain.action() for chain in chains]
    shapes = [chain.shapes() for chain in chains]
    flat = [shape for group in shapes for shape in group]
    arrays = [array for _, _, group in actions for array in group]
    outs = launch(
        functools.partial(turn_body, actions=[(k, n, [None] * len(a)) for k, n, a in actions]),
        "turn",
        (1,),
        [(a, full(a.shape)) for a in arrays],
        [(shape, BF16, full(shape)) for shape in flat],
        cost(0, sum(a.size for a in arrays) * 4),
        prefetch=(place,),
        after=after,
    )
    outs = list(outs)
    mark = outs[-1]
    for chain, group in zip(chains, shapes):
        chain.take([outs.pop(0) for _ in group])
    return [mark]


def by_side(place_ref, number, mine_ref, other_ref, write):
    for half in range(2):
        for ref, here in ((mine_ref, place_ref[number] == half), (other_ref, place_ref[number] != half)):

            @pl.when(here)
            def _(ref=ref, half=half):
                write(ref, half)


def ffn_unpack_body(place_ref, mine_ref, other_ref, up_ref, down_ref, *, number, chunk):
    dim = up_ref.shape[0]
    units = up_ref.shape[1]

    def write(ref, half):
        count = units * dim // LANES
        first = half * count
        spot = 0
        for step in range(units // chunk):
            for col in range(chunk // LANES):
                if first <= spot < first + count:
                    begin = step * chunk + col * LANES
                    up_ref[:, begin : begin + LANES] = ref[spot - first : spot - first + dim, :].astype(F32)
                spot += dim
            for col in range(dim // LANES):
                if first <= spot < first + count:
                    down_ref[step * chunk : (step + 1) * chunk, col * LANES : (col + 1) * LANES] = ref[
                        spot - first : spot - first + chunk, :
                    ].astype(F32)
                spot += chunk

    by_side(place_ref, number, mine_ref, other_ref, write)


def ffn_unpack(place, number, mine, other, dim, half, units, part, held=(), after=()):
    spec = full(mine.shape)
    one = pl.Buffered(1)
    return launch(
        functools.partial(ffn_unpack_body, number=number, chunk=min(FFN_CHUNK, units)),
        "ffn_unpack",
        (1,),
        [(mine, spec), (other, spec)],
        [
            ((dim, half), F32, pl.BlockSpec((dim, units), lambda i, place: (0, part), pipeline_mode=one), True),
            ((half, dim), F32, pl.BlockSpec((units, dim), lambda i, place: (part, 0), pipeline_mode=one), True),
        ],
        cost(0, mine.size * 12),
        prefetch=(place,),
        held=held,
        after=after,
    )


def tail_unpack_body(place_ref, mine_ref, other_ref, q_ref, k_ref, v_ref, more_ref, *, number, last):
    dim, width = q_ref.shape
    cols = width // LANES
    cut = dim // 2
    count = 3 * cols

    def write(ref, half):
        for spot in range(count):
            unit, part = divmod(half * count + spot, 2)
            kind, col = unit // cols, unit % cols
            (q_ref, k_ref, v_ref)[kind][
                part * cut : (part + 1) * cut, col * LANES : (col + 1) * LANES
            ] = ref[spot * cut : (spot + 1) * cut, :].astype(F32)
        spot = count * cut
        if last:
            if half == 0:
                more_ref[...] = ref[spot : spot + LANES, :].astype(F32)
            return
        rows, wide = more_ref.shape[0], more_ref.shape[1] // LANES // 2
        for col in range(wide):
            begin = (half * wide + col) * LANES
            more_ref[:, begin : begin + LANES] = ref[spot : spot + rows, :].astype(F32)
            spot += rows

    by_side(place_ref, number, mine_ref, other_ref, write)


def tail_unpack(place, number, mine, other, dim, half, first, width, held=()):
    spec = full(mine.shape)
    last = bool(held)
    block = pl.BlockSpec((dim, width), lambda i, place: (0, first // width), pipeline_mode=pl.Buffered(1))
    more = (LANES, LANES) if last else (half, dim)
    return launch(
        functools.partial(tail_unpack_body, number=number, last=last),
        "tail_unpack",
        (1,),
        [(mine, spec), (other, spec)],
        [((dim, half), F32, block, True)] * 3 + [(more, F32, full(more))],
        cost(0, mine.size * 12),
        prefetch=(place,),
        held=held,
    )


def finish_body(mine_ref, theirs_ref, *outs):
    rows = 0
    for number, out_ref in enumerate(outs):
        count = out_ref.shape[0] // LANES
        pieces = []
        for row in range(rows, rows + count):
            piece = mine_ref[row : row + 1, :]
            pieces.append(piece + theirs_ref[row : row + 1, :] if number < 6 else piece)
        out_ref[...] = jnp.concatenate(pieces, 1).reshape(-1)
        rows += count


def finish(mine, theirs, sizes):
    return launch(
        finish_body,
        "finish",
        (1,),
        [(mine, full(mine.shape)), (theirs, full(theirs.shape))],
        [((size,), F32, full((size,))) for size in sizes],
        cost(0, 4 * sum(sizes)),
    )


def per_device(
    tokens, glob_tokens, w_query, b_query, w_key, w_value, b_value, w_out, b_out, w_up, b_up,
    w_down, b_down, gain_attn, shift_attn, gain_ffn, shift_ffn, doc_blocks, doc_tail,
    grad_tokens, grad_glob,
):
    seq_size = lax.axis_size("seq")
    seq_pos = lax.axis_index("seq")
    tp_pos = lax.axis_index("tp")
    rows, dim = tokens.shape
    own_glob = glob_tokens.shape[0]
    half = w_query.shape[1]
    units = w_up.shape[1]
    pairs = 2 * half // PAIR
    blocks = rows // BLOCK
    glob_rows = 2 * GLOB
    rows_all = rows + glob_rows
    group_size = GROUP_BLOCKS // (2 * blocks)
    group_bits = group_size.bit_length() - 1
    seq_bits = seq_size.bit_length() - 1
    group_pos = seq_pos % group_size
    own_first = (group_pos * 2 + tp_pos) * own_glob

    def flip(value, bit):
        return lax.ppermute(value, "seq", [(s, s ^ (1 << bit)) for s in range(seq_size)])

    def swap(value):
        return lax.ppermute(value, "tp", [(0, 1), (1, 0)])

    rest = tuple(range(3, seq_bits))
    orders = {
        "one": ((0, 1, 2, *rest), (2, 0, 1, *rest)),
        "two": ((1, 0, 2, *rest), (0, 2, 1, *rest)),
        "three": ((0, 1, 2, *rest), (2, 0, 1, *rest)),
        "four": ((1, 0, 2, *rest), (0, 2, 1, *rest)),
    }
    place = [
        (seq_pos * 2 + tp_pos) * blocks,
        (seq_pos // group_size) * 2,
        own_first,
        jnp.int32(own_glob),
        group_pos,
        tp_pos,
    ]
    group_sides = len(place)
    place += [(seq_pos >> bit) & 1 for bit in range(group_bits)] + [tp_pos]
    job_sides = {}
    for name, (zero, one) in orders.items():
        job_sides[name] = len(place)
        place += [(seq_pos >> jnp.where(tp_pos == 0, a, b)) & 1 for a, b in zip(zero, one)]
    place = jnp.stack(place).astype(jnp.int32)

    def trade(value, name, step):
        zero, one = orders[name][0][step], orders[name][1][step]
        links = [(2 * s, 2 * (s ^ (1 << zero))) for s in range(seq_size)]
        links += [(2 * s + 1, 2 * (s ^ (1 << one)) + 1) for s in range(seq_size)]
        return lax.ppermute(value, ("seq", "tp"), links)

    gathered = jnp.stack([glob_tokens, grad_glob])[None]
    vecs, half_own = pack_vectors(
        [gain_attn, shift_attn, gain_ffn, shift_ffn, b_out, b_down], [b_query, b_value, b_up]
    )
    half_par = swap(half_own)
    halves = (half_own, half_par)
    weights = [w_query, w_key, w_value]
    weights += [swap(weight) for weight in weights]
    marks = ()
    for bit in range(group_bits):
        other = flip(gathered, bit)
        if bit == 1:
            qkv, turned, qkv_both = project(tokens, vecs, halves, weights, (gathered,))
            marks = (turned,)
        if bit == group_bits - 1:
            docs, augk, augq, mask, seen = layout(
                place, doc_blocks, doc_tail, rows_all, glob_rows, blocks, (gathered,)
            )
            marks = (augq,)
        gathered = stack_two(gathered, other, marks)
    x_glob, dz_all = order_rows(place, gathered, swap(gathered), grad_tokens)
    qkv_glob, turned_glob = project(x_glob, vecs, halves, [qkv_both])
    out_par = swap(w_out)
    up_par = swap(w_up)
    down_par = swap(w_down)

    mine, theirs = glob_forward(qkv, qkv_glob, augk, augq, seen, pairs)
    state = merge(mine, swap(theirs))
    outs = ()
    for bit in range(group_bits):
        other = flip(state, bit)
        first, end = pairs * bit // group_bits, pairs * (bit + 1) // group_bits
        outs = local_forward(
            docs, qkv, qkv_glob, augk, pairs, blocks, first, end - first, outs, (state,)
        )
        state = merge(state, other, (outs[1],))
    state_par = swap(state)
    high, lse = outs
    held = middle_local(high, tokens, w_out, out_par, vecs, (state,))
    middle, hidden, ffn_turned, high, lse_glob = middle_glob(
        state, state_par, x_glob, w_out, out_par, vecs, [*held, high]
    )

    def job(name, pairs):
        first, count = job_sides[name], seq_bits
        steps = [("start", first)]
        steps += [("split", first + step) for step in range(1, count)]
        steps += [("add", None)]
        steps += [("join", first + step) for step in range(count - 1, 0, -1)]
        order = [*range(count), *range(count - 1, -1, -1)]
        sends = [lambda value, step=step: trade(value, name, step) for step in order]
        return Chain(steps, sends, [array for pair in pairs for array in pair])

    def apart(value):
        return value

    part = units // 2
    acts, ups, grads = [], [[], []], []
    dn = None
    marks = []
    for which, (up, down, vec) in ((1, (up_par, down_par, half_par)), (0, (w_up, w_down, half_own))):
        for number in range(2):
            dn, act, grad, up_sum = ffn_part(
                hidden, ffn_turned, dz_all, up, vec, down, mask, number * part, part, dn, marks
            )
            grad = grad.reshape(2, -1, LANES)
            acts.append((act, down, number))
            ups[which].append(up_sum)
            grads.append(swap(grad) if which else grad)
            if not which and not number:
                one = job("one", [(grads[2], grads[0])])
                marks = turn(place, [one], (up_sum,))
    two = job("two", [(grads[3], grads[1])])
    marks = turn(place, [one, two], (up_sum,))

    d_mid, d_attn, delta, out_grad, mid_sums = middle_back(
        dn, middle, dz_all, high, w_out, out_par, vecs, mask, marks
    )
    out_grad = out_grad.reshape(2, 2, -1, LANES)
    out_got = Chain([("copy", None)], [swap], [out_grad[1]])
    marks = turn(place, [one, out_got], (mid_sums,))
    own = pairs // 2
    some = 2 * LANES
    spots = {0: 0, 1: 1, own: 2, own + 1: 3, 2: 4, own + 2: 5}
    places = ((0, 1, 4), (2, 3, 5))
    plan = (
        (0, (one, two)), (own, (one, two)), (1, (one, two)), (own + 1, (one, two)), (2, (two,)),
        (own + 2, (two,)),
    )
    grads = ()
    for number, (pair, chains) in enumerate(plan):
        if number == 4:
            carries = []
            for which in (1, 0):
                grad, carry = project_grad(
                    turned, turned_glob, *grads, qkv_both, vecs, which, 0, some, which, after=marks
                )
                carries.append(carry)
                if which:
                    got = swap(grad)
                    marks = [carry]
            three = job("three", [(grad, got), (out_grad[0], out_got.other)])
            marks = turn(place, [one, two, three], (carry,))
        grads = attention_back(
            docs, qkv, qkv_glob, d_attn, lse, lse_glob, delta, augk, augq, pairs, pair, spots[pair],
            grads, marks,
        )
        if pair == own + 2:
            chains = (*chains, three)
        marks = turn(place, chains, (grads[0],))
    for which in (1, 0):
        grad = project_grad(
            turned, turned_glob, *grads, qkv_both, vecs, which, some, LANES, 4 + which,
            carries[1 - which], mid_sums, ups[which], marks,
        )[0]
        if which:
            got = swap(grad)
            marks = turn(place, [three], (grad,))
    four = job("four", [(grad, got)])
    marks = turn(place, [three, four])

    back = glob_back(*grads, qkv_both, places, marks)
    sends = [lambda value, bit=bit: flip(value, bit) for bit in reversed(range(group_bits))] + [swap]
    numbers = [*reversed(range(group_sides, group_sides + group_bits)), group_sides + group_bits]
    steps = [("pick", numbers[0])] + [("split", number) for number in numbers[1:]]
    globs = Chain(steps, sends, [halved(back)])
    marks = turn(place, [four, three, globs])
    tokens_grad = input_back(*grads, qkv_both, tokens, d_mid, vecs, places, marks)
    marks = turn(place, [four, three, globs], (far(tokens_grad),))
    kinds = ()
    for number, chain in enumerate((one, two)):
        while chain.left:
            marks = turn(place, [chain], marks)
        name = ("one", "two")[number]
        kinds = ffn_unpack(
            place, job_sides[name], chain.stay, chain.other, dim, units, part, number, kinds, marks
        )
        marks = turn(place, [c for c in (four, three, globs) if c.left], (far(kinds[0]),))
    up_grad, down_grad = kinds
    marks = turn(place, [c for c in (four, three) if c.left], marks)
    glob_grad = glob_input(place, globs.stay, globs.other, glob_tokens, d_mid, vecs, marks)
    marks = turn(place, [c for c in (four, three) if c.left], (far(glob_grad),))
    while four.left or three.left:
        marks = turn(place, [c for c in (four, three) if c.left], marks)
    out_tokens, out_all = output_rows(
        place, middle, vecs, [a for a, _, _ in acts], [(w, n) for _, w, n in acts], own_glob, marks
    )
    out_glob = lax.dynamic_slice_in_dim(out_all, own_first, own_glob, 0)
    *kinds, w_out_grad = tail_unpack(
        place, job_sides["three"], three.stay, three.other, dim, half, 0, some
    )
    q_grad, k_grad, v_grad, small = tail_unpack(
        place, job_sides["four"], four.stay, four.other, dim, half, some, LANES, kinds
    )
    (
        gain_f_grad, shift_f_grad, out_bias, down_bias, gain_a_grad, shift_a_grad, b_query_grad,
        b_value_grad, b_up_grad,
    ) = finish(small, swap(small), [dim] * 6 + [half, half, units])
    return (
        out_tokens, out_glob, tokens_grad, glob_grad, q_grad, b_query_grad, k_grad,
        v_grad, b_value_grad, w_out_grad, out_bias, up_grad, b_up_grad, down_grad, down_bias,
        gain_a_grad, shift_a_grad, gain_f_grad, shift_f_grad,
    )


def solution(mesh):
    rows = P(("seq", "tp"), None)
    cols, part, whole = P(None, "tp"), P("tp"), P()
    lines = P("tp", None)
    return jax.shard_map(
        per_device,
        mesh=mesh,
        in_specs=(
            rows, rows, cols, part, cols, cols, part, lines, whole, cols, part, lines, whole,
            whole, whole, whole, whole, whole, whole, rows, rows,
        ),
        out_specs=(
            rows, rows, rows, rows, cols, part, cols, cols, part, lines, whole, cols, part, lines,
            whole, whole, whole, whole, whole,
        ),
        check_vma=False,
    )
```

```python
import functools

import jax
import jax.numpy as jnp
from jax import lax
from jax.experimental import pallas as pl
from jax.experimental.pallas import tpu as pltpu
from jax.sharding import PartitionSpec as P

HD = 64
BLOCK = 512
GLOB = 128
GROUP_BLOCKS = 32
EPS = 1e-05
SCALE = 0.125
NEG = -1e30
SHIFT = -10.0
FAINT = 1e-25
TILE = 256
PAIR = 2 * HD
LANES = 128
STATS = 16
HEAD_ROWS = 16
FFN_CHUNK = 256
WEIGHT = 1
F32 = jnp.float32
BF16 = jnp.bfloat16
VMEM_BYTES = 12 * 2**20


def nn(left, right):
    return jnp.dot(left, right, preferred_element_type=F32)


def nt(left, right):
    return lax.dot_general(left, right, (((1,), (1,)), ((), ())), preferred_element_type=F32)


def tn(left, right):
    return lax.dot_general(left, right, (((0,), (0,)), ((), ())), preferred_element_type=F32)


def normed(values):
    row_mean = jnp.mean(values, axis=-1, keepdims=True)
    centred = values - row_mean
    row_var = jnp.mean(centred * centred, axis=-1, keepdims=True)
    inv = lax.rsqrt(row_var + EPS)
    return centred * inv, inv


def norm_back(xhat, inv, gain_vec, cotangent):
    scaled = cotangent * gain_vec
    mean_one = jnp.mean(scaled, axis=-1, keepdims=True)
    mean_two = jnp.mean(scaled * xhat, axis=-1, keepdims=True)
    return inv * (scaled - mean_one - xhat * mean_two)


def full(shape):
    zeros = (0,) * len(shape)
    return pl.BlockSpec(shape, lambda *_: zeros, pipeline_mode=pl.Buffered(1))


ANY = pl.BlockSpec(memory_space=pl.ANY)


def far(array):
    return pltpu.with_memory_space_constraint(array, pltpu.HBM)


def launch(
    body, name, grid, operands, outs, work, prefetch=(), held=(), after=(), scratch=(), aliased=0
):
    arrays = [*prefetch, *(a for a, _ in operands), *held, *after]
    specs = [*(spec for _, spec in operands), *([ANY] * (len(held) + len(after)))]
    first = len(prefetch) + len(operands)
    spare = len(held) + len(after)

    def whole(*refs):
        return body(*refs[:first], *refs[first + spare :])

    return pl.pallas_call(
        whole,
        grid_spec=pltpu.PrefetchScalarGridSpec(
            num_scalar_prefetch=len(prefetch),
            grid=grid,
            in_specs=specs,
            out_specs=[out[2] for out in outs],
            scratch_shapes=list(scratch),
        ),
        out_shape=[(pltpu.HBM if out[3:] else jax.ShapeDtypeStruct)(out[0], out[1]) for out in outs],
        input_output_aliases={first + i: aliased + i for i in range(len(held))},
        compiler_params=pltpu.CompilerParams(
            vmem_limit_bytes=VMEM_BYTES, dimension_semantics=("arbitrary",) * len(grid)
        ),
        cost_estimate=work,
        name=name,
    )(*arrays)


def cost(flops, nbytes, trans=0):
    scale = WEIGHT if flops > 2**28 else 1
    return pl.CostEstimate(
        flops=int(scale * flops), bytes_accessed=int(scale * nbytes), transcendentals=int(trans)
    )


def head_lanes(head):
    lane = lax.broadcasted_iota(jnp.int32, (1, LANES), 1)
    here = jnp.where(lane < HD, 1.0, 0.0)
    mine = here if head == 0 else 1.0 - here
    return mine.astype(BF16), (1.0 - mine).astype(BF16)


def lane_one(slot):
    lane = lax.broadcasted_iota(jnp.int32, (1, LANES), 1)
    return jnp.where((lane == slot) | (lane == slot + HD), 1.0, 0.0).astype(BF16)


def layout_body(
    place_ref, blocks_ref, tails_ref, docs_ref, augk_ref, augq_ref, mask_ref, seen_ref
):
    first_block, group_first, own_first = place_ref[0], place_ref[1], place_ref[2]
    own_count = place_ref[3]
    count = augq_ref.shape[0]
    rows = augk_ref.shape[0] - count
    lane = lax.broadcasted_iota(jnp.int32, (1, LANES), 1)
    slot = jnp.where(lane < HD, lane, lane - HD)
    column = lax.broadcasted_iota(jnp.int32, (8, count), 1)
    seen = (column >= own_first) & (column < own_first + own_count)
    for block in range(rows // BLOCK):
        index = first_block + block
        start, doc, real = jnp.int32(0), jnp.int32(0), jnp.int32(BLOCK)
        for number in range(blocks_ref.shape[0]):
            end = start + blocks_ref[number]
            inside = jnp.logical_and(index >= start, index < end)
            doc = jnp.where(inside, number, doc)
            real = jnp.where(
                jnp.logical_and(inside, index == end - 1), tails_ref[number], real
            )
            start = end
        doc = doc - group_first
        docs_ref[block] = doc
        seen = seen | ((column >= doc * GLOB) & (column < (doc + 1) * GLOB))
        row = lax.broadcasted_iota(jnp.int32, (BLOCK, 1), 0)
        padded = row >= real
        shut = ((slot == 1) & (doc != 0)) | ((slot == 2) & (doc != 1))
        shut = jnp.where(shut, 1, 0) + jnp.where(padded & (slot < 3), 1, 0)
        augk_ref[block * BLOCK : (block + 1) * BLOCK, :] = jnp.where(
            shut > 0, NEG, jnp.where(slot < 3, SHIFT, 0.0)
        ).astype(BF16)
    row = lax.broadcasted_iota(jnp.int32, (count, 1), 0)
    late = row >= GLOB
    shut = ((slot == 1) & late) | ((slot == 2) & ~late) | (slot == 3)
    augk_ref[rows:, :] = jnp.where(shut, NEG, jnp.where(slot < 3, SHIFT, 0.0)).astype(BF16)
    owned = (row >= own_first) & (row < own_first + own_count)
    on = ((slot == 1) & ~late) | ((slot == 2) & late) | ((slot == 3) & ~owned)
    augq_ref[...] = jnp.where(on, 1.0, 0.0).astype(BF16)
    seen_ref[...] = jnp.where(seen, 1.0, 0.0)
    mask_ref[:rows, :] = jnp.ones((rows, 1), F32)
    mask_ref[rows:, :] = jnp.where(owned, 1.0, 0.0)


def layout(place, doc_blocks, doc_tail, rows_all, count, blocks, after=()):
    smem = pl.BlockSpec(memory_space=pltpu.SMEM)
    return launch(
        layout_body,
        "layout",
        (1,),
        [],
        [
            ((blocks,), jnp.int32, smem),
            ((rows_all, LANES), BF16, full((rows_all, LANES))),
            ((count, LANES), BF16, full((count, LANES))),
            ((rows_all, 1), F32, full((rows_all, 1))),
            ((8, count), F32, full((8, count))),
        ],
        cost(0, rows_all * LANES * 4),
        prefetch=(place, doc_blocks, doc_tail),
        after=after,
    )


def pack_body(*refs):
    vecs_ref, half_ref = refs[-2:]
    for row, ref in enumerate(refs[:6]):
        vecs_ref[row : row + 1, :] = ref[...].reshape(1, -1)
    vecs_ref[6:, :] = jnp.zeros((2, vecs_ref.shape[1]), F32)
    half_ref[...] = jnp.zeros(half_ref.shape, F32)
    first = 0
    for ref in refs[6:9]:
        count = ref.shape[0]
        half_ref[0:1, first : first + count] = ref[...].reshape(1, -1)
        first += count


def pack_vectors(vectors, parts):
    arrays = [far(array) for array in (*vectors, *parts)]
    dim = vectors[0].shape[0]
    width = sum(part.shape[0] for part in parts)
    return launch(
        pack_body,
        "pack_vectors",
        (1,),
        [(a, full(a.shape)) for a in arrays],
        [((8, dim), F32, full((8, dim))), ((8, width), F32, full((8, width)))],
        cost(0, 32 * (dim + width)),
    )


def order_body(place_ref, mine_ref, theirs_ref, grads_ref, x_ref, dz_ref):
    step = pl.program_id(0)
    last = pl.num_programs(0) - 1
    chips, _, own, _ = mine_ref.shape

    @pl.when(step < last)
    def _():
        dz_ref[...] = grads_ref[...]

    @pl.when(step == last)
    def _():
        for chip in range(chips):
            for side, ref in enumerate((mine_ref, theirs_ref)):
                spot = (place_ref[4] ^ chip) * 2 + (place_ref[5] ^ side)
                here = pl.ds(pl.multiple_of(spot * own, own), own)
                x_ref[here, :] = ref[chip, 0]
                dz_ref[here, :] = ref[chip, 1]


def order_rows(place, mine, theirs, grads, after=()):
    chips, _, own, dim = mine.shape
    count = chips * 2 * own
    tiles = grads.shape[0] // count
    return launch(
        order_body,
        "order_rows",
        (tiles + 1,),
        [
            (mine, full(mine.shape)),
            (theirs, full(mine.shape)),
            (grads, pl.BlockSpec((count, dim), lambda i, place: (jnp.minimum(i, tiles - 1), 0))),
        ],
        [
            ((count, dim), BF16, full((count, dim))),
            (
                (grads.shape[0] + count, dim),
                BF16,
                pl.BlockSpec((count, dim), lambda i, place: (i, 0)),
            ),
        ],
        cost(0, 4 * grads.size),
        prefetch=(place,),
        after=after,
    )


def stack_body(left_ref, right_ref, out_ref):
    count = left_ref.shape[0]
    out_ref[:count] = left_ref[...]
    out_ref[count:] = right_ref[...]


def stack_two(left, right, after=()):
    shape = (2 * left.shape[0], *left.shape[1:])
    return launch(
        stack_body,
        "stack_two",
        (1,),
        [(left, full(left.shape)), (right, full(right.shape))],
        [(shape, left.dtype, full(shape))],
        cost(0, left.size * 8),
        after=after,
    )[0]


def project_body(x_ref, vecs_ref, own_vec_ref, par_vec_ref, *rest, given):
    qkv_ref, turned_ref = rest[-2 - given : len(rest) - given]
    if given:
        both_ref = rest[-1]
        parts = rest[:6]
        width = parts[0].shape[1]

        @pl.when(pl.program_id(0) == 0)
        def _():
            for number, part in enumerate(parts):
                half, kind = divmod(number, 3)
                both_ref[half, :, kind * width : (kind + 1) * width] = part[...]

    else:
        both_ref = rest[0]
    xhat, _ = normed(x_ref[...].astype(F32))
    hidden = (xhat * vecs_ref[0:1, :] + vecs_ref[1:2, :]).astype(BF16)
    turned_ref[...] = hidden.T
    width = both_ref.shape[2]
    third = width // 3
    for half, vec_ref in enumerate((own_vec_ref, par_vec_ref)):
        first = half * width
        made = nn(hidden, both_ref[half])
        bias = vec_ref[0:1, : 2 * third]
        qkv_ref[:, first : first + third] = (
            (made[:, :third] + bias[:, :third]) * SCALE
        ).astype(BF16)
        qkv_ref[:, first + third : first + 2 * third] = made[:, third : 2 * third].astype(BF16)
        qkv_ref[:, first + 2 * third : first + width] = (
            made[:, 2 * third :] + bias[:, third:]
        ).astype(BF16)


def project(x, vecs, halves, weights, after=()):
    rows, dim = x.shape
    given = len(weights) > 1
    half = 3 * weights[0].shape[1] if given else weights[0].shape[2]
    width = 2 * half
    both = (2, dim, half)
    return launch(
        functools.partial(project_body, given=int(given)),
        "project",
        (rows // TILE,),
        [
            (far(x) if given else x, pl.BlockSpec((TILE, dim), lambda i: (i, 0))),
            (vecs, full(vecs.shape)),
            (halves[0], full(halves[0].shape)),
            (halves[1], full(halves[1].shape)),
        ]
        + [(far(w), full(w.shape)) for w in weights],
        [
            ((rows, width), BF16, pl.BlockSpec((TILE, width), lambda i: (i, 0))),
            ((dim, rows), BF16, pl.BlockSpec((dim, TILE), lambda i: (0, i))),
        ]
        + ([(both, BF16, full(both), True)] if given else []),
        cost(2 * rows * dim * width, 2 * (rows * (2 * dim + width) + dim * width)),
        after=after,
    )


def pair_column(kind, pairs):
    half = pairs // 2
    return lambda p: (p // half) * 3 * half + kind * half + p % half


def write_stats(out_ref, head, lse):
    first = lse.astype(BF16).astype(F32)
    second = (lse - first).astype(BF16).astype(F32)
    third = lse - first - second
    row = lax.broadcasted_iota(jnp.int32, (STATS, lse.shape[1]), 0)
    held = jnp.where(row == 0, first, jnp.where(row == 1, second, jnp.where(row == 2, third, 0.0)))
    out_ref[head, HD : HD + STATS, :] = held.astype(BF16)


def read_stats(ref, head):
    held = ref[head, HD : HD + STATS, :].astype(F32)
    return held[0:1] + held[1:2] + held[2:3]


def summed_up(scores, values, seen=None):
    weights = jnp.exp(scores)
    total = jnp.sum(weights, axis=0, keepdims=True)
    summed = nn(values, weights.astype(BF16))
    faint = total < FAINT
    if seen is not None:
        faint = faint & (seen > 0.0)
    return summed, total, jnp.max(jnp.where(faint, 1.0, 0.0))


def summed_faint(scores, values):
    top = jnp.max(scores, axis=0, keepdims=True)
    weights = jnp.exp(scores - top)
    total = jnp.sum(weights, axis=0, keepdims=True)
    return nn(values, weights.astype(BF16)) / total, top + jnp.log(total)


def glob_forward_body(
    q_ref, k_ref, v_ref, kg_ref, vg_ref, augk_ref, augq_ref, seen_ref, own_ref, par_ref
):
    queries = q_ref[...]
    keys = jnp.concatenate([k_ref[...], kg_ref[...]], 0)
    values_turned = jnp.concatenate([v_ref[...], vg_ref[...]], 0).T
    seen = seen_ref[0:1, :]
    half = pl.num_programs(0) // 2

    def write(head, summed, lse):
        for ref, here in ((par_ref, pl.program_id(0) < half), (own_ref, pl.program_id(0) >= half)):

            @pl.when(here)
            def _(ref=ref):
                ref[head, :HD, :] = summed
                write_stats(ref, head, lse)

    both = []
    for head in range(2):
        mine, other = head_lanes(head)
        key_head = keys * mine + augk_ref[...] * other
        query_head = queries * mine + augq_ref[...] * other
        both.append(nt(key_head, query_head))
    results = []
    for head in range(2):
        values = values_turned[head * HD : (head + 1) * HD, :]
        summed, total, faint = summed_up(both[head], values, seen)
        some = total > 0.0
        safe = jnp.where(some, total, 1.0)
        results.append((summed / safe, jnp.where(some, jnp.log(safe), NEG), faint))
    for head, (summed, lse, _) in enumerate(results):
        write(head, summed.astype(BF16), lse)
    for head, (_, _, faint) in enumerate(results):

        @pl.when(faint > 0.0)
        def _(head=head):
            values = values_turned[head * HD : (head + 1) * HD, :]
            summed, lse = summed_faint(both[head], values)
            write(head, summed.astype(BF16), jnp.where(seen > 0.0, lse, NEG))


def glob_forward(qkv, qkv_glob, augk, augq, seen, pairs):
    count = augq.shape[0]
    half = pairs // 2

    def block(array, kind):
        column = pair_column(kind, pairs)
        return (
            array,
            pl.BlockSpec((array.shape[0], LANES), lambda p: (0, column((p + half) % pairs))),
        )

    work = 2 * pairs * augk.shape[0] * count
    shape = (pairs, HD + STATS, count)
    size = (2, HD + STATS, count)
    return launch(
        glob_forward_body,
        "glob_forward",
        (pairs,),
        [
            block(qkv_glob, 0),
            block(qkv, 1),
            block(qkv, 2),
            block(qkv_glob, 1),
            block(qkv_glob, 2),
            (augk, full(augk.shape)),
            (augq, full(augq.shape)),
            (seen, full(seen.shape)),
        ],
        [
            (shape, BF16, pl.BlockSpec(size, lambda p: (jnp.maximum(p - half, 0), 0, 0))),
            (shape, BF16, pl.BlockSpec(size, lambda p: (jnp.minimum(p, half - 1), 0, 0))),
        ],
        cost(work * 2 * 512, qkv.size * 2, work),
    )


def merge_body(left_ref, right_ref, out_ref):
    for head in range(left_ref.shape[0]):
        lse_left, lse_right = read_stats(left_ref, head), read_stats(right_ref, head)
        top = jnp.maximum(lse_left, lse_right)
        weight_left, weight_right = jnp.exp(lse_left - top), jnp.exp(lse_right - top)
        total = weight_left + weight_right
        out_left = left_ref[head, :HD, :].astype(F32)
        out_right = right_ref[head, :HD, :].astype(F32)
        merged = (out_left * weight_left + out_right * weight_right) / total
        out_ref[head, :HD, :] = merged.astype(BF16)
        write_stats(out_ref, head, top + jnp.log(total))


def merge(left, right, after=()):
    spec = full(left.shape)
    return launch(
        merge_body, "merge", (1,), [(left, spec), (right, spec)], [(left.shape, BF16, spec)],
        cost(left.size * 8, left.size * 6), after=after,
    )[0]


def local_forward_body(docs_ref, q_ref, k_ref, v_ref, kg_ref, vg_ref, augk_ref, augg_ref, out_ref, lse_ref):
    keys = jnp.concatenate([k_ref[...], kg_ref[...]], 0)
    values_turned = jnp.concatenate([v_ref[...], vg_ref[...]], 0).T
    bias = jnp.concatenate([augk_ref[...], augg_ref[...]], 0)
    both = []
    for head in range(2):
        mine, other = head_lanes(head)
        key_head = keys * mine + bias * other
        query_head = q_ref[...] * mine + lane_one(0) * other
        both.append(nt(key_head, query_head))
    outs, faints = [], []
    for head in range(2):
        values = values_turned[head * HD : (head + 1) * HD, :]
        summed, total, faint = summed_up(both[head], values)
        outs.append(summed / total)
        faints.append(faint)
        lse_ref[0, 0, head : head + 1, :] = jnp.log(total)
    out_ref[...] = jnp.concatenate(outs, 0).T.astype(BF16)

    @pl.when(faints[0] + faints[1] > 0.0)
    def _():
        again = []
        for head in range(2):
            values = values_turned[head * HD : (head + 1) * HD, :]
            summed, lse = summed_faint(both[head], values)
            again.append(summed)
            lse_ref[0, 0, head : head + 1, :] = lse
        out_ref[...] = jnp.concatenate(again, 0).T.astype(BF16)


def local_forward(docs, qkv, qkv_glob, augk, pairs, blocks, first, count, held=(), after=()):
    rows_all = augk.shape[0]
    glob_first = blocks * BLOCK // GLOB

    def block(kind):
        column = pair_column(kind, pairs)
        return (
            qkv,
            pl.BlockSpec((BLOCK, LANES), lambda b, p, docs: (b, column(p + first))),
        )

    def glob_block(kind):
        column = pair_column(kind, pairs)
        return (
            qkv_glob,
            pl.BlockSpec((GLOB, LANES), lambda b, p, docs: (docs[b], column(p + first))),
        )

    work = 2 * count * blocks * BLOCK * (BLOCK + GLOB)
    width = pairs * LANES
    straight = pl.BlockSpec((BLOCK, LANES), lambda b, p, docs: (b, p + first))
    return launch(
        local_forward_body,
        "local_forward",
        (blocks, count),
        [
            block(0),
            block(1),
            block(2),
            glob_block(1),
            glob_block(2),
            (augk, pl.BlockSpec((BLOCK, LANES), lambda b, p, docs: (b, 0))),
            (augk, pl.BlockSpec((GLOB, LANES), lambda b, p, docs: (glob_first, 0))),
        ],
        [
            ((rows_all, width), BF16, straight),
            (
                (blocks, pairs, 2, BLOCK),
                F32,
                pl.BlockSpec((1, 1, 2, BLOCK), lambda b, p, docs: (b, p + first, 0, 0)),
            ),
        ],
        cost(work * 2 * 512, count * rows_all * LANES * 12, work),
        prefetch=(docs,),
        held=held,
        after=after,
    )


def middle_of(out_high, x, own_ref, par_ref, vecs_ref):
    half = own_ref.shape[0]
    branch = nn(out_high[:, :half], own_ref[...]) + nn(out_high[:, half:], par_ref[...])
    middle = x.astype(F32) + branch + vecs_ref[4:5, :]
    xhat, _ = normed(middle)
    hidden = (xhat * vecs_ref[2:3, :] + vecs_ref[3:4, :]).astype(BF16)
    return middle, hidden


def middle_body(out_ref, x_ref, own_ref, par_ref, vecs_ref, mid_ref, hid_ref, turned_ref):
    middle, hidden = middle_of(out_ref[...], x_ref[...], own_ref, par_ref, vecs_ref)
    mid_ref[...] = middle
    hid_ref[...] = hidden
    turned_ref[...] = hidden.T


def middle_local(out_high, x, w_own, w_par, vecs, after=()):
    rows_all, dim = out_high.shape
    rows = x.shape[0]
    row = pl.BlockSpec((TILE, dim), lambda i: (i, 0))
    return launch(
        middle_body,
        "middle_local",
        (rows // TILE,),
        [
            (out_high, row),
            (far(x), row),
            (w_own, full(w_own.shape)),
            (w_par, full(w_par.shape)),
            (vecs, full(vecs.shape)),
        ],
        [
            ((rows_all, dim), F32, row, True),
            ((rows_all, dim), BF16, row),
            ((dim, rows_all), BF16, pl.BlockSpec((dim, TILE), lambda i: (0, i))),
        ],
        cost(2 * rows * dim * dim, 12 * rows * dim + 2 * dim * dim),
        after=after,
    )


def middle_glob_body(
    own_out_ref, par_out_ref, x_ref, own_ref, par_ref, vecs_ref,
    mid_ref, hid_ref, turned_ref, high_ref, lse_ref,
):
    heads = own_out_ref.shape[0]
    parts = [own_out_ref[head, :HD, :] for head in range(heads)]
    parts += [par_out_ref[head, :HD, :] for head in range(heads)]
    turned = jnp.concatenate(parts, 0)
    high = turned.T
    high_ref[...] = high
    stats = [read_stats(own_out_ref, head) for head in range(heads)]
    stats += [read_stats(par_out_ref, head) for head in range(heads)]
    spare = lse_ref.shape[0] - 2 * heads
    lse_ref[...] = jnp.concatenate(stats + [jnp.zeros((spare, x_ref.shape[0]), F32)], 0)
    middle, hidden = middle_of(high, x_ref[...], own_ref, par_ref, vecs_ref)
    mid_ref[...] = middle
    hid_ref[...] = hidden
    turned_ref[...] = hidden.T


def middle_glob(own_out, par_out, x, w_own, w_par, vecs, held):
    rows, dim = x.shape
    first = held[0].shape[0] // rows - 1
    row = pl.BlockSpec((rows, dim), lambda i: (first, 0))
    col = pl.BlockSpec((dim, rows), lambda i: (0, first))
    operands = [own_out, par_out, x, w_own, w_par, vecs]
    specs = [row, row, col, row]
    return launch(
        middle_glob_body,
        "middle_glob",
        (1,),
        [(a, full(a.shape)) for a in operands],
        [(h.shape, h.dtype, spec, *pin) for h, spec, pin in zip(held, specs, ((True,), (), (), ()))]
        + [((HEAD_ROWS, rows), F32, full((HEAD_ROWS, rows)))],
        cost(2 * rows * dim * dim, 12 * rows * dim + 2 * dim * dim),
        held=held,
    )


def ffn_body(
    hid_ref, turned_ref, dz_ref, up_ref, bias_ref, down_ref, mask_ref, *rest, chunks
):
    dn_in_ref = rest[0] if len(rest) == 8 else None
    dnorm_ref, act_ref, grads_ref, bias_grad_ref, act_s, dup_s, sum_s = rest[-7:]
    step = pl.program_id(0)
    rows_all, dim = hid_ref.shape
    chunk = bias_grad_ref.shape[1]
    tail = slice(rows_all - mask_ref.shape[0], rows_all)

    @pl.when(step < chunks)
    def _():
        cols = pl.ds(pl.multiple_of(step * chunk, chunk), chunk)
        up = nn(hid_ref[...], up_ref[:, cols]) + bias_ref[0:1, :]
        share = 0.5 * (1.0 + lax.erf(up * (2.0**-0.5)))
        density = jnp.exp(up * up * -0.5) * 0.3989422804014327
        active = (up * share).astype(BF16)
        slope = share + up * density
        d_up = (nt(dz_ref[...], down_ref[cols, :]) * slope).astype(BF16)
        act_ref[...] = active
        dup_s[:, cols] = d_up
        act_s[...] = active
        sum_s[...] = d_up
        mask = mask_ref[...]
        act_s[tail, :] = (active[tail].astype(F32) * mask).astype(BF16)
        sum_s[tail, :] = (d_up[tail].astype(F32) * mask).astype(BF16)
        bias_grad_ref[...] = jnp.sum(sum_s[...].astype(F32), axis=0, keepdims=True)
        up_grad = nn(turned_ref[...], sum_s[...]).astype(BF16)
        down_grad = tn(act_s[...], dz_ref[...]).astype(BF16)
        place = 0
        for grad in (up_grad, down_grad):
            rows = grad.shape[0]
            for col in range(grad.shape[1] // LANES):
                grads_ref[0, place : place + rows, :] = grad[:, col * LANES : (col + 1) * LANES]
                place += rows

    @pl.when(step >= chunks)
    def _():
        start = pl.multiple_of((step - chunks) * TILE, TILE)
        made = nt(dup_s[pl.ds(start, TILE), :], up_ref[...])
        dnorm_ref[...] = made if dn_in_ref is None else made + dn_in_ref[...]


def ffn_part(hidden, turned, dz, w_up, vec, w_down, mask, first, units, dn_in=None, after=()):
    rows_all, dim = hidden.shape
    half = w_up.shape[1]
    chunk = min(FFN_CHUNK, units)
    chunks = units // chunk
    skip = first // units
    packed = 2 * chunk * dim // LANES
    bias_first = (vec.shape[1] - half + first) // chunk

    def now(j):
        return jnp.minimum(j, chunks - 1)

    row = pl.BlockSpec((TILE, dim), lambda j: (jnp.maximum(j - chunks, 0), 0))
    tail = mask.shape[0] // TILE - 1
    one = pl.Buffered(1)
    operands = [
        (hidden, full(hidden.shape)),
        (turned, full(turned.shape)),
        (dz, full(dz.shape)),
        (w_up, pl.BlockSpec((dim, units), lambda j: (0, skip), pipeline_mode=one)),
        (vec, pl.BlockSpec((vec.shape[0], chunk), lambda j: (0, bias_first + now(j)))),
        (w_down, pl.BlockSpec((units, dim), lambda j: (skip, 0), pipeline_mode=one)),
        (mask, pl.BlockSpec((TILE, 1), lambda j: (tail, 0))),
    ]
    if dn_in is not None:
        operands.append((dn_in, row))
    return launch(
        functools.partial(ffn_body, chunks=chunks),
        "ffn_part",
        (chunks + rows_all // TILE,),
        operands,
        [
            ((rows_all, dim), F32, row),
            ((rows_all, units), BF16, pl.BlockSpec((rows_all, chunk), lambda j: (0, now(j))), True),
            ((chunks, packed, LANES), BF16, pl.BlockSpec((1, packed, LANES), lambda j: (now(j), 0, 0))),
            ((1, units), F32, pl.BlockSpec((1, chunk), lambda j: (0, now(j)))),
        ],
        cost(10 * rows_all * dim * units, rows_all * dim * 14 + units * dim * 8, 2 * rows_all * units),
        after=after,
        scratch=[
            pltpu.VMEM((rows_all, chunk), BF16),
            pltpu.VMEM((rows_all, units), BF16),
            pltpu.VMEM((rows_all, chunk), BF16),
        ],
    )


def output_body(place_ref, mid_ref, vecs_ref, *rest):
    out_ref, glob_ref = rest[-2:]
    parts = len(rest) // 2 - 1
    made = mid_ref[...] + vecs_ref[5:6, :]
    for part in range(parts):
        made = made + nn(rest[part][...], rest[parts + part][...])
    step = pl.program_id(0)
    last = pl.num_programs(0) - 1

    @pl.when(step < last)
    def _():
        out_ref[...] = made.astype(BF16)

    @pl.when(step == last)
    def _():
        glob_ref[...] = made.astype(BF16)


def output_rows(place, middle, vecs, acts, weights, own, after=()):
    rows_all, dim = middle.shape
    tiles = rows_all // TILE
    rows = rows_all - TILE
    row = pl.BlockSpec((TILE, dim), lambda i, place: (i, 0))
    operands = [(far(middle), row), (vecs, full(vecs.shape))]
    operands += [
        (far(act), pl.BlockSpec((TILE, act.shape[1]), lambda i, place: (i, 0))) for act in acts
    ]
    for act, (weight, number) in zip(acts, weights):
        operands.append(
            (
                far(weight),
                pl.BlockSpec(
                    (act.shape[1], dim),
                    lambda i, place, number=number: (number, 0),
                    pipeline_mode=pl.Buffered(1),
                ),
            )
        )
    units = sum(act.shape[1] for act in acts)
    out, glob = launch(
        output_body,
        "output_rows",
        (tiles,),
        operands,
        [
            ((rows, dim), BF16, pl.BlockSpec((TILE, dim), lambda i, place: (jnp.minimum(i, tiles - 2), 0))),
            ((TILE, dim), BF16, full((TILE, dim))),
        ],
        cost(2 * rows_all * dim * units, rows_all * (units * 2 + dim * 6) + units * dim * 2),
        prefetch=(place,),
        after=after,
    )
    return out, glob


def middle_back_body(
    dn_ref, mid_ref, dz_ref, high_ref, own_ref, par_ref, vecs_ref, mask_ref,
    dmid_ref, dattn_ref, delta_ref, grads_ref, sums_ref, acc_s,
):
    step = pl.program_id(0)
    dim = mid_ref.shape[1]
    half = own_ref.shape[0]
    xhat, inv = normed(mid_ref[...])
    dn = dn_ref[...]
    dz = dz_ref[...].astype(F32)
    d_mid = dz + norm_back(xhat, inv, vecs_ref[2:3, :], dn)
    dmid_ref[...] = d_mid
    d_branch = d_mid.astype(BF16)
    for part, weight in enumerate((own_ref, par_ref)):
        dattn_ref[:, part * half : (part + 1) * half] = nt(d_branch, weight[...]).astype(BF16)
    product = dattn_ref[...].astype(F32) * high_ref[...].astype(F32)
    first = product.astype(BF16)
    second = (product - first.astype(F32)).astype(BF16)
    head = lax.broadcasted_iota(jnp.int32, (delta_ref.shape[0], dim), 0)
    column = lax.broadcasted_iota(jnp.int32, (delta_ref.shape[0], dim), 1)
    picked = jnp.where((column >= head * HD) & (column < (head + 1) * HD), 1.0, 0.0).astype(BF16)
    delta_ref[...] = nt(picked, first) + nt(picked, second)
    mask = mask_ref[...]
    masked = (d_branch.astype(F32) * mask).astype(BF16)
    made = tn(high_ref[...], masked)
    sums = [
        jnp.sum(dn * xhat * mask, axis=0, keepdims=True),
        jnp.sum(dn * mask, axis=0, keepdims=True),
        jnp.sum(masked.astype(F32), axis=0, keepdims=True),
        jnp.sum(dz * mask, axis=0, keepdims=True),
    ]
    sums = jnp.concatenate(sums + [jnp.zeros((4, dim), F32)], 0)

    @pl.when(step == 0)
    def _():
        acc_s[...] = made
        sums_ref[...] = sums

    @pl.when(step > 0)
    def _():
        acc_s[...] += made
        sums_ref[...] += sums

    @pl.when(step == pl.num_programs(0) - 1)
    def _():
        for part in range(2):
            for col in range(dim // LANES):
                grads_ref[part, col * half : (col + 1) * half, :] = acc_s[
                    part * half : (part + 1) * half, col * LANES : (col + 1) * LANES
                ].astype(BF16)


def middle_back(dn, middle, dz, high, w_own, w_par, vecs, mask, after=()):
    rows_all, dim = middle.shape
    row = pl.BlockSpec((TILE, dim), lambda i: (i, 0))
    packed = w_own.size // LANES
    return launch(
        middle_back_body,
        "middle_back",
        (rows_all // TILE,),
        [
            (dn, row),
            (middle, row),
            (dz, row),
            (high, row),
            (w_own, full(w_own.shape)),
            (w_par, full(w_par.shape)),
            (vecs, full(vecs.shape)),
            (mask, pl.BlockSpec((TILE, 1), lambda i: (i, 0))),
        ],
        [
            ((rows_all, dim), F32, row, True),
            ((rows_all, dim), BF16, row),
            ((HEAD_ROWS, rows_all), F32, pl.BlockSpec((HEAD_ROWS, TILE), lambda i: (0, i))),
            ((2, packed, LANES), BF16, full((2, packed, LANES))),
            ((8, dim), F32, full((8, dim))),
        ],
        cost(4 * rows_all * dim * dim, rows_all * dim * 24),
        after=after,
        scratch=[pltpu.VMEM((dim, dim), F32)],
    )


def attention_back_body(
    docs_ref, ql_ref, kl_ref, vl_ref, qg_ref, kg_ref, vg_ref, do_ref, lse_ref, lseg_ref, delta_ref,
    augk_ref, augq_ref, dq_ref, dk_ref, dv_ref, q_ref, key_s, value_s, turned_s, dk_s, dv_s, *, first,
):
    pair = pl.program_id(0) + first
    rows_all = q_ref.shape[0]
    count = augq_ref.shape[0]
    local_rows = rows_all - count
    blocks = local_rows // BLOCK
    q_ref[:local_rows, :] = ql_ref[...]
    q_ref[local_rows:, :] = qg_ref[...]
    turned_s[:, :local_rows] = kl_ref[...].T
    turned_s[:, local_rows:] = kg_ref[...].T
    dk_s[...] = jnp.zeros_like(dk_s)
    dv_s[...] = jnp.zeros_like(dv_s)
    dq_parts = [[] for _ in range(blocks + 1)]
    for head in range(2):
        mine, other = head_lanes(head)
        key_s[:local_rows, :] = kl_ref[...] * mine + augk_ref[:local_rows, :] * other
        key_s[local_rows:, :] = kg_ref[...] * mine + augk_ref[local_rows:, :] * other
        value_s[:local_rows, :] = vl_ref[...] * mine
        value_s[local_rows:, :] = vg_ref[...] * mine
        head_rows = slice(head * HD, (head + 1) * HD)
        index = 2 * pair + head

        def grads(key_cat, value_cat, turned_cat, query_rows, aug, lse):
            queries = q_ref[query_rows, :] * mine
            douts = do_ref[query_rows, :] * mine
            delta = delta_ref[pl.ds(index, 1), query_rows]
            probs = jnp.exp(nt(key_cat, queries + aug * other) - lse)
            d_scores = (probs * (nt(value_cat, douts) - delta)).astype(BF16)
            d_key = nn(d_scores, queries)
            d_value = nn(probs.astype(BF16), douts)
            return nn(turned_cat, d_scores), d_key, d_value

        for block in range(blocks):
            rows = slice(block * BLOCK, (block + 1) * BLOCK)
            start = pl.multiple_of(local_rows + docs_ref[block] * GLOB, GLOB)
            doc_rows = pl.ds(start, GLOB)
            key_cat = jnp.concatenate([key_s[rows, :], key_s[doc_rows, :]], 0)
            value_cat = jnp.concatenate([value_s[rows, :], value_s[doc_rows, :]], 0)
            turned_cat = jnp.concatenate(
                [turned_s[head_rows, rows], turned_s[head_rows, doc_rows]], 1
            )
            d_query, d_key, d_value = grads(
                key_cat, value_cat, turned_cat, rows, lane_one(0), lse_ref[block, 0, head : head + 1, :]
            )
            dq_parts[block].append(d_query)
            dk_s[rows, :] += d_key[:BLOCK]
            dk_s[doc_rows, :] += d_key[BLOCK:]
            dv_s[rows, :] += d_value[:BLOCK]
            dv_s[doc_rows, :] += d_value[BLOCK:]
        rows = slice(local_rows, rows_all)
        d_query, d_key, d_value = grads(
            key_s[...], value_s[...], turned_s[head_rows, :], rows, augq_ref[...],
            lseg_ref[pl.ds(index, 1), :],
        )
        dq_parts[blocks].append(d_query)
        dk_s[...] += d_key
        dv_s[...] += d_value
    for block in range(blocks + 1):
        begin = block * BLOCK
        made = jnp.concatenate(dq_parts[block], 0).T
        dq_ref[begin : begin + made.shape[0], :] = (
            made.astype(BF16).astype(F32) * SCALE
        ).astype(BF16)
    dk_ref[...] = dk_s[...].astype(BF16)
    dv_ref[...] = dv_s[...].astype(BF16)


def attention_back(
    docs, qkv, qkv_glob, d_attn, lse, lse_glob, delta, augk, augq, pairs, first, spot, held=(),
    after=(),
):
    number = 1
    rows_all = augk.shape[0]
    count = augq.shape[0]
    blocks = (rows_all - count) // BLOCK

    def block(array, kind):
        column = pair_column(kind, pairs)
        return (
            array,
            pl.BlockSpec((array.shape[0], LANES), lambda p, docs: (0, column(p + first))),
        )

    straight = pl.BlockSpec((rows_all, LANES), lambda p, docs: (0, p + first))
    work = 2 * number * (blocks * BLOCK * (BLOCK + GLOB) + rows_all * count)
    return launch(
        functools.partial(attention_back_body, first=first),
        "attention_back",
        (number,),
        [
            block(qkv, 0),
            block(qkv, 1),
            block(qkv, 2),
            block(qkv_glob, 0),
            block(qkv_glob, 1),
            block(qkv_glob, 2),
            (d_attn, straight),
            (lse, pl.BlockSpec((blocks, 1, 2, BLOCK), lambda p, docs: (0, p + first, 0, 0))),
            (lse_glob, full(lse_glob.shape)),
            (delta, full(delta.shape)),
            (augk, full(augk.shape)),
            (augq, full(augq.shape)),
        ],
        [((rows_all, pairs * LANES), BF16, pl.BlockSpec((rows_all, LANES), lambda p, docs: (0, spot)))] * 3,
        cost(work * 5 * 512, number * rows_all * LANES * 14, work),
        prefetch=(docs,),
        held=held,
        after=after,
        scratch=[
            pltpu.VMEM((rows_all, LANES), BF16),
            pltpu.VMEM((rows_all, LANES), BF16),
            pltpu.VMEM((rows_all, LANES), BF16),
            pltpu.VMEM((LANES, rows_all), BF16),
            pltpu.VMEM((rows_all, LANES), F32),
            pltpu.VMEM((rows_all, LANES), F32),
        ],
    )


def project_grad_body(
    turned_ref, turned_glob_ref, dq_ref, dk_ref, dv_ref, weight_ref, vecs_ref, *rest, first, last, shared
):
    dim, local_rows = turned_ref.shape
    width = dq_ref.shape[1]
    third = weight_ref.shape[1] // 3
    cols = width // LANES
    cut = dim // 2
    count = 3 * cols
    if last:
        carry_ref, mid_ref, *up_refs, grads_ref = rest
    else:
        grads_ref, next_ref = rest
    ones = jnp.ones((8, width), BF16)
    sums, dots, shifts = [], None, None
    for kind, ref in enumerate((dq_ref, dk_ref, dv_ref)):
        made = nn(turned_ref[...], ref[:local_rows, :]) + nn(turned_glob_ref[...], ref[local_rows:, :])
        begin = kind * third + first
        weight = weight_ref[:, begin : begin + width]
        total = jnp.sum(ref[...].astype(F32), axis=0, keepdims=True)
        sums.append(total)
        scaled = made * weight.astype(F32)
        high = scaled.astype(BF16)
        low = (scaled - high.astype(F32)).astype(BF16)
        dot = nt(ones, high) + nt(ones, low)
        high = total.astype(BF16).astype(F32)
        low = (total - high).astype(BF16).astype(F32)
        parts = jnp.concatenate([high, low, jnp.zeros((6, width), F32)], 0)
        shift = jnp.sum(nt(parts.astype(BF16), weight), axis=0, keepdims=True)
        dots = dot if dots is None else dots + dot
        shifts = shift if shifts is None else shifts + shift
        rounded = made.astype(BF16)
        for col in range(cols):
            for part in range(2):
                number = 2 * (kind * cols + col) + part
                spot = number % count * cut
                grads_ref[number // count, spot : spot + cut, :] = rounded[
                    part * cut : (part + 1) * cut, col * LANES : (col + 1) * LANES
                ]
    if not last:
        row = jnp.concatenate([sums[0], sums[2], jnp.zeros((1, dim - 2 * width), F32)], 1)
        next_ref[...] = jnp.concatenate([dots[0:1, :], shifts, row, jnp.zeros((5, dim), F32)], 0)
        return
    dots = dots[0:1, :] + carry_ref[0:1, :]
    shifts = shifts + carry_ref[1:2, :]
    gains = (dots - vecs_ref[1:2, :] * shifts) / vecs_ref[0:1, :]
    small = [mid_ref[row : row + 1, :] * shared for row in range(4)]
    small += [gains, shifts]
    for number, total in enumerate((sums[0], sums[2])):
        small += [carry_ref[2:3, number * first : (number + 1) * first], total]
    small += [ref[...] for ref in up_refs]
    pieces = []
    for row in small:
        pieces += [row[:, col * LANES : (col + 1) * LANES] for col in range(row.shape[1] // LANES)]
    pieces.append(jnp.zeros((LANES - len(pieces), LANES), F32))
    grads_ref[0, count * cut :, :] = jnp.concatenate(pieces, 0).astype(BF16)
    grads_ref[1, count * cut :, :] = jnp.zeros((LANES, LANES), BF16)


def project_grad(
    turned, turned_glob, dq, dk, dv, weight, vecs, half, first, width, spot, carry=None, mid_sums=None,
    up_sums=(), after=(),
):
    dim = turned.shape[0]
    rows_all = dq.shape[0]
    last = carry is not None
    grads = pl.BlockSpec((rows_all, width), lambda i: (0, spot))
    shape = (2, 3 * width // LANES * dim // 2 + (LANES if last else 0), LANES)
    more = [carry, mid_sums, *up_sums] if last else []
    return launch(
        functools.partial(project_grad_body, first=first, last=last, shared=1.0 - half),
        "project_grad",
        (1,),
        [
            (turned, full(turned.shape)),
            (turned_glob, full(turned_glob.shape)),
            (dq, grads),
            (dk, grads),
            (dv, grads),
            (weight, pl.BlockSpec((None, *weight.shape[1:]), lambda i: (half, 0, 0))),
            (vecs, full(vecs.shape)),
        ]
        + [(array, full(array.shape)) for array in more],
        [(shape, BF16, full(shape))] + ([] if last else [((8, dim), F32, full((8, dim)))]),
        cost(6 * rows_all * dim * width, rows_all * (dim + 3 * width) * 2),
        after=after,
    )


def hidden_back(dq_ref, dk_ref, dv_ref, both_ref, places):
    d_hidden = None
    for part, spots in enumerate(places):
        joined = jnp.concatenate(
            [ref[:, s * LANES : (s + 1) * LANES] for ref in (dq_ref, dk_ref, dv_ref) for s in spots], 1
        )
        made = nt(joined, both_ref[part])
        d_hidden = made if d_hidden is None else d_hidden + made
    return d_hidden


def input_back_body(
    dq_ref, dk_ref, dv_ref, both_ref, x_ref, dmid_ref, vecs_ref, tokens_ref, *, places
):
    d_hidden = hidden_back(dq_ref, dk_ref, dv_ref, both_ref, places)
    xhat, inv = normed(x_ref[...].astype(F32))
    tokens_ref[...] = dmid_ref[...] + norm_back(xhat, inv, vecs_ref[0:1, :], d_hidden)


def input_back(dq, dk, dv, both, x, d_mid, vecs, places, after=()):
    rows, dim = x.shape
    row = pl.BlockSpec((TILE, dim), lambda i: (i, 0))
    return launch(
        functools.partial(input_back_body, places=places),
        "input_back",
        (rows // TILE,),
        [
            (dq, row),
            (dk, row),
            (dv, row),
            (both, full(both.shape)),
            (x, row),
            (d_mid, row),
            (vecs, full(vecs.shape)),
        ],
        [(x.shape, F32, row, True)],
        cost(6 * rows * dim * dim, rows * dim * 16 + 6 * dim * dim),
        after=after,
    )[0]


def glob_back_body(dq_ref, dk_ref, dv_ref, both_ref, out_ref, *, places):
    out_ref[...] = hidden_back(dq_ref, dk_ref, dv_ref, both_ref, places).astype(BF16)


def glob_back(dq, dk, dv, both, places, after=()):
    rows_all, dim = dq.shape
    last = rows_all // TILE - 1
    row = pl.BlockSpec((TILE, dim), lambda i: (last, 0))
    return launch(
        functools.partial(glob_back_body, places=places),
        "glob_back",
        (1,),
        [(dq, row), (dk, row), (dv, row), (both, full(both.shape))],
        [((TILE, dim), BF16, full((TILE, dim)))],
        cost(6 * TILE * dim * dim, TILE * dim * 16 + 6 * dim * dim),
        after=after,
    )[0]


def glob_input_body(kept_ref, got_ref, x_ref, dmid_ref, vecs_ref, out_ref):
    d_hidden = kept_ref[...].astype(F32) + got_ref[...].astype(F32)
    xhat, inv = normed(x_ref[...].astype(F32))
    out_ref[...] = dmid_ref[...] + norm_back(xhat, inv, vecs_ref[0:1, :], d_hidden)


def glob_input(place, kept, got, x, d_mid, vecs, after=()):
    own, dim = x.shape
    first = (d_mid.shape[0] - 2 * GLOB) // own
    spec = pl.BlockSpec((own, dim), lambda i, place: (0, 0))
    here = pl.BlockSpec((own, dim), lambda i, place: (first + place[2] // own, 0))

    def body(place_ref, *refs):
        glob_input_body(*refs)

    return launch(
        body,
        "glob_input",
        (1,),
        [(kept, spec), (got, spec), (x, spec), (d_mid, here), (vecs, full(vecs.shape))],
        [((own, dim), F32, spec, True)],
        cost(0, own * dim * 14),
        prefetch=(place,),
        after=after,
    )[0]


def pair_add(left, right):
    return (left.astype(F32) + right.astype(F32)).astype(BF16)


def turn_body(place_ref, *refs, actions):
    count = sum(len(action[2]) for action in actions)
    ins, outs = list(refs[:count]), list(refs[count:])
    for kind, number, arrays in actions:
        mine = [ins.pop(0) for _ in arrays]
        side = None if number is None else place_ref[number]
        if kind == "start":
            go_ref, stay_ref = outs.pop(0), outs.pop(0)
            first = 0
            for own_ref, got_ref in zip(mine[::2], mine[1::2]):
                rows = slice(first, first + own_ref.shape[1])
                go_ref[rows, :] = pair_add(own_ref[1 - side], got_ref[1 - side])
                stay_ref[rows, :] = pair_add(own_ref[side], got_ref[side])
                first = rows.stop
        elif kind == "pick":
            go_ref, stay_ref = outs.pop(0), outs.pop(0)
            go_ref[...] = mine[0][1 - side]
            stay_ref[...] = mine[0][side]
        elif kind == "split":
            go_ref, stay_ref = outs.pop(0), outs.pop(0)
            go_ref[...] = pair_add(mine[0][1 - side], mine[1][1 - side])
            stay_ref[...] = pair_add(mine[0][side], mine[1][side])
        elif kind == "add":
            outs.pop(0)[...] = pair_add(mine[0][...], mine[1][...])
        elif kind == "join":
            out_ref = outs.pop(0)
            out_ref[side] = mine[0][...]
            out_ref[1 - side] = mine[1][...]
        else:
            outs.pop(0)[...] = mine[0][...]


def halved(array):
    return array.reshape(2, -1, array.shape[-1])


class Chain:
    def __init__(self, steps, sends, first):
        self.steps, self.sends, self.first, self.at = steps, sends, first, 0

    def action(self):
        kind, number = self.steps[self.at]
        if kind in ("start", "pick", "copy"):
            return kind, number, self.first
        arrays = [self.stay, self.other]
        return kind, number, [halved(a) for a in arrays] if kind == "split" else arrays

    def shapes(self):
        kind, _, arrays = self.action()
        lanes = arrays[0].shape[-1]
        if kind == "start":
            return [(sum(own.shape[1] for own in arrays[::2]), lanes)] * 2
        if kind in ("pick", "split"):
            return [arrays[0].shape[1:]] * 2
        if kind == "join":
            return [(2, *arrays[0].shape)]
        return [arrays[0].shape]

    def take(self, outs):
        kind, _ = self.steps[self.at]
        self.stay = outs[-1].reshape(-1, outs[-1].shape[-1]) if kind == "join" else outs[-1]
        self.other = self.sends[self.at](outs[0] if len(outs) > 1 else self.stay)
        self.at += 1

    @property
    def left(self):
        return len(self.steps) - self.at


def turn(place, chains, after=()):
    actions = [chain.action() for chain in chains]
    shapes = [chain.shapes() for chain in chains]
    flat = [shape for group in shapes for shape in group]
    arrays = [array for _, _, group in actions for array in group]
    outs = launch(
        functools.partial(turn_body, actions=[(k, n, [None] * len(a)) for k, n, a in actions]),
        "turn",
        (1,),
        [(a, full(a.shape)) for a in arrays],
        [(shape, BF16, full(shape)) for shape in flat],
        cost(0, sum(a.size for a in arrays) * 4),
        prefetch=(place,),
        after=after,
    )
    outs = list(outs)
    mark = outs[-1]
    for chain, group in zip(chains, shapes):
        chain.take([outs.pop(0) for _ in group])
    return [mark]


def by_side(place_ref, number, mine_ref, other_ref, write):
    for half in range(2):
        for ref, here in ((mine_ref, place_ref[number] == half), (other_ref, place_ref[number] != half)):

            @pl.when(here)
            def _(ref=ref, half=half):
                write(ref, half)


def ffn_unpack_body(place_ref, mine_ref, other_ref, up_ref, down_ref, *, number, chunk):
    dim = up_ref.shape[0]
    units = up_ref.shape[1]

    def write(ref, half):
        count = units * dim // LANES
        first = half * count
        spot = 0
        for step in range(units // chunk):
            for col in range(chunk // LANES):
                if first <= spot < first + count:
                    begin = step * chunk + col * LANES
                    up_ref[:, begin : begin + LANES] = ref[spot - first : spot - first + dim, :].astype(F32)
                spot += dim
            for col in range(dim // LANES):
                if first <= spot < first + count:
                    down_ref[step * chunk : (step + 1) * chunk, col * LANES : (col + 1) * LANES] = ref[
                        spot - first : spot - first + chunk, :
                    ].astype(F32)
                spot += chunk

    by_side(place_ref, number, mine_ref, other_ref, write)


def ffn_unpack(place, number, mine, other, dim, half, units, part, held=(), after=()):
    spec = full(mine.shape)
    one = pl.Buffered(1)
    return launch(
        functools.partial(ffn_unpack_body, number=number, chunk=min(FFN_CHUNK, units)),
        "ffn_unpack",
        (1,),
        [(mine, spec), (other, spec)],
        [
            ((dim, half), F32, pl.BlockSpec((dim, units), lambda i, place: (0, part), pipeline_mode=one), True),
            ((half, dim), F32, pl.BlockSpec((units, dim), lambda i, place: (part, 0), pipeline_mode=one), True),
        ],
        cost(0, mine.size * 12),
        prefetch=(place,),
        held=held,
        after=after,
    )


def tail_unpack_body(place_ref, mine_ref, other_ref, q_ref, k_ref, v_ref, more_ref, *, number, last):
    dim, width = q_ref.shape
    cols = width // LANES
    cut = dim // 2
    count = 3 * cols

    def write(ref, half):
        for spot in range(count):
            unit, part = divmod(half * count + spot, 2)
            kind, col = unit // cols, unit % cols
            (q_ref, k_ref, v_ref)[kind][
                part * cut : (part + 1) * cut, col * LANES : (col + 1) * LANES
            ] = ref[spot * cut : (spot + 1) * cut, :].astype(F32)
        spot = count * cut
        if last:
            if half == 0:
                more_ref[...] = ref[spot : spot + LANES, :].astype(F32)
            return
        rows, wide = more_ref.shape[0], more_ref.shape[1] // LANES // 2
        for col in range(wide):
            begin = (half * wide + col) * LANES
            more_ref[:, begin : begin + LANES] = ref[spot : spot + rows, :].astype(F32)
            spot += rows

    by_side(place_ref, number, mine_ref, other_ref, write)


def tail_unpack(place, number, mine, other, dim, half, first, width, held=()):
    spec = full(mine.shape)
    last = bool(held)
    block = pl.BlockSpec((dim, width), lambda i, place: (0, first // width), pipeline_mode=pl.Buffered(1))
    more = (LANES, LANES) if last else (half, dim)
    return launch(
        functools.partial(tail_unpack_body, number=number, last=last),
        "tail_unpack",
        (1,),
        [(mine, spec), (other, spec)],
        [((dim, half), F32, block, True)] * 3 + [(more, F32, full(more))],
        cost(0, mine.size * 12),
        prefetch=(place,),
        held=held,
    )


def finish_body(mine_ref, theirs_ref, *outs):
    rows = 0
    for number, out_ref in enumerate(outs):
        count = out_ref.shape[0] // LANES
        pieces = []
        for row in range(rows, rows + count):
            piece = mine_ref[row : row + 1, :]
            pieces.append(piece + theirs_ref[row : row + 1, :] if number < 6 else piece)
        out_ref[...] = jnp.concatenate(pieces, 1).reshape(-1)
        rows += count


def finish(mine, theirs, sizes):
    return launch(
        finish_body,
        "finish",
        (1,),
        [(mine, full(mine.shape)), (theirs, full(theirs.shape))],
        [((size,), F32, full((size,))) for size in sizes],
        cost(0, 4 * sum(sizes)),
    )


def per_device(
    tokens, glob_tokens, w_query, b_query, w_key, w_value, b_value, w_out, b_out, w_up, b_up,
    w_down, b_down, gain_attn, shift_attn, gain_ffn, shift_ffn, doc_blocks, doc_tail,
    grad_tokens, grad_glob,
):
    seq_size = lax.axis_size("seq")
    seq_pos = lax.axis_index("seq")
    tp_pos = lax.axis_index("tp")
    rows, dim = tokens.shape
    own_glob = glob_tokens.shape[0]
    half = w_query.shape[1]
    units = w_up.shape[1]
    pairs = 2 * half // PAIR
    blocks = rows // BLOCK
    glob_rows = 2 * GLOB
    rows_all = rows + glob_rows
    group_size = GROUP_BLOCKS // (2 * blocks)
    group_bits = group_size.bit_length() - 1
    seq_bits = seq_size.bit_length() - 1
    group_pos = seq_pos % group_size
    own_first = (group_pos * 2 + tp_pos) * own_glob

    def flip(value, bit):
        return lax.ppermute(value, "seq", [(s, s ^ (1 << bit)) for s in range(seq_size)])

    def swap(value):
        return lax.ppermute(value, "tp", [(0, 1), (1, 0)])

    rest = tuple(range(3, seq_bits))
    orders = {
        "one": ((0, 1, 2, *rest), (2, 0, 1, *rest)),
        "two": ((1, 0, 2, *rest), (0, 2, 1, *rest)),
        "three": ((0, 1, 2, *rest), (2, 0, 1, *rest)),
        "four": ((1, 0, 2, *rest), (0, 2, 1, *rest)),
    }
    place = [
        (seq_pos * 2 + tp_pos) * blocks,
        (seq_pos // group_size) * 2,
        own_first,
        jnp.int32(own_glob),
        group_pos,
        tp_pos,
    ]
    group_sides = len(place)
    place += [(seq_pos >> bit) & 1 for bit in range(group_bits)] + [tp_pos]
    job_sides = {}
    for name, (zero, one) in orders.items():
        job_sides[name] = len(place)
        place += [(seq_pos >> jnp.where(tp_pos == 0, a, b)) & 1 for a, b in zip(zero, one)]
    place = jnp.stack(place).astype(jnp.int32)

    def trade(value, name, step):
        zero, one = orders[name][0][step], orders[name][1][step]
        links = [(2 * s, 2 * (s ^ (1 << zero))) for s in range(seq_size)]
        links += [(2 * s + 1, 2 * (s ^ (1 << one)) + 1) for s in range(seq_size)]
        return lax.ppermute(value, ("seq", "tp"), links)

    gathered = jnp.stack([glob_tokens, grad_glob])[None]
    vecs, half_own = pack_vectors(
        [gain_attn, shift_attn, gain_ffn, shift_ffn, b_out, b_down], [b_query, b_value, b_up]
    )
    half_par = swap(half_own)
    halves = (half_own, half_par)
    weights = [w_query, w_key, w_value]
    weights += [swap(weight) for weight in weights]
    marks = ()
    for bit in range(group_bits):
        other = flip(gathered, bit)
        if bit == 1:
            qkv, turned, qkv_both = project(tokens, vecs, halves, weights, (gathered,))
            marks = (turned,)
        if bit == group_bits - 1:
            docs, augk, augq, mask, seen = layout(
                place, doc_blocks, doc_tail, rows_all, glob_rows, blocks, (gathered,)
            )
            marks = (augq,)
        gathered = stack_two(gathered, other, marks)
    x_glob, dz_all = order_rows(place, gathered, swap(gathered), grad_tokens)
    qkv_glob, turned_glob = project(x_glob, vecs, halves, [qkv_both])
    out_par = swap(w_out)
    up_par = swap(w_up)
    down_par = swap(w_down)

    mine, theirs = glob_forward(qkv, qkv_glob, augk, augq, seen, pairs)
    state = merge(mine, swap(theirs))
    outs = ()
    for bit in range(group_bits):
        other = flip(state, bit)
        first, end = pairs * bit // group_bits, pairs * (bit + 1) // group_bits
        outs = local_forward(
            docs, qkv, qkv_glob, augk, pairs, blocks, first, end - first, outs, (state,)
        )
        state = merge(state, other, (outs[1],))
    state_par = swap(state)
    high, lse = outs
    held = middle_local(high, tokens, w_out, out_par, vecs, (state,))
    middle, hidden, ffn_turned, high, lse_glob = middle_glob(
        state, state_par, x_glob, w_out, out_par, vecs, [*held, high]
    )

    def job(name, pairs):
        first, count = job_sides[name], seq_bits
        steps = [("start", first)]
        steps += [("split", first + step) for step in range(1, count)]
        steps += [("add", None)]
        steps += [("join", first + step) for step in range(count - 1, 0, -1)]
        order = [*range(count), *range(count - 1, -1, -1)]
        sends = [lambda value, step=step: trade(value, name, step) for step in order]
        return Chain(steps, sends, [array for pair in pairs for array in pair])

    def apart(value):
        return value

    part = units // 2
    acts, ups, grads = [], [[], []], []
    dn = None
    marks = []
    for which, (up, down, vec) in ((1, (up_par, down_par, half_par)), (0, (w_up, w_down, half_own))):
        for number in range(2):
            dn, act, grad, up_sum = ffn_part(
                hidden, ffn_turned, dz_all, up, vec, down, mask, number * part, part, dn, marks
            )
            grad = grad.reshape(2, -1, LANES)
            acts.append((act, down, number))
            ups[which].append(up_sum)
            grads.append(swap(grad) if which else grad)
            if not which and not number:
                one = job("one", [(grads[2], grads[0])])
                marks = turn(place, [one], (up_sum,))
    two = job("two", [(grads[3], grads[1])])
    marks = turn(place, [one, two], (up_sum,))

    d_mid, d_attn, delta, out_grad, mid_sums = middle_back(
        dn, middle, dz_all, high, w_out, out_par, vecs, mask, marks
    )
    out_grad = out_grad.reshape(2, 2, -1, LANES)
    out_got = Chain([("copy", None)], [swap], [out_grad[1]])
    marks = turn(place, [one, out_got], (mid_sums,))
    own = pairs // 2
    some = 2 * LANES
    spots = {0: 0, 1: 1, own: 2, own + 1: 3, 2: 4, own + 2: 5}
    places = ((0, 1, 4), (2, 3, 5))
    plan = (
        (0, (one, two)), (own, (one, two)), (1, (one, two)), (own + 1, (one, two)), (2, (two,)),
        (own + 2, (two,)),
    )
    grads = ()
    for number, (pair, chains) in enumerate(plan):
        if number == 4:
            carries = []
            for which in (1, 0):
                grad, carry = project_grad(
                    turned, turned_glob, *grads, qkv_both, vecs, which, 0, some, which, after=marks
                )
                carries.append(carry)
                if which:
                    got = swap(grad)
                    marks = [carry]
            three = job("three", [(grad, got), (out_grad[0], out_got.other)])
            marks = turn(place, [one, two, three], (carry,))
        grads = attention_back(
            docs, qkv, qkv_glob, d_attn, lse, lse_glob, delta, augk, augq, pairs, pair, spots[pair],
            grads, marks,
        )
        if pair == own + 2:
            chains = (*chains, three)
        marks = turn(place, chains, (grads[0],))
    for which in (1, 0):
        grad = project_grad(
            turned, turned_glob, *grads, qkv_both, vecs, which, some, LANES, 4 + which,
            carries[1 - which], mid_sums, ups[which], marks,
        )[0]
        if which:
            got = swap(grad)
            marks = turn(place, [three], (grad,))
    four = job("four", [(grad, got)])
    marks = turn(place, [three, four])

    back = glob_back(*grads, qkv_both, places, marks)
    sends = [lambda value, bit=bit: flip(value, bit) for bit in reversed(range(group_bits))] + [swap]
    numbers = [*reversed(range(group_sides, group_sides + group_bits)), group_sides + group_bits]
    steps = [("pick", numbers[0])] + [("split", number) for number in numbers[1:]]
    globs = Chain(steps, sends, [halved(back)])
    marks = turn(place, [four, three, globs])
    tokens_grad = input_back(*grads, qkv_both, tokens, d_mid, vecs, places, marks)
    marks = turn(place, [four, three, globs], (far(tokens_grad),))
    kinds = ()
    for number, chain in enumerate((one, two)):
        while chain.left:
            marks = turn(place, [chain], marks)
        name = ("one", "two")[number]
        kinds = ffn_unpack(
            place, job_sides[name], chain.stay, chain.other, dim, units, part, number, kinds, marks
        )
        chosen = (four, globs) if number else (four, three, globs)
        marks = turn(place, [c for c in chosen if c.left], (far(kinds[0]),))
    up_grad, down_grad = kinds
    marks = turn(place, [c for c in (four, three) if c.left], marks)
    glob_grad = glob_input(place, globs.stay, globs.other, glob_tokens, d_mid, vecs, marks)
    marks = turn(place, [c for c in (four, three) if c.left], (far(glob_grad),))
    while four.left or three.left:
        marks = turn(place, [c for c in (four, three) if c.left], marks)
    out_tokens, out_all = output_rows(
        place, middle, vecs, [a for a, _, _ in acts], [(w, n) for _, w, n in acts], own_glob, marks
    )
    out_glob = lax.dynamic_slice_in_dim(out_all, own_first, own_glob, 0)
    *kinds, w_out_grad = tail_unpack(
        place, job_sides["three"], three.stay, three.other, dim, half, 0, some
    )
    q_grad, k_grad, v_grad, small = tail_unpack(
        place, job_sides["four"], four.stay, four.other, dim, half, some, LANES, kinds
    )
    (
        gain_f_grad, shift_f_grad, out_bias, down_bias, gain_a_grad, shift_a_grad, b_query_grad,
        b_value_grad, b_up_grad,
    ) = finish(small, swap(small), [dim] * 6 + [half, half, units])
    return (
        out_tokens, out_glob, tokens_grad, glob_grad, q_grad, b_query_grad, k_grad,
        v_grad, b_value_grad, w_out_grad, out_bias, up_grad, b_up_grad, down_grad, down_bias,
        gain_a_grad, shift_a_grad, gain_f_grad, shift_f_grad,
    )


def solution(mesh):
    rows = P(("seq", "tp"), None)
    cols, part, whole = P(None, "tp"), P("tp"), P()
    lines = P("tp", None)
    return jax.shard_map(
        per_device,
        mesh=mesh,
        in_specs=(
            rows, rows, cols, part, cols, cols, part, lines, whole, cols, part, lines, whole,
            whole, whole, whole, whole, whole, whole, rows, rows,
        ),
        out_specs=(
            rows, rows, rows, rows, cols, part, cols, cols, part, lines, whole, cols, part, lines,
            whole, whole, whole, whole, whole,
        ),
        check_vma=False,
    )
```

```python
import functools

import jax
import jax.numpy as jnp
from jax import lax
from jax.experimental import pallas as pl
from jax.experimental.pallas import tpu as pltpu
from jax.sharding import PartitionSpec as P

HD = 64
BLOCK = 512
GLOB = 128
GROUP_BLOCKS = 32
EPS = 1e-05
SCALE = 0.125
NEG = -1e30
SHIFT = -10.0
FAINT = 1e-25
TILE = 256
PAIR = 2 * HD
LANES = 128
STATS = 16
HEAD_ROWS = 16
FFN_CHUNK = 256
WEIGHT = 1
F32 = jnp.float32
BF16 = jnp.bfloat16
VMEM_BYTES = 12 * 2**20


def nn(left, right):
    return jnp.dot(left, right, preferred_element_type=F32)


def nt(left, right):
    return lax.dot_general(left, right, (((1,), (1,)), ((), ())), preferred_element_type=F32)


def tn(left, right):
    return lax.dot_general(left, right, (((0,), (0,)), ((), ())), preferred_element_type=F32)


def normed(values):
    row_mean = jnp.mean(values, axis=-1, keepdims=True)
    centred = values - row_mean
    row_var = jnp.mean(centred * centred, axis=-1, keepdims=True)
    inv = lax.rsqrt(row_var + EPS)
    return centred * inv, inv


def norm_back(xhat, inv, gain_vec, cotangent):
    scaled = cotangent * gain_vec
    mean_one = jnp.mean(scaled, axis=-1, keepdims=True)
    mean_two = jnp.mean(scaled * xhat, axis=-1, keepdims=True)
    return inv * (scaled - mean_one - xhat * mean_two)


def full(shape):
    zeros = (0,) * len(shape)
    return pl.BlockSpec(shape, lambda *_: zeros, pipeline_mode=pl.Buffered(1))


ANY = pl.BlockSpec(memory_space=pl.ANY)


def far(array):
    return pltpu.with_memory_space_constraint(array, pltpu.HBM)


def launch(
    body, name, grid, operands, outs, work, prefetch=(), held=(), after=(), scratch=(), aliased=0
):
    arrays = [*prefetch, *(a for a, _ in operands), *held, *after]
    specs = [*(spec for _, spec in operands), *([ANY] * (len(held) + len(after)))]
    first = len(prefetch) + len(operands)
    spare = len(held) + len(after)

    def whole(*refs):
        return body(*refs[:first], *refs[first + spare :])

    return pl.pallas_call(
        whole,
        grid_spec=pltpu.PrefetchScalarGridSpec(
            num_scalar_prefetch=len(prefetch),
            grid=grid,
            in_specs=specs,
            out_specs=[out[2] for out in outs],
            scratch_shapes=list(scratch),
        ),
        out_shape=[(pltpu.HBM if out[3:] else jax.ShapeDtypeStruct)(out[0], out[1]) for out in outs],
        input_output_aliases={first + i: aliased + i for i in range(len(held))},
        compiler_params=pltpu.CompilerParams(
            vmem_limit_bytes=VMEM_BYTES, dimension_semantics=("arbitrary",) * len(grid)
        ),
        cost_estimate=work,
        name=name,
    )(*arrays)


def cost(flops, nbytes, trans=0):
    scale = WEIGHT if flops > 2**28 else 1
    return pl.CostEstimate(
        flops=int(scale * flops), bytes_accessed=int(scale * nbytes), transcendentals=int(trans)
    )


def head_lanes(head):
    lane = lax.broadcasted_iota(jnp.int32, (1, LANES), 1)
    here = jnp.where(lane < HD, 1.0, 0.0)
    mine = here if head == 0 else 1.0 - here
    return mine.astype(BF16), (1.0 - mine).astype(BF16)


def lane_one(slot):
    lane = lax.broadcasted_iota(jnp.int32, (1, LANES), 1)
    return jnp.where((lane == slot) | (lane == slot + HD), 1.0, 0.0).astype(BF16)


def layout_body(
    place_ref, blocks_ref, tails_ref, docs_ref, augk_ref, augq_ref, mask_ref, seen_ref
):
    first_block, group_first, own_first = place_ref[0], place_ref[1], place_ref[2]
    own_count = place_ref[3]
    count = augq_ref.shape[0]
    rows = augk_ref.shape[0] - count
    lane = lax.broadcasted_iota(jnp.int32, (1, LANES), 1)
    slot = jnp.where(lane < HD, lane, lane - HD)
    column = lax.broadcasted_iota(jnp.int32, (8, count), 1)
    seen = (column >= own_first) & (column < own_first + own_count)
    for block in range(rows // BLOCK):
        index = first_block + block
        start, doc, real = jnp.int32(0), jnp.int32(0), jnp.int32(BLOCK)
        for number in range(blocks_ref.shape[0]):
            end = start + blocks_ref[number]
            inside = jnp.logical_and(index >= start, index < end)
            doc = jnp.where(inside, number, doc)
            real = jnp.where(
                jnp.logical_and(inside, index == end - 1), tails_ref[number], real
            )
            start = end
        doc = doc - group_first
        docs_ref[block] = doc
        seen = seen | ((column >= doc * GLOB) & (column < (doc + 1) * GLOB))
        row = lax.broadcasted_iota(jnp.int32, (BLOCK, 1), 0)
        padded = row >= real
        shut = ((slot == 1) & (doc != 0)) | ((slot == 2) & (doc != 1))
        shut = jnp.where(shut, 1, 0) + jnp.where(padded & (slot < 3), 1, 0)
        augk_ref[block * BLOCK : (block + 1) * BLOCK, :] = jnp.where(
            shut > 0, NEG, jnp.where(slot < 3, SHIFT, 0.0)
        ).astype(BF16)
    row = lax.broadcasted_iota(jnp.int32, (count, 1), 0)
    late = row >= GLOB
    shut = ((slot == 1) & late) | ((slot == 2) & ~late) | (slot == 3)
    augk_ref[rows:, :] = jnp.where(shut, NEG, jnp.where(slot < 3, SHIFT, 0.0)).astype(BF16)
    owned = (row >= own_first) & (row < own_first + own_count)
    on = ((slot == 1) & ~late) | ((slot == 2) & late) | ((slot == 3) & ~owned)
    augq_ref[...] = jnp.where(on, 1.0, 0.0).astype(BF16)
    seen_ref[...] = jnp.where(seen, 1.0, 0.0)
    mask_ref[:rows, :] = jnp.ones((rows, 1), F32)
    mask_ref[rows:, :] = jnp.where(owned, 1.0, 0.0)


def layout(place, doc_blocks, doc_tail, rows_all, count, blocks, after=()):
    smem = pl.BlockSpec(memory_space=pltpu.SMEM)
    return launch(
        layout_body,
        "layout",
        (1,),
        [],
        [
            ((blocks,), jnp.int32, smem),
            ((rows_all, LANES), BF16, full((rows_all, LANES))),
            ((count, LANES), BF16, full((count, LANES))),
            ((rows_all, 1), F32, full((rows_all, 1))),
            ((8, count), F32, full((8, count))),
        ],
        cost(0, rows_all * LANES * 4),
        prefetch=(place, doc_blocks, doc_tail),
        after=after,
    )


def pack_body(*refs):
    vecs_ref, half_ref = refs[-2:]
    for row, ref in enumerate(refs[:6]):
        vecs_ref[row : row + 1, :] = ref[...].reshape(1, -1)
    vecs_ref[6:, :] = jnp.zeros((2, vecs_ref.shape[1]), F32)
    half_ref[...] = jnp.zeros(half_ref.shape, F32)
    first = 0
    for ref in refs[6:9]:
        count = ref.shape[0]
        half_ref[0:1, first : first + count] = ref[...].reshape(1, -1)
        first += count


def pack_vectors(vectors, parts):
    arrays = [far(array) for array in (*vectors, *parts)]
    dim = vectors[0].shape[0]
    width = sum(part.shape[0] for part in parts)
    return launch(
        pack_body,
        "pack_vectors",
        (1,),
        [(a, full(a.shape)) for a in arrays],
        [((8, dim), F32, full((8, dim))), ((8, width), F32, full((8, width)))],
        cost(0, 32 * (dim + width)),
    )


def order_body(place_ref, mine_ref, theirs_ref, grads_ref, x_ref, dz_ref):
    step = pl.program_id(0)
    last = pl.num_programs(0) - 1
    chips, _, own, _ = mine_ref.shape

    @pl.when(step < last)
    def _():
        dz_ref[...] = grads_ref[...]

    @pl.when(step == last)
    def _():
        for chip in range(chips):
            for side, ref in enumerate((mine_ref, theirs_ref)):
                spot = (place_ref[4] ^ chip) * 2 + (place_ref[5] ^ side)
                here = pl.ds(pl.multiple_of(spot * own, own), own)
                x_ref[here, :] = ref[chip, 0]
                dz_ref[here, :] = ref[chip, 1]


def order_rows(place, mine, theirs, grads, after=()):
    chips, _, own, dim = mine.shape
    count = chips * 2 * own
    tiles = grads.shape[0] // count
    return launch(
        order_body,
        "order_rows",
        (tiles + 1,),
        [
            (mine, full(mine.shape)),
            (theirs, full(mine.shape)),
            (grads, pl.BlockSpec((count, dim), lambda i, place: (jnp.minimum(i, tiles - 1), 0))),
        ],
        [
            ((count, dim), BF16, full((count, dim))),
            (
                (grads.shape[0] + count, dim),
                BF16,
                pl.BlockSpec((count, dim), lambda i, place: (i, 0)),
            ),
        ],
        cost(0, 4 * grads.size),
        prefetch=(place,),
        after=after,
    )


def stack_body(left_ref, right_ref, out_ref):
    count = left_ref.shape[0]
    out_ref[:count] = left_ref[...]
    out_ref[count:] = right_ref[...]


def stack_two(left, right, after=()):
    shape = (2 * left.shape[0], *left.shape[1:])
    return launch(
        stack_body,
        "stack_two",
        (1,),
        [(left, full(left.shape)), (right, full(right.shape))],
        [(shape, left.dtype, full(shape))],
        cost(0, left.size * 8),
        after=after,
    )[0]


def project_body(x_ref, vecs_ref, own_vec_ref, par_vec_ref, *rest, given):
    qkv_ref, turned_ref = rest[-2 - given : len(rest) - given]
    if given:
        both_ref = rest[-1]
        parts = rest[:6]
        width = parts[0].shape[1]

        @pl.when(pl.program_id(0) == 0)
        def _():
            for number, part in enumerate(parts):
                half, kind = divmod(number, 3)
                both_ref[half, :, kind * width : (kind + 1) * width] = part[...]

    else:
        both_ref = rest[0]
    xhat, _ = normed(x_ref[...].astype(F32))
    hidden = (xhat * vecs_ref[0:1, :] + vecs_ref[1:2, :]).astype(BF16)
    turned_ref[...] = hidden.T
    width = both_ref.shape[2]
    third = width // 3
    for half, vec_ref in enumerate((own_vec_ref, par_vec_ref)):
        first = half * width
        made = nn(hidden, both_ref[half])
        bias = vec_ref[0:1, : 2 * third]
        qkv_ref[:, first : first + third] = (
            (made[:, :third] + bias[:, :third]) * SCALE
        ).astype(BF16)
        qkv_ref[:, first + third : first + 2 * third] = made[:, third : 2 * third].astype(BF16)
        qkv_ref[:, first + 2 * third : first + width] = (
            made[:, 2 * third :] + bias[:, third:]
        ).astype(BF16)


def project(x, vecs, halves, weights, after=()):
    rows, dim = x.shape
    given = len(weights) > 1
    half = 3 * weights[0].shape[1] if given else weights[0].shape[2]
    width = 2 * half
    both = (2, dim, half)
    return launch(
        functools.partial(project_body, given=int(given)),
        "project",
        (rows // TILE,),
        [
            (far(x) if given else x, pl.BlockSpec((TILE, dim), lambda i: (i, 0))),
            (vecs, full(vecs.shape)),
            (halves[0], full(halves[0].shape)),
            (halves[1], full(halves[1].shape)),
        ]
        + [(far(w), full(w.shape)) for w in weights],
        [
            ((rows, width), BF16, pl.BlockSpec((TILE, width), lambda i: (i, 0))),
            ((dim, rows), BF16, pl.BlockSpec((dim, TILE), lambda i: (0, i))),
        ]
        + ([(both, BF16, full(both), True)] if given else []),
        cost(2 * rows * dim * width, 2 * (rows * (2 * dim + width) + dim * width)),
        after=after,
    )


def pair_column(kind, pairs):
    half = pairs // 2
    return lambda p: (p // half) * 3 * half + kind * half + p % half


def write_stats(out_ref, head, lse):
    first = lse.astype(BF16).astype(F32)
    second = (lse - first).astype(BF16).astype(F32)
    third = lse - first - second
    row = lax.broadcasted_iota(jnp.int32, (STATS, lse.shape[1]), 0)
    held = jnp.where(row == 0, first, jnp.where(row == 1, second, jnp.where(row == 2, third, 0.0)))
    out_ref[head, HD : HD + STATS, :] = held.astype(BF16)


def read_stats(ref, head):
    held = ref[head, HD : HD + STATS, :].astype(F32)
    return held[0:1] + held[1:2] + held[2:3]


def summed_up(scores, values, seen=None):
    weights = jnp.exp(scores)
    total = jnp.sum(weights, axis=0, keepdims=True)
    summed = nn(values, weights.astype(BF16))
    faint = total < FAINT
    if seen is not None:
        faint = faint & (seen > 0.0)
    return summed, total, jnp.max(jnp.where(faint, 1.0, 0.0))


def summed_faint(scores, values):
    top = jnp.max(scores, axis=0, keepdims=True)
    weights = jnp.exp(scores - top)
    total = jnp.sum(weights, axis=0, keepdims=True)
    return nn(values, weights.astype(BF16)) / total, top + jnp.log(total)


def glob_forward_body(
    q_ref, k_ref, v_ref, kg_ref, vg_ref, augk_ref, augq_ref, seen_ref, own_ref, par_ref
):
    queries = q_ref[...]
    keys = jnp.concatenate([k_ref[...], kg_ref[...]], 0)
    values_turned = jnp.concatenate([v_ref[...], vg_ref[...]], 0).T
    seen = seen_ref[0:1, :]
    half = pl.num_programs(0) // 2

    def write(head, summed, lse):
        for ref, here in ((par_ref, pl.program_id(0) < half), (own_ref, pl.program_id(0) >= half)):

            @pl.when(here)
            def _(ref=ref):
                ref[head, :HD, :] = summed
                write_stats(ref, head, lse)

    both = []
    for head in range(2):
        mine, other = head_lanes(head)
        key_head = keys * mine + augk_ref[...] * other
        query_head = queries * mine + augq_ref[...] * other
        both.append(nt(key_head, query_head))
    results = []
    for head in range(2):
        values = values_turned[head * HD : (head + 1) * HD, :]
        summed, total, faint = summed_up(both[head], values, seen)
        some = total > 0.0
        safe = jnp.where(some, total, 1.0)
        results.append((summed / safe, jnp.where(some, jnp.log(safe), NEG), faint))
    for head, (summed, lse, _) in enumerate(results):
        write(head, summed.astype(BF16), lse)
    for head, (_, _, faint) in enumerate(results):

        @pl.when(faint > 0.0)
        def _(head=head):
            values = values_turned[head * HD : (head + 1) * HD, :]
            summed, lse = summed_faint(both[head], values)
            write(head, summed.astype(BF16), jnp.where(seen > 0.0, lse, NEG))


def glob_forward(qkv, qkv_glob, augk, augq, seen, pairs):
    count = augq.shape[0]
    half = pairs // 2

    def block(array, kind):
        column = pair_column(kind, pairs)
        return (
            array,
            pl.BlockSpec((array.shape[0], LANES), lambda p: (0, column((p + half) % pairs))),
        )

    work = 2 * pairs * augk.shape[0] * count
    shape = (pairs, HD + STATS, count)
    size = (2, HD + STATS, count)
    return launch(
        glob_forward_body,
        "glob_forward",
        (pairs,),
        [
            block(qkv_glob, 0),
            block(qkv, 1),
            block(qkv, 2),
            block(qkv_glob, 1),
            block(qkv_glob, 2),
            (augk, full(augk.shape)),
            (augq, full(augq.shape)),
            (seen, full(seen.shape)),
        ],
        [
            (shape, BF16, pl.BlockSpec(size, lambda p: (jnp.maximum(p - half, 0), 0, 0))),
            (shape, BF16, pl.BlockSpec(size, lambda p: (jnp.minimum(p, half - 1), 0, 0))),
        ],
        cost(work * 2 * 512, qkv.size * 2, work),
    )


def merge_body(left_ref, right_ref, out_ref):
    for head in range(left_ref.shape[0]):
        lse_left, lse_right = read_stats(left_ref, head), read_stats(right_ref, head)
        top = jnp.maximum(lse_left, lse_right)
        weight_left, weight_right = jnp.exp(lse_left - top), jnp.exp(lse_right - top)
        total = weight_left + weight_right
        out_left = left_ref[head, :HD, :].astype(F32)
        out_right = right_ref[head, :HD, :].astype(F32)
        merged = (out_left * weight_left + out_right * weight_right) / total
        out_ref[head, :HD, :] = merged.astype(BF16)
        write_stats(out_ref, head, top + jnp.log(total))


def merge(left, right, after=()):
    spec = full(left.shape)
    return launch(
        merge_body, "merge", (1,), [(left, spec), (right, spec)], [(left.shape, BF16, spec)],
        cost(left.size * 8, left.size * 6), after=after,
    )[0]


def local_forward_body(docs_ref, q_ref, k_ref, v_ref, kg_ref, vg_ref, augk_ref, augg_ref, out_ref, lse_ref):
    keys = jnp.concatenate([k_ref[...], kg_ref[...]], 0)
    values_turned = jnp.concatenate([v_ref[...], vg_ref[...]], 0).T
    bias = jnp.concatenate([augk_ref[...], augg_ref[...]], 0)
    both = []
    for head in range(2):
        mine, other = head_lanes(head)
        key_head = keys * mine + bias * other
        query_head = q_ref[...] * mine + lane_one(0) * other
        both.append(nt(key_head, query_head))
    outs, faints = [], []
    for head in range(2):
        values = values_turned[head * HD : (head + 1) * HD, :]
        summed, total, faint = summed_up(both[head], values)
        outs.append(summed / total)
        faints.append(faint)
        lse_ref[0, 0, head : head + 1, :] = jnp.log(total)
    out_ref[...] = jnp.concatenate(outs, 0).T.astype(BF16)

    @pl.when(faints[0] + faints[1] > 0.0)
    def _():
        again = []
        for head in range(2):
            values = values_turned[head * HD : (head + 1) * HD, :]
            summed, lse = summed_faint(both[head], values)
            again.append(summed)
            lse_ref[0, 0, head : head + 1, :] = lse
        out_ref[...] = jnp.concatenate(again, 0).T.astype(BF16)


def local_forward(docs, qkv, qkv_glob, augk, pairs, blocks, first, count, held=(), after=()):
    rows_all = augk.shape[0]
    glob_first = blocks * BLOCK // GLOB

    def block(kind):
        column = pair_column(kind, pairs)
        return (
            qkv,
            pl.BlockSpec((BLOCK, LANES), lambda b, p, docs: (b, column(p + first))),
        )

    def glob_block(kind):
        column = pair_column(kind, pairs)
        return (
            qkv_glob,
            pl.BlockSpec((GLOB, LANES), lambda b, p, docs: (docs[b], column(p + first))),
        )

    work = 2 * count * blocks * BLOCK * (BLOCK + GLOB)
    width = pairs * LANES
    straight = pl.BlockSpec((BLOCK, LANES), lambda b, p, docs: (b, p + first))
    return launch(
        local_forward_body,
        "local_forward",
        (blocks, count),
        [
            block(0),
            block(1),
            block(2),
            glob_block(1),
            glob_block(2),
            (augk, pl.BlockSpec((BLOCK, LANES), lambda b, p, docs: (b, 0))),
            (augk, pl.BlockSpec((GLOB, LANES), lambda b, p, docs: (glob_first, 0))),
        ],
        [
            ((rows_all, width), BF16, straight),
            (
                (blocks, pairs, 2, BLOCK),
                F32,
                pl.BlockSpec((1, 1, 2, BLOCK), lambda b, p, docs: (b, p + first, 0, 0)),
            ),
        ],
        cost(work * 2 * 512, count * rows_all * LANES * 12, work),
        prefetch=(docs,),
        held=held,
        after=after,
    )


def middle_of(out_high, x, own_ref, par_ref, vecs_ref):
    half = own_ref.shape[0]
    branch = nn(out_high[:, :half], own_ref[...]) + nn(out_high[:, half:], par_ref[...])
    middle = x.astype(F32) + branch + vecs_ref[4:5, :]
    xhat, _ = normed(middle)
    hidden = (xhat * vecs_ref[2:3, :] + vecs_ref[3:4, :]).astype(BF16)
    return middle, hidden


def middle_body(out_ref, x_ref, own_ref, par_ref, vecs_ref, mid_ref, hid_ref, turned_ref):
    middle, hidden = middle_of(out_ref[...], x_ref[...], own_ref, par_ref, vecs_ref)
    mid_ref[...] = middle
    hid_ref[...] = hidden
    turned_ref[...] = hidden.T


def middle_local(out_high, x, w_own, w_par, vecs, after=()):
    rows_all, dim = out_high.shape
    rows = x.shape[0]
    row = pl.BlockSpec((TILE, dim), lambda i: (i, 0))
    return launch(
        middle_body,
        "middle_local",
        (rows // TILE,),
        [
            (out_high, row),
            (far(x), row),
            (w_own, full(w_own.shape)),
            (w_par, full(w_par.shape)),
            (vecs, full(vecs.shape)),
        ],
        [
            ((rows_all, dim), F32, row, True),
            ((rows_all, dim), BF16, row),
            ((dim, rows_all), BF16, pl.BlockSpec((dim, TILE), lambda i: (0, i))),
        ],
        cost(2 * rows * dim * dim, 12 * rows * dim + 2 * dim * dim),
        after=after,
    )


def middle_glob_body(
    own_out_ref, par_out_ref, x_ref, own_ref, par_ref, vecs_ref,
    mid_ref, hid_ref, turned_ref, high_ref, lse_ref,
):
    heads = own_out_ref.shape[0]
    parts = [own_out_ref[head, :HD, :] for head in range(heads)]
    parts += [par_out_ref[head, :HD, :] for head in range(heads)]
    turned = jnp.concatenate(parts, 0)
    high = turned.T
    high_ref[...] = high
    stats = [read_stats(own_out_ref, head) for head in range(heads)]
    stats += [read_stats(par_out_ref, head) for head in range(heads)]
    spare = lse_ref.shape[0] - 2 * heads
    lse_ref[...] = jnp.concatenate(stats + [jnp.zeros((spare, x_ref.shape[0]), F32)], 0)
    middle, hidden = middle_of(high, x_ref[...], own_ref, par_ref, vecs_ref)
    mid_ref[...] = middle
    hid_ref[...] = hidden
    turned_ref[...] = hidden.T


def middle_glob(own_out, par_out, x, w_own, w_par, vecs, held):
    rows, dim = x.shape
    first = held[0].shape[0] // rows - 1
    row = pl.BlockSpec((rows, dim), lambda i: (first, 0))
    col = pl.BlockSpec((dim, rows), lambda i: (0, first))
    operands = [own_out, par_out, x, w_own, w_par, vecs]
    specs = [row, row, col, row]
    return launch(
        middle_glob_body,
        "middle_glob",
        (1,),
        [(a, full(a.shape)) for a in operands],
        [(h.shape, h.dtype, spec, *pin) for h, spec, pin in zip(held, specs, ((True,), (), (), ()))]
        + [((HEAD_ROWS, rows), F32, full((HEAD_ROWS, rows)))],
        cost(2 * rows * dim * dim, 12 * rows * dim + 2 * dim * dim),
        held=held,
    )


def ffn_body(
    hid_ref, turned_ref, dz_ref, up_ref, bias_ref, down_ref, mask_ref, *rest, chunks
):
    dn_in_ref = rest[0] if len(rest) == 8 else None
    dnorm_ref, act_ref, grads_ref, bias_grad_ref, act_s, dup_s, sum_s = rest[-7:]
    step = pl.program_id(0)
    rows_all, dim = hid_ref.shape
    chunk = bias_grad_ref.shape[1]
    tail = slice(rows_all - mask_ref.shape[0], rows_all)

    @pl.when(step < chunks)
    def _():
        cols = pl.ds(pl.multiple_of(step * chunk, chunk), chunk)
        up = nn(hid_ref[...], up_ref[:, cols]) + bias_ref[0:1, :]
        share = 0.5 * (1.0 + lax.erf(up * (2.0**-0.5)))
        density = jnp.exp(up * up * -0.5) * 0.3989422804014327
        active = (up * share).astype(BF16)
        slope = share + up * density
        d_up = (nt(dz_ref[...], down_ref[cols, :]) * slope).astype(BF16)
        act_ref[...] = active
        dup_s[:, cols] = d_up
        act_s[...] = active
        sum_s[...] = d_up
        mask = mask_ref[...]
        act_s[tail, :] = (active[tail].astype(F32) * mask).astype(BF16)
        sum_s[tail, :] = (d_up[tail].astype(F32) * mask).astype(BF16)
        bias_grad_ref[...] = jnp.sum(sum_s[...].astype(F32), axis=0, keepdims=True)
        up_grad = nn(turned_ref[...], sum_s[...]).astype(BF16)
        down_grad = tn(act_s[...], dz_ref[...]).astype(BF16)
        place = 0
        for grad in (up_grad, down_grad):
            rows = grad.shape[0]
            for col in range(grad.shape[1] // LANES):
                grads_ref[0, place : place + rows, :] = grad[:, col * LANES : (col + 1) * LANES]
                place += rows

    @pl.when(step >= chunks)
    def _():
        start = pl.multiple_of((step - chunks) * TILE, TILE)
        made = nt(dup_s[pl.ds(start, TILE), :], up_ref[...])
        dnorm_ref[...] = made if dn_in_ref is None else made + dn_in_ref[...]


def ffn_part(hidden, turned, dz, w_up, vec, w_down, mask, first, units, dn_in=None, after=()):
    rows_all, dim = hidden.shape
    half = w_up.shape[1]
    chunk = min(FFN_CHUNK, units)
    chunks = units // chunk
    skip = first // units
    packed = 2 * chunk * dim // LANES
    bias_first = (vec.shape[1] - half + first) // chunk

    def now(j):
        return jnp.minimum(j, chunks - 1)

    row = pl.BlockSpec((TILE, dim), lambda j: (jnp.maximum(j - chunks, 0), 0))
    tail = mask.shape[0] // TILE - 1
    one = pl.Buffered(1)
    operands = [
        (hidden, full(hidden.shape)),
        (turned, full(turned.shape)),
        (dz, full(dz.shape)),
        (w_up, pl.BlockSpec((dim, units), lambda j: (0, skip), pipeline_mode=one)),
        (vec, pl.BlockSpec((vec.shape[0], chunk), lambda j: (0, bias_first + now(j)))),
        (w_down, pl.BlockSpec((units, dim), lambda j: (skip, 0), pipeline_mode=one)),
        (mask, pl.BlockSpec((TILE, 1), lambda j: (tail, 0))),
    ]
    if dn_in is not None:
        operands.append((dn_in, row))
    return launch(
        functools.partial(ffn_body, chunks=chunks),
        "ffn_part",
        (chunks + rows_all // TILE,),
        operands,
        [
            ((rows_all, dim), F32, row),
            ((rows_all, units), BF16, pl.BlockSpec((rows_all, chunk), lambda j: (0, now(j))), True),
            ((chunks, packed, LANES), BF16, pl.BlockSpec((1, packed, LANES), lambda j: (now(j), 0, 0))),
            ((1, units), F32, pl.BlockSpec((1, chunk), lambda j: (0, now(j)))),
        ],
        cost(10 * rows_all * dim * units, rows_all * dim * 14 + units * dim * 8, 2 * rows_all * units),
        after=after,
        scratch=[
            pltpu.VMEM((rows_all, chunk), BF16),
            pltpu.VMEM((rows_all, units), BF16),
            pltpu.VMEM((rows_all, chunk), BF16),
        ],
    )


def output_body(place_ref, mid_ref, vecs_ref, *rest):
    out_ref, glob_ref = rest[-2:]
    parts = len(rest) // 2 - 1
    made = mid_ref[...] + vecs_ref[5:6, :]
    for part in range(parts):
        made = made + nn(rest[part][...], rest[parts + part][...])
    step = pl.program_id(0)
    last = pl.num_programs(0) - 1

    @pl.when(step < last)
    def _():
        out_ref[...] = made.astype(BF16)

    @pl.when(step == last)
    def _():
        glob_ref[...] = made.astype(BF16)


def output_rows(place, middle, vecs, acts, weights, own, after=()):
    rows_all, dim = middle.shape
    tiles = rows_all // TILE
    rows = rows_all - TILE
    row = pl.BlockSpec((TILE, dim), lambda i, place: (i, 0))
    operands = [(far(middle), row), (vecs, full(vecs.shape))]
    operands += [
        (far(act), pl.BlockSpec((TILE, act.shape[1]), lambda i, place: (i, 0))) for act in acts
    ]
    for act, (weight, number) in zip(acts, weights):
        operands.append(
            (
                far(weight),
                pl.BlockSpec(
                    (act.shape[1], dim),
                    lambda i, place, number=number: (number, 0),
                    pipeline_mode=pl.Buffered(1),
                ),
            )
        )
    units = sum(act.shape[1] for act in acts)
    out, glob = launch(
        output_body,
        "output_rows",
        (tiles,),
        operands,
        [
            ((rows, dim), BF16, pl.BlockSpec((TILE, dim), lambda i, place: (jnp.minimum(i, tiles - 2), 0))),
            ((TILE, dim), BF16, full((TILE, dim))),
        ],
        cost(2 * rows_all * dim * units, rows_all * (units * 2 + dim * 6) + units * dim * 2),
        prefetch=(place,),
        after=after,
    )
    return out, glob


def middle_back_body(
    dn_ref, mid_ref, dz_ref, high_ref, own_ref, par_ref, vecs_ref, mask_ref,
    dmid_ref, dattn_ref, delta_ref, grads_ref, sums_ref, acc_s,
):
    step = pl.program_id(0)
    dim = mid_ref.shape[1]
    half = own_ref.shape[0]
    xhat, inv = normed(mid_ref[...])
    dn = dn_ref[...]
    dz = dz_ref[...].astype(F32)
    d_mid = dz + norm_back(xhat, inv, vecs_ref[2:3, :], dn)
    dmid_ref[...] = d_mid
    d_branch = d_mid.astype(BF16)
    for part, weight in enumerate((own_ref, par_ref)):
        dattn_ref[:, part * half : (part + 1) * half] = nt(d_branch, weight[...]).astype(BF16)
    product = dattn_ref[...].astype(F32) * high_ref[...].astype(F32)
    first = product.astype(BF16)
    second = (product - first.astype(F32)).astype(BF16)
    head = lax.broadcasted_iota(jnp.int32, (delta_ref.shape[0], dim), 0)
    column = lax.broadcasted_iota(jnp.int32, (delta_ref.shape[0], dim), 1)
    picked = jnp.where((column >= head * HD) & (column < (head + 1) * HD), 1.0, 0.0).astype(BF16)
    delta_ref[...] = nt(picked, first) + nt(picked, second)
    mask = mask_ref[...]
    masked = (d_branch.astype(F32) * mask).astype(BF16)
    made = tn(high_ref[...], masked)
    sums = [
        jnp.sum(dn * xhat * mask, axis=0, keepdims=True),
        jnp.sum(dn * mask, axis=0, keepdims=True),
        jnp.sum(masked.astype(F32), axis=0, keepdims=True),
        jnp.sum(dz * mask, axis=0, keepdims=True),
    ]
    sums = jnp.concatenate(sums + [jnp.zeros((4, dim), F32)], 0)

    @pl.when(step == 0)
    def _():
        acc_s[...] = made
        sums_ref[...] = sums

    @pl.when(step > 0)
    def _():
        acc_s[...] += made
        sums_ref[...] += sums

    @pl.when(step == pl.num_programs(0) - 1)
    def _():
        for part in range(2):
            for col in range(dim // LANES):
                grads_ref[part, col * half : (col + 1) * half, :] = acc_s[
                    part * half : (part + 1) * half, col * LANES : (col + 1) * LANES
                ].astype(BF16)


def middle_back(dn, middle, dz, high, w_own, w_par, vecs, mask, after=()):
    rows_all, dim = middle.shape
    row = pl.BlockSpec((TILE, dim), lambda i: (i, 0))
    packed = w_own.size // LANES
    return launch(
        middle_back_body,
        "middle_back",
        (rows_all // TILE,),
        [
            (dn, row),
            (middle, row),
            (dz, row),
            (high, row),
            (w_own, full(w_own.shape)),
            (w_par, full(w_par.shape)),
            (vecs, full(vecs.shape)),
            (mask, pl.BlockSpec((TILE, 1), lambda i: (i, 0))),
        ],
        [
            ((rows_all, dim), F32, row, True),
            ((rows_all, dim), BF16, row),
            ((HEAD_ROWS, rows_all), F32, pl.BlockSpec((HEAD_ROWS, TILE), lambda i: (0, i))),
            ((2, packed, LANES), BF16, full((2, packed, LANES))),
            ((8, dim), F32, full((8, dim))),
        ],
        cost(4 * rows_all * dim * dim, rows_all * dim * 24),
        after=after,
        scratch=[pltpu.VMEM((dim, dim), F32)],
    )


def attention_back_body(
    docs_ref, ql_ref, kl_ref, vl_ref, qg_ref, kg_ref, vg_ref, do_ref, lse_ref, lseg_ref, delta_ref,
    augk_ref, augq_ref, dq_ref, dk_ref, dv_ref, q_ref, key_s, value_s, turned_s, dk_s, dv_s, *, first,
):
    pair = pl.program_id(0) + first
    rows_all = q_ref.shape[0]
    count = augq_ref.shape[0]
    local_rows = rows_all - count
    blocks = local_rows // BLOCK
    q_ref[:local_rows, :] = ql_ref[...]
    q_ref[local_rows:, :] = qg_ref[...]
    turned_s[:, :local_rows] = kl_ref[...].T
    turned_s[:, local_rows:] = kg_ref[...].T
    dk_s[...] = jnp.zeros_like(dk_s)
    dv_s[...] = jnp.zeros_like(dv_s)
    dq_parts = [[] for _ in range(blocks + 1)]
    for head in range(2):
        mine, other = head_lanes(head)
        key_s[:local_rows, :] = kl_ref[...] * mine + augk_ref[:local_rows, :] * other
        key_s[local_rows:, :] = kg_ref[...] * mine + augk_ref[local_rows:, :] * other
        value_s[:local_rows, :] = vl_ref[...] * mine
        value_s[local_rows:, :] = vg_ref[...] * mine
        head_rows = slice(head * HD, (head + 1) * HD)
        index = 2 * pair + head

        def grads(key_cat, value_cat, turned_cat, query_rows, aug, lse):
            queries = q_ref[query_rows, :] * mine
            douts = do_ref[query_rows, :] * mine
            delta = delta_ref[pl.ds(index, 1), query_rows]
            probs = jnp.exp(nt(key_cat, queries + aug * other) - lse)
            d_scores = (probs * (nt(value_cat, douts) - delta)).astype(BF16)
            d_key = nn(d_scores, queries)
            d_value = nn(probs.astype(BF16), douts)
            return nn(turned_cat, d_scores), d_key, d_value

        for block in range(blocks):
            rows = slice(block * BLOCK, (block + 1) * BLOCK)
            start = pl.multiple_of(local_rows + docs_ref[block] * GLOB, GLOB)
            doc_rows = pl.ds(start, GLOB)
            key_cat = jnp.concatenate([key_s[rows, :], key_s[doc_rows, :]], 0)
            value_cat = jnp.concatenate([value_s[rows, :], value_s[doc_rows, :]], 0)
            turned_cat = jnp.concatenate(
                [turned_s[head_rows, rows], turned_s[head_rows, doc_rows]], 1
            )
            d_query, d_key, d_value = grads(
                key_cat, value_cat, turned_cat, rows, lane_one(0), lse_ref[block, 0, head : head + 1, :]
            )
            dq_parts[block].append(d_query)
            dk_s[rows, :] += d_key[:BLOCK]
            dk_s[doc_rows, :] += d_key[BLOCK:]
            dv_s[rows, :] += d_value[:BLOCK]
            dv_s[doc_rows, :] += d_value[BLOCK:]
        rows = slice(local_rows, rows_all)
        d_query, d_key, d_value = grads(
            key_s[...], value_s[...], turned_s[head_rows, :], rows, augq_ref[...],
            lseg_ref[pl.ds(index, 1), :],
        )
        dq_parts[blocks].append(d_query)
        dk_s[...] += d_key
        dv_s[...] += d_value
    for block in range(blocks + 1):
        begin = block * BLOCK
        made = jnp.concatenate(dq_parts[block], 0).T
        dq_ref[begin : begin + made.shape[0], :] = (
            made.astype(BF16).astype(F32) * SCALE
        ).astype(BF16)
    dk_ref[...] = dk_s[...].astype(BF16)
    dv_ref[...] = dv_s[...].astype(BF16)


def attention_back(
    docs, qkv, qkv_glob, d_attn, lse, lse_glob, delta, augk, augq, pairs, first, spot, held=(),
    after=(),
):
    number = 1
    rows_all = augk.shape[0]
    count = augq.shape[0]
    blocks = (rows_all - count) // BLOCK

    def block(array, kind):
        column = pair_column(kind, pairs)
        return (
            array,
            pl.BlockSpec((array.shape[0], LANES), lambda p, docs: (0, column(p + first))),
        )

    straight = pl.BlockSpec((rows_all, LANES), lambda p, docs: (0, p + first))
    work = 2 * number * (blocks * BLOCK * (BLOCK + GLOB) + rows_all * count)
    return launch(
        functools.partial(attention_back_body, first=first),
        "attention_back",
        (number,),
        [
            block(qkv, 0),
            block(qkv, 1),
            block(qkv, 2),
            block(qkv_glob, 0),
            block(qkv_glob, 1),
            block(qkv_glob, 2),
            (d_attn, straight),
            (lse, pl.BlockSpec((blocks, 1, 2, BLOCK), lambda p, docs: (0, p + first, 0, 0))),
            (lse_glob, full(lse_glob.shape)),
            (delta, full(delta.shape)),
            (augk, full(augk.shape)),
            (augq, full(augq.shape)),
        ],
        [((rows_all, pairs * LANES), BF16, pl.BlockSpec((rows_all, LANES), lambda p, docs: (0, spot)))] * 3,
        cost(work * 5 * 512, number * rows_all * LANES * 14, work),
        prefetch=(docs,),
        held=held,
        after=after,
        scratch=[
            pltpu.VMEM((rows_all, LANES), BF16),
            pltpu.VMEM((rows_all, LANES), BF16),
            pltpu.VMEM((rows_all, LANES), BF16),
            pltpu.VMEM((LANES, rows_all), BF16),
            pltpu.VMEM((rows_all, LANES), F32),
            pltpu.VMEM((rows_all, LANES), F32),
        ],
    )


def project_grad_body(
    turned_ref, turned_glob_ref, dq_ref, dk_ref, dv_ref, weight_ref, vecs_ref, *rest, first, last, shared
):
    dim, local_rows = turned_ref.shape
    width = dq_ref.shape[1]
    third = weight_ref.shape[1] // 3
    cols = width // LANES
    cut = dim // 2
    count = 3 * cols
    if last:
        carry_ref, mid_ref, *up_refs, grads_ref = rest
    else:
        grads_ref, next_ref = rest
    ones = jnp.ones((8, width), BF16)
    sums, dots, shifts = [], None, None
    for kind, ref in enumerate((dq_ref, dk_ref, dv_ref)):
        made = nn(turned_ref[...], ref[:local_rows, :]) + nn(turned_glob_ref[...], ref[local_rows:, :])
        begin = kind * third + first
        weight = weight_ref[:, begin : begin + width]
        total = jnp.sum(ref[...].astype(F32), axis=0, keepdims=True)
        sums.append(total)
        scaled = made * weight.astype(F32)
        high = scaled.astype(BF16)
        low = (scaled - high.astype(F32)).astype(BF16)
        dot = nt(ones, high) + nt(ones, low)
        high = total.astype(BF16).astype(F32)
        low = (total - high).astype(BF16).astype(F32)
        parts = jnp.concatenate([high, low, jnp.zeros((6, width), F32)], 0)
        shift = jnp.sum(nt(parts.astype(BF16), weight), axis=0, keepdims=True)
        dots = dot if dots is None else dots + dot
        shifts = shift if shifts is None else shifts + shift
        rounded = made.astype(BF16)
        for col in range(cols):
            for part in range(2):
                number = 2 * (kind * cols + col) + part
                spot = number % count * cut
                grads_ref[number // count, spot : spot + cut, :] = rounded[
                    part * cut : (part + 1) * cut, col * LANES : (col + 1) * LANES
                ]
    if not last:
        row = jnp.concatenate([sums[0], sums[2], jnp.zeros((1, dim - 2 * width), F32)], 1)
        next_ref[...] = jnp.concatenate([dots[0:1, :], shifts, row, jnp.zeros((5, dim), F32)], 0)
        return
    dots = dots[0:1, :] + carry_ref[0:1, :]
    shifts = shifts + carry_ref[1:2, :]
    gains = (dots - vecs_ref[1:2, :] * shifts) / vecs_ref[0:1, :]
    small = [mid_ref[row : row + 1, :] * shared for row in range(4)]
    small += [gains, shifts]
    for number, total in enumerate((sums[0], sums[2])):
        small += [carry_ref[2:3, number * first : (number + 1) * first], total]
    small += [ref[...] for ref in up_refs]
    pieces = []
    for row in small:
        pieces += [row[:, col * LANES : (col + 1) * LANES] for col in range(row.shape[1] // LANES)]
    pieces.append(jnp.zeros((LANES - len(pieces), LANES), F32))
    grads_ref[0, count * cut :, :] = jnp.concatenate(pieces, 0).astype(BF16)
    grads_ref[1, count * cut :, :] = jnp.zeros((LANES, LANES), BF16)


def project_grad(
    turned, turned_glob, dq, dk, dv, weight, vecs, half, first, width, spot, carry=None, mid_sums=None,
    up_sums=(), after=(),
):
    dim = turned.shape[0]
    rows_all = dq.shape[0]
    last = carry is not None
    grads = pl.BlockSpec((rows_all, width), lambda i: (0, spot))
    shape = (2, 3 * width // LANES * dim // 2 + (LANES if last else 0), LANES)
    more = [carry, mid_sums, *up_sums] if last else []
    return launch(
        functools.partial(project_grad_body, first=first, last=last, shared=1.0 - half),
        "project_grad",
        (1,),
        [
            (turned, full(turned.shape)),
            (turned_glob, full(turned_glob.shape)),
            (dq, grads),
            (dk, grads),
            (dv, grads),
            (weight, pl.BlockSpec((None, *weight.shape[1:]), lambda i: (half, 0, 0))),
            (vecs, full(vecs.shape)),
        ]
        + [(array, full(array.shape)) for array in more],
        [(shape, BF16, full(shape))] + ([] if last else [((8, dim), F32, full((8, dim)))]),
        cost(6 * rows_all * dim * width, rows_all * (dim + 3 * width) * 2),
        after=after,
    )


def hidden_back(dq_ref, dk_ref, dv_ref, both_ref, places):
    d_hidden = None
    for part, spots in enumerate(places):
        joined = jnp.concatenate(
            [ref[:, s * LANES : (s + 1) * LANES] for ref in (dq_ref, dk_ref, dv_ref) for s in spots], 1
        )
        made = nt(joined, both_ref[part])
        d_hidden = made if d_hidden is None else d_hidden + made
    return d_hidden


def input_back_body(
    dq_ref, dk_ref, dv_ref, both_ref, x_ref, dmid_ref, vecs_ref, tokens_ref, *, places
):
    d_hidden = hidden_back(dq_ref, dk_ref, dv_ref, both_ref, places)
    xhat, inv = normed(x_ref[...].astype(F32))
    tokens_ref[...] = dmid_ref[...] + norm_back(xhat, inv, vecs_ref[0:1, :], d_hidden)


def input_back(dq, dk, dv, both, x, d_mid, vecs, places, after=()):
    rows, dim = x.shape
    row = pl.BlockSpec((TILE, dim), lambda i: (i, 0))
    return launch(
        functools.partial(input_back_body, places=places),
        "input_back",
        (rows // TILE,),
        [
            (dq, row),
            (dk, row),
            (dv, row),
            (both, full(both.shape)),
            (x, row),
            (d_mid, row),
            (vecs, full(vecs.shape)),
        ],
        [(x.shape, F32, row, True)],
        cost(6 * rows * dim * dim, rows * dim * 16 + 6 * dim * dim),
        after=after,
    )[0]


def glob_back_body(dq_ref, dk_ref, dv_ref, both_ref, out_ref, *, places):
    out_ref[...] = hidden_back(dq_ref, dk_ref, dv_ref, both_ref, places).astype(BF16)


def glob_back(dq, dk, dv, both, places, after=()):
    rows_all, dim = dq.shape
    last = rows_all // TILE - 1
    row = pl.BlockSpec((TILE, dim), lambda i: (last, 0))
    return launch(
        functools.partial(glob_back_body, places=places),
        "glob_back",
        (1,),
        [(dq, row), (dk, row), (dv, row), (both, full(both.shape))],
        [((TILE, dim), BF16, full((TILE, dim)))],
        cost(6 * TILE * dim * dim, TILE * dim * 16 + 6 * dim * dim),
        after=after,
    )[0]


def glob_input_body(kept_ref, got_ref, x_ref, dmid_ref, vecs_ref, out_ref):
    d_hidden = kept_ref[...].astype(F32) + got_ref[...].astype(F32)
    xhat, inv = normed(x_ref[...].astype(F32))
    out_ref[...] = dmid_ref[...] + norm_back(xhat, inv, vecs_ref[0:1, :], d_hidden)


def glob_input(place, kept, got, x, d_mid, vecs, after=()):
    own, dim = x.shape
    first = (d_mid.shape[0] - 2 * GLOB) // own
    spec = pl.BlockSpec((own, dim), lambda i, place: (0, 0))
    here = pl.BlockSpec((own, dim), lambda i, place: (first + place[2] // own, 0))

    def body(place_ref, *refs):
        glob_input_body(*refs)

    return launch(
        body,
        "glob_input",
        (1,),
        [(kept, spec), (got, spec), (x, spec), (d_mid, here), (vecs, full(vecs.shape))],
        [((own, dim), F32, spec, True)],
        cost(0, own * dim * 14),
        prefetch=(place,),
        after=after,
    )[0]


def pair_add(left, right):
    return (left.astype(F32) + right.astype(F32)).astype(BF16)


def turn_body(place_ref, *refs, actions):
    count = sum(len(action[2]) for action in actions)
    ins, outs = list(refs[:count]), list(refs[count:])
    for kind, number, arrays in actions:
        mine = [ins.pop(0) for _ in arrays]
        side = None if number is None else place_ref[number]
        if kind == "start":
            go_ref, stay_ref = outs.pop(0), outs.pop(0)
            first = 0
            for own_ref, got_ref in zip(mine[::2], mine[1::2]):
                rows = slice(first, first + own_ref.shape[1])
                go_ref[rows, :] = pair_add(own_ref[1 - side], got_ref[1 - side])
                stay_ref[rows, :] = pair_add(own_ref[side], got_ref[side])
                first = rows.stop
        elif kind == "pick":
            go_ref, stay_ref = outs.pop(0), outs.pop(0)
            go_ref[...] = mine[0][1 - side]
            stay_ref[...] = mine[0][side]
        elif kind == "split":
            go_ref, stay_ref = outs.pop(0), outs.pop(0)
            go_ref[...] = pair_add(mine[0][1 - side], mine[1][1 - side])
            stay_ref[...] = pair_add(mine[0][side], mine[1][side])
        elif kind == "add":
            outs.pop(0)[...] = pair_add(mine[0][...], mine[1][...])
        elif kind == "join":
            out_ref = outs.pop(0)
            out_ref[side] = mine[0][...]
            out_ref[1 - side] = mine[1][...]
        else:
            outs.pop(0)[...] = mine[0][...]


def halved(array):
    return array.reshape(2, -1, array.shape[-1])


class Chain:
    def __init__(self, steps, sends, first):
        self.steps, self.sends, self.first, self.at = steps, sends, first, 0

    def action(self):
        kind, number = self.steps[self.at]
        if kind in ("start", "pick", "copy"):
            return kind, number, self.first
        arrays = [self.stay, self.other]
        return kind, number, [halved(a) for a in arrays] if kind == "split" else arrays

    def shapes(self):
        kind, _, arrays = self.action()
        lanes = arrays[0].shape[-1]
        if kind == "start":
            return [(sum(own.shape[1] for own in arrays[::2]), lanes)] * 2
        if kind in ("pick", "split"):
            return [arrays[0].shape[1:]] * 2
        if kind == "join":
            return [(2, *arrays[0].shape)]
        return [arrays[0].shape]

    def take(self, outs):
        kind, _ = self.steps[self.at]
        self.stay = outs[-1].reshape(-1, outs[-1].shape[-1]) if kind == "join" else outs[-1]
        self.other = self.sends[self.at](outs[0] if len(outs) > 1 else self.stay)
        self.at += 1

    @property
    def left(self):
        return len(self.steps) - self.at


def turn(place, chains, after=()):
    actions = [chain.action() for chain in chains]
    shapes = [chain.shapes() for chain in chains]
    flat = [shape for group in shapes for shape in group]
    arrays = [array for _, _, group in actions for array in group]
    outs = launch(
        functools.partial(turn_body, actions=[(k, n, [None] * len(a)) for k, n, a in actions]),
        "turn",
        (1,),
        [(a, full(a.shape)) for a in arrays],
        [(shape, BF16, full(shape)) for shape in flat],
        cost(0, sum(a.size for a in arrays) * 4),
        prefetch=(place,),
        after=after,
    )
    outs = list(outs)
    mark = outs[-1]
    for chain, group in zip(chains, shapes):
        chain.take([outs.pop(0) for _ in group])
    return [mark]


def by_side(place_ref, number, mine_ref, other_ref, write):
    for half in range(2):
        for ref, here in ((mine_ref, place_ref[number] == half), (other_ref, place_ref[number] != half)):

            @pl.when(here)
            def _(ref=ref, half=half):
                write(ref, half)


def ffn_unpack_body(place_ref, mine_ref, other_ref, up_ref, down_ref, *, number, chunk):
    dim = up_ref.shape[0]
    units = up_ref.shape[1]

    def write(ref, half):
        count = units * dim // LANES
        first = half * count
        spot = 0
        for step in range(units // chunk):
            for col in range(chunk // LANES):
                if first <= spot < first + count:
                    begin = step * chunk + col * LANES
                    up_ref[:, begin : begin + LANES] = ref[spot - first : spot - first + dim, :].astype(F32)
                spot += dim
            for col in range(dim // LANES):
                if first <= spot < first + count:
                    down_ref[step * chunk : (step + 1) * chunk, col * LANES : (col + 1) * LANES] = ref[
                        spot - first : spot - first + chunk, :
                    ].astype(F32)
                spot += chunk

    by_side(place_ref, number, mine_ref, other_ref, write)


def ffn_unpack(place, number, mine, other, dim, half, units, part, held=(), after=()):
    spec = full(mine.shape)
    one = pl.Buffered(1)
    return launch(
        functools.partial(ffn_unpack_body, number=number, chunk=min(FFN_CHUNK, units)),
        "ffn_unpack",
        (1,),
        [(mine, spec), (other, spec)],
        [
            ((dim, half), F32, pl.BlockSpec((dim, units), lambda i, place: (0, part), pipeline_mode=one), True),
            ((half, dim), F32, pl.BlockSpec((units, dim), lambda i, place: (part, 0), pipeline_mode=one), True),
        ],
        cost(0, mine.size * 12),
        prefetch=(place,),
        held=held,
        after=after,
    )


def tail_unpack_body(place_ref, mine_ref, other_ref, q_ref, k_ref, v_ref, more_ref, *, number, last):
    dim, width = q_ref.shape
    cols = width // LANES
    cut = dim // 2
    count = 3 * cols

    def write(ref, half):
        for spot in range(count):
            unit, part = divmod(half * count + spot, 2)
            kind, col = unit // cols, unit % cols
            (q_ref, k_ref, v_ref)[kind][
                part * cut : (part + 1) * cut, col * LANES : (col + 1) * LANES
            ] = ref[spot * cut : (spot + 1) * cut, :].astype(F32)
        spot = count * cut
        if last:
            if half == 0:
                more_ref[...] = ref[spot : spot + LANES, :].astype(F32)
            return
        rows, wide = more_ref.shape[0], more_ref.shape[1] // LANES // 2
        for col in range(wide):
            begin = (half * wide + col) * LANES
            more_ref[:, begin : begin + LANES] = ref[spot : spot + rows, :].astype(F32)
            spot += rows

    by_side(place_ref, number, mine_ref, other_ref, write)


def tail_unpack(place, number, mine, other, dim, half, first, width, held=()):
    spec = full(mine.shape)
    last = bool(held)
    block = pl.BlockSpec((dim, width), lambda i, place: (0, first // width), pipeline_mode=pl.Buffered(1))
    more = (LANES, LANES) if last else (half, dim)
    return launch(
        functools.partial(tail_unpack_body, number=number, last=last),
        "tail_unpack",
        (1,),
        [(mine, spec), (other, spec)],
        [((dim, half), F32, block, True)] * 3 + [(more, F32, full(more))],
        cost(0, mine.size * 12),
        prefetch=(place,),
        held=held,
    )


def finish_body(mine_ref, theirs_ref, *outs):
    rows = 0
    for number, out_ref in enumerate(outs):
        count = out_ref.shape[0] // LANES
        pieces = []
        for row in range(rows, rows + count):
            piece = mine_ref[row : row + 1, :]
            pieces.append(piece + theirs_ref[row : row + 1, :] if number < 6 else piece)
        out_ref[...] = jnp.concatenate(pieces, 1).reshape(-1)
        rows += count


def finish(mine, theirs, sizes):
    return launch(
        finish_body,
        "finish",
        (1,),
        [(mine, full(mine.shape)), (theirs, full(theirs.shape))],
        [((size,), F32, full((size,))) for size in sizes],
        cost(0, 4 * sum(sizes)),
    )


def per_device(
    tokens, glob_tokens, w_query, b_query, w_key, w_value, b_value, w_out, b_out, w_up, b_up,
    w_down, b_down, gain_attn, shift_attn, gain_ffn, shift_ffn, doc_blocks, doc_tail,
    grad_tokens, grad_glob,
):
    seq_size = lax.axis_size("seq")
    seq_pos = lax.axis_index("seq")
    tp_pos = lax.axis_index("tp")
    rows, dim = tokens.shape
    own_glob = glob_tokens.shape[0]
    half = w_query.shape[1]
    units = w_up.shape[1]
    pairs = 2 * half // PAIR
    blocks = rows // BLOCK
    glob_rows = 2 * GLOB
    rows_all = rows + glob_rows
    group_size = GROUP_BLOCKS // (2 * blocks)
    group_bits = group_size.bit_length() - 1
    seq_bits = seq_size.bit_length() - 1
    group_pos = seq_pos % group_size
    own_first = (group_pos * 2 + tp_pos) * own_glob

    def flip(value, bit):
        return lax.ppermute(value, "seq", [(s, s ^ (1 << bit)) for s in range(seq_size)])

    def swap(value):
        return lax.ppermute(value, "tp", [(0, 1), (1, 0)])

    rest = tuple(range(3, seq_bits))
    orders = {
        "one": ((0, 1, 2, *rest), (2, 0, 1, *rest)),
        "two": ((1, 0, 2, *rest), (0, 2, 1, *rest)),
        "three": ((0, 1, 2, *rest), (2, 0, 1, *rest)),
        "four": ((1, 0, 2, *rest), (0, 2, 1, *rest)),
    }
    place = [
        (seq_pos * 2 + tp_pos) * blocks,
        (seq_pos // group_size) * 2,
        own_first,
        jnp.int32(own_glob),
        group_pos,
        tp_pos,
    ]
    group_sides = len(place)
    place += [(seq_pos >> bit) & 1 for bit in range(group_bits)] + [tp_pos]
    job_sides = {}
    for name, (zero, one) in orders.items():
        job_sides[name] = len(place)
        place += [(seq_pos >> jnp.where(tp_pos == 0, a, b)) & 1 for a, b in zip(zero, one)]
    place = jnp.stack(place).astype(jnp.int32)

    def trade(value, name, step):
        zero, one = orders[name][0][step], orders[name][1][step]
        links = [(2 * s, 2 * (s ^ (1 << zero))) for s in range(seq_size)]
        links += [(2 * s + 1, 2 * (s ^ (1 << one)) + 1) for s in range(seq_size)]
        return lax.ppermute(value, ("seq", "tp"), links)

    gathered = jnp.stack([glob_tokens, grad_glob])[None]
    vecs, half_own = pack_vectors(
        [gain_attn, shift_attn, gain_ffn, shift_ffn, b_out, b_down], [b_query, b_value, b_up]
    )
    half_par = swap(half_own)
    halves = (half_own, half_par)
    weights = [w_query, w_key, w_value]
    weights += [swap(weight) for weight in weights]
    marks = ()
    for bit in range(group_bits):
        other = flip(gathered, bit)
        if bit == 1:
            qkv, turned, qkv_both = project(tokens, vecs, halves, weights, (gathered,))
            marks = (turned,)
        if bit == group_bits - 1:
            docs, augk, augq, mask, seen = layout(
                place, doc_blocks, doc_tail, rows_all, glob_rows, blocks, (gathered,)
            )
            marks = (augq,)
        gathered = stack_two(gathered, other, marks)
    x_glob, dz_all = order_rows(place, gathered, swap(gathered), grad_tokens)
    qkv_glob, turned_glob = project(x_glob, vecs, halves, [qkv_both])
    out_par = swap(w_out)
    up_par = swap(w_up)
    down_par = swap(w_down)

    mine, theirs = glob_forward(qkv, qkv_glob, augk, augq, seen, pairs)
    state = merge(mine, swap(theirs))
    outs = ()
    for bit in range(group_bits):
        other = flip(state, bit)
        first, end = pairs * bit // group_bits, pairs * (bit + 1) // group_bits
        outs = local_forward(
            docs, qkv, qkv_glob, augk, pairs, blocks, first, end - first, outs, (state,)
        )
        state = merge(state, other, (outs[1],))
    state_par = swap(state)
    high, lse = outs
    held = middle_local(high, tokens, w_out, out_par, vecs, (state,))
    middle, hidden, ffn_turned, high, lse_glob = middle_glob(
        state, state_par, x_glob, w_out, out_par, vecs, [*held, high]
    )

    def job(name, pairs):
        first, count = job_sides[name], seq_bits
        steps = [("start", first)]
        steps += [("split", first + step) for step in range(1, count)]
        steps += [("add", None)]
        steps += [("join", first + step) for step in range(count - 1, 0, -1)]
        order = [*range(count), *range(count - 1, -1, -1)]
        sends = [lambda value, step=step: trade(value, name, step) for step in order]
        return Chain(steps, sends, [array for pair in pairs for array in pair])

    def apart(value):
        return value

    part = units // 2
    acts, ups, grads = [], [[], []], []
    dn = None
    marks = []
    for which, (up, down, vec) in ((1, (up_par, down_par, half_par)), (0, (w_up, w_down, half_own))):
        for number in range(2):
            dn, act, grad, up_sum = ffn_part(
                hidden, ffn_turned, dz_all, up, vec, down, mask, number * part, part, dn, marks
            )
            grad = grad.reshape(2, -1, LANES)
            acts.append((act, down, number))
            ups[which].append(up_sum)
            grads.append(swap(grad) if which else grad)
            if not which and not number:
                one = job("one", [(grads[2], grads[0])])
                marks = turn(place, [one], (up_sum,))
    two = job("two", [(grads[3], grads[1])])
    marks = turn(place, [one, two], (up_sum,))

    d_mid, d_attn, delta, out_grad, mid_sums = middle_back(
        dn, middle, dz_all, high, w_out, out_par, vecs, mask, marks
    )
    out_grad = out_grad.reshape(2, 2, -1, LANES)
    out_got = Chain([("copy", None)], [swap], [out_grad[1]])
    marks = turn(place, [one, out_got], (mid_sums,))
    own = pairs // 2
    some = 2 * LANES
    spots = {0: 0, 1: 1, own: 2, own + 1: 3, 2: 4, own + 2: 5}
    places = ((0, 1, 4), (2, 3, 5))
    plan = (
        (0, (one, two)), (own, (one, two)), (1, (one, two)), (own + 1, (one, two)), (2, (two,)),
        (own + 2, (two,)),
    )
    grads = ()
    for number, (pair, chains) in enumerate(plan):
        if number == 4:
            carries = []
            for which in (1, 0):
                grad, carry = project_grad(
                    turned, turned_glob, *grads, qkv_both, vecs, which, 0, some, which, after=marks
                )
                carries.append(carry)
                if which:
                    got = swap(grad)
                    marks = [carry]
            three = job("three", [(grad, got), (out_grad[0], out_got.other)])
            marks = turn(place, [one, three], (carry,))
        grads = attention_back(
            docs, qkv, qkv_glob, d_attn, lse, lse_glob, delta, augk, augq, pairs, pair, spots[pair],
            grads, marks,
        )
        if pair == own + 2:
            chains = (*chains, three)
        marks = turn(place, chains, (grads[0],))
    for which in (1, 0):
        grad = project_grad(
            turned, turned_glob, *grads, qkv_both, vecs, which, some, LANES, 4 + which,
            carries[1 - which], mid_sums, ups[which], marks,
        )[0]
        if which:
            got = swap(grad)
            marks = turn(place, [three, two], (grad,))
    four = job("four", [(grad, got)])
    marks = turn(place, [three, four])

    back = glob_back(*grads, qkv_both, places, marks)
    sends = [lambda value, bit=bit: flip(value, bit) for bit in reversed(range(group_bits))] + [swap]
    numbers = [*reversed(range(group_sides, group_sides + group_bits)), group_sides + group_bits]
    steps = [("pick", numbers[0])] + [("split", number) for number in numbers[1:]]
    globs = Chain(steps, sends, [halved(back)])
    marks = turn(place, [four, three, globs])
    tokens_grad = input_back(*grads, qkv_both, tokens, d_mid, vecs, places, marks)
    marks = turn(place, [four, three, globs], (far(tokens_grad),))
    kinds = ()
    for number, chain in enumerate((one, two)):
        while chain.left:
            marks = turn(place, [chain], marks)
        name = ("one", "two")[number]
        kinds = ffn_unpack(
            place, job_sides[name], chain.stay, chain.other, dim, units, part, number, kinds, marks
        )
        chosen = (four, globs) if number else (four, three, globs)
        marks = turn(place, [c for c in chosen if c.left], (far(kinds[0]),))
    up_grad, down_grad = kinds
    marks = turn(place, [c for c in (four, three) if c.left], marks)
    glob_grad = glob_input(place, globs.stay, globs.other, glob_tokens, d_mid, vecs, marks)
    marks = turn(place, [c for c in (four, three) if c.left], (far(glob_grad),))
    while four.left or three.left:
        marks = turn(place, [c for c in (four, three) if c.left], marks)
    out_tokens, out_all = output_rows(
        place, middle, vecs, [a for a, _, _ in acts], [(w, n) for _, w, n in acts], own_glob, marks
    )
    out_glob = lax.dynamic_slice_in_dim(out_all, own_first, own_glob, 0)
    *kinds, w_out_grad = tail_unpack(
        place, job_sides["three"], three.stay, three.other, dim, half, 0, some
    )
    q_grad, k_grad, v_grad, small = tail_unpack(
        place, job_sides["four"], four.stay, four.other, dim, half, some, LANES, kinds
    )
    (
        gain_f_grad, shift_f_grad, out_bias, down_bias, gain_a_grad, shift_a_grad, b_query_grad,
        b_value_grad, b_up_grad,
    ) = finish(small, swap(small), [dim] * 6 + [half, half, units])
    return (
        out_tokens, out_glob, tokens_grad, glob_grad, q_grad, b_query_grad, k_grad,
        v_grad, b_value_grad, w_out_grad, out_bias, up_grad, b_up_grad, down_grad, down_bias,
        gain_a_grad, shift_a_grad, gain_f_grad, shift_f_grad,
    )


def solution(mesh):
    rows = P(("seq", "tp"), None)
    cols, part, whole = P(None, "tp"), P("tp"), P()
    lines = P("tp", None)
    return jax.shard_map(
        per_device,
        mesh=mesh,
        in_specs=(
            rows, rows, cols, part, cols, cols, part, lines, whole, cols, part, lines, whole,
            whole, whole, whole, whole, whole, whole, rows, rows,
        ),
        out_specs=(
            rows, rows, rows, rows, cols, part, cols, cols, part, lines, whole, cols, part, lines,
            whole, whole, whole, whole, whole,
        ),
        check_vma=False,
    )
```
